32 devices in a mesh: dp: 4 (over z), expert: 8 (over y, x, core).
Axes of the slice: x: 2, y: 2, z: 4, core: 2. Of those that a mesh axis runs over, the one named last changes fastest.
Arguments:
- tokens: bfloat16 [4096, 2048], P(('dp', 'expert')), may hold values from -6 to 6
- routes: int32 [4096, 8], P(('dp', 'expert')), may hold values from 0 to 31, all different within a row; in each aligned block of 128 rows (0 to 127, 128 to 255, ...) at most 38 rows name the same one
- prefix_len: int32 [4], P('dp'), may hold values from 102 to 512
- query_weight: bfloat16 [2048, 4096], P('dp', 'expert'), may hold values from -0.125 to 0.125
- key_matrix: bfloat16 [2048, 512], P('dp', 'expert'), may hold values from -0.125 to 0.125
- value_matrix: bfloat16 [2048, 512], P('dp', 'expert'), may hold values from -0.125 to 0.125
- out_weight: bfloat16 [4096, 2048], P('dp', 'expert'), may hold values from -2 to 2
- router_weight: bfloat16 [2048, 32], P('dp', 'expert'), may hold values from -0.0625 to 0.0625
- attention_gain: float32 [2048], replicated, may hold values from 0.25 to 1.75
- mixture_gain: float32 [2048], replicated, may hold values from 0.25 to 1.75
- query_gain: float32 [128], replicated, may hold values from 0.25 to 1.75
- key_norm_gain: float32 [128], replicated, may hold values from 0.25 to 1.75
- expert_gate: bfloat16 [32, 2048, 768], P(('dp', 'expert')), may hold values from -0.125 to 0.125
- expert_up: bfloat16 [32, 2048, 768], P(('dp', 'expert')), may hold values from -0.125 to 0.125
- expert_down: bfloat16 [32, 768, 2048], P(('dp', 'expert')), may hold values from -0.875 to 0.875
- cotangent: bfloat16 [4096, 2048], P(('dp', 'expert')), may hold values from -6 to 6
Outputs:
- layer_out: bfloat16 [4096, 2048], P(('dp', 'expert'))
- input_grad: float32 [4096, 2048], P(('dp', 'expert'))
- query_weight_grad: float32 [2048, 4096], P('dp', 'expert')
- key_weight_grad: float32 [2048, 512], P('dp', 'expert')
- value_weight_grad: float32 [2048, 512], P('dp', 'expert')
- out_weight_grad: float32 [4096, 2048], P('dp', 'expert')
- router_grad: float32 [2048, 32], P('dp', 'expert')
- attention_gain_grad: float32 [2048], replicated
- mixture_gain_grad: float32 [2048], replicated
- query_gain_grad: float32 [128], replicated
- key_gain_grad: float32 [128], replicated
- expert_gate_grad: float32 [32, 2048, 768], P(('dp', 'expert'))
- expert_up_grad: float32 [32, 2048, 768], P(('dp', 'expert'))
- expert_down_grad: float32 [32, 768, 2048], P(('dp', 'expert'))
The draws below stay inside these ranges and needn't reach their ends.
Inputs may be any that keep to these rules, and one draw needn't show every extreme that they name: `routes`: each row names 8 different experts. In the rows of one device no expert is named more than 38 times, and in every draw the rows of some device name some expert exactly 38 times.
All inputs are finite; a program needn't handle non-finite values.
Results may differ from the reference program's by a relative error of at most 0.025.
Values may be sent and summed in bfloat16 or wider, within the bound.
No kernel may reach another device: no remote copies, remote signals or barrier semaphores. Data moves between devices by JAX's collectives and lax.ppermute only.
A program may use at most 256 MiB of HBM per device.

```python
import math
import jax
import jax.numpy as jnp
import numpy as np
from jax import lax

MODEL_WIDTH = 2048
QUERY_HEADS = 32
KEY_VALUE_HEADS = 4
HEAD_SIZE = 128
FFE = 768
TOP = 8
TOK_DEV = 128
EXPERTS = 32
CAP = 38
SEQUENCE_LENGTH = 1024
SEQUENCE_COUNT = 4
TOKENS = 4096
N_DP = 4
N_EXPERT = 8


def with_ends(drawn, own_key, smallest, high):
    place = [jax.random.randint(jax.random.fold_in(own_key, axis), (), 0, length) for axis, length in enumerate(drawn.shape)]
    longest = drawn.shape.index(max(drawn.shape))
    beside = place[:longest] + [(place[longest] + 1) % drawn.shape[longest]] + place[longest + 1:]
    return drawn.at[tuple(place)].set(smallest).at[tuple(beside)].set(high)


def level_of(rng, shape, shards, smallest, largest):
    factor_of = 1.0
    for axis_at, shards_of in shards:
        steps = jax.random.uniform(jax.random.fold_in(jax.random.fold_in(rng, 6), axis_at), (shards_of,), jnp.float32, smallest / len(shards), largest / len(shards))
        factor_of = factor_of * jnp.repeat(jnp.exp(steps), shape[axis_at] // shards_of).reshape((-1,) + (1,) * (len(shape) - 1 - axis_at))
    return factor_of


def assign_block(stream_key, own, number, rows, number_of, top, bound, slope):
    sequence = jax.random.permutation(stream_key, number_of)
    crowded, common = shares(number_of, rows * top, bound, slope, True), shares(number_of, rows * top, bound, slope, False)
    places = jnp.arange(number_of)

    def named(tallies, rotation):
        used = int((tallies > 0).sum())
        fixed = max(1, used // 4)
        passed = fixed + (places - fixed + rotation * (used - fixed)) % max(1, number_of - fixed)
        return jnp.zeros((number_of,), jnp.int32).at[sequence[jnp.where(places < fixed, places, passed)]].set(jnp.asarray(tallies, jnp.int32))

    tallies = jnp.where(number % 4 == 0, named(crowded, number // 4), named(common, number - number // 4 - 1))
    mixed = jax.random.permutation(jax.random.fold_in(own, 3), number_of)
    donor, receiver = mixed[0:number_of // 2 * 2:2], mixed[1:number_of // 2 * 2:2]
    room = jnp.minimum(tallies[donor] - 1, bound - tallies[receiver]) // 2
    room = jnp.where((donor == sequence[0]) | (receiver == sequence[0]) | (tallies[receiver] == 0), 0, jnp.maximum(room, 0))
    passed = jax.random.randint(jax.random.fold_in(own, 4), (number_of // 2,), 0, 1 << 20) % (room + 1)
    tallies = tallies.at[donor].add(-passed).at[receiver].add(passed)
    items = jnp.searchsorted(jnp.cumsum(tallies), jnp.arange(rows * top), side="right").astype(jnp.int32)
    grid = items.reshape(top, rows).T
    grid = grid[jax.random.permutation(jax.random.fold_in(own, 1), rows)]
    rotation = jax.random.randint(jax.random.fold_in(own, 2), (rows, 1), 0, top)
    return jnp.take_along_axis(grid, (jnp.arange(top)[None, :] + rotation) % top, axis=1)


def shares(amount, total, bound, lean, full):
    weights = [(1 << 20) // math.isqrt(rank ** lean) + 1 for rank in range(1, amount + 1)]
    largest = bound if full else min(bound, max(-(-total // amount), total * weights[0] // sum(weights)))
    least = 1 if total - largest >= amount - 1 else 0
    holding, rest = [largest] + [least] * (amount - 1), total - largest - least * (amount - 1)
    while rest > 0:
        movable = [i for i in range(1, amount) if holding[i] < largest] or [i for i in range(1, amount) if holding[i] < bound]
        mass, left = sum([weights[i] for i in movable]), rest
        for i in movable:
            more = min(bound - holding[i], max(1, left * weights[i] // mass), rest)
            holding[i] = holding[i] + more
            rest = rest - more
    return np.array(holding)


def gaussian(rng, shape, width, limit, split=(), kind=jnp.bfloat16):
    array = jax.random.normal(rng, shape, jnp.float32) * width
    if len(split) > 0:
        array = level_of(rng, shape, split, -0.22, 0.18) * array
    return jnp.clip(array, min=-limit, max=limit).astype(kind)


def setup_inputs(seed: int = 0) -> dict:
    splits = jax.random.split(jax.random.key(seed), 17)
    tokens = gaussian(splits[0], (TOKENS, MODEL_WIDTH), 1.0, 6.0, ((0, 32),))
    routes_keys = jax.random.split(jax.random.fold_in(splits[1], 1), TOKENS // TOK_DEV)
    routes_turns = jax.random.permutation(jax.random.fold_in(splits[1], 3), TOKENS // TOK_DEV)
    routes = jax.vmap(lambda own, number: assign_block(jax.random.fold_in(splits[1], 2), own, number, TOK_DEV, EXPERTS, TOP, CAP, 1))(routes_keys, routes_turns).reshape((TOKENS, TOP))
    prefix_len = with_ends(jax.random.randint(splits[2], (SEQUENCE_COUNT,), SEQUENCE_LENGTH // 10, SEQUENCE_LENGTH // 2 + 1), jax.random.fold_in(splits[2], 1), SEQUENCE_LENGTH // 10, (SEQUENCE_LENGTH // 2 + 1) - 1).astype(jnp.int32)
    query_weight = gaussian(splits[3], (MODEL_WIDTH, QUERY_HEADS * HEAD_SIZE), MODEL_WIDTH ** -0.5, 0.125, ((0, 4), (1, 8)))
    key_matrix = gaussian(splits[4], (MODEL_WIDTH, KEY_VALUE_HEADS * HEAD_SIZE), MODEL_WIDTH ** -0.5, 0.125, ((0, 4), (1, 8)))
    value_matrix = gaussian(splits[5], (MODEL_WIDTH, KEY_VALUE_HEADS * HEAD_SIZE), MODEL_WIDTH ** -0.5, 0.125, ((0, 4), (1, 8)))
    out_weight = gaussian(splits[6], (QUERY_HEADS * HEAD_SIZE, MODEL_WIDTH), (max(8, QUERY_HEADS * HEAD_SIZE // 512)) ** -0.5, 2.0, ((0, 4), (1, 8)))
    router_weight = gaussian(splits[7], (MODEL_WIDTH, EXPERTS), (MODEL_WIDTH * 4) ** -0.5, 0.0625, ((0, 4), (1, 8)))
    attention_gain = jnp.clip(1.0 + 0.15 * jax.random.normal(splits[8], (MODEL_WIDTH,), jnp.float32), 0.25, 1.75)
    mixture_gain = jnp.clip(1.0 + 0.15 * jax.random.normal(splits[9], (MODEL_WIDTH,), jnp.float32), 0.25, 1.75)
    query_gain = jnp.clip(1.0 + 0.15 * jax.random.normal(splits[10], (HEAD_SIZE,), jnp.float32), 0.25, 1.75)
    key_norm_gain = jnp.clip(1.0 + 0.15 * jax.random.normal(splits[11], (HEAD_SIZE,), jnp.float32), 0.25, 1.75)
    expert_gate = gaussian(splits[12], (EXPERTS, MODEL_WIDTH, FFE), MODEL_WIDTH ** -0.5, 0.125, ((0, 32),))
    expert_up = gaussian(splits[13], (EXPERTS, MODEL_WIDTH, FFE), MODEL_WIDTH ** -0.5, 0.125, ((0, 32),))
    expert_down = gaussian(splits[14], (EXPERTS, FFE, MODEL_WIDTH), (FFE // 16) ** -0.5, 0.875, ((0, 32),))
    cotangent = gaussian(splits[15], (TOKENS, MODEL_WIDTH), 1.0, 6.0, ((0, 32),))
    return dict(tokens=tokens, routes=routes, prefix_len=prefix_len, query_weight=query_weight, key_matrix=key_matrix, value_matrix=value_matrix, out_weight=out_weight, router_weight=router_weight, attention_gain=attention_gain, mixture_gain=mixture_gain, query_gain=query_gain, key_norm_gain=key_norm_gain, expert_gate=expert_gate, expert_up=expert_up, expert_down=expert_down, cotangent=cotangent)


EPS = 1e-06
ROTARY_BASE = 1000000.0
VERY_NEGATIVE = -1e+30
PRECISE = lax.Precision.HIGHEST

@jax.custom_vjp
def narrow_precision(v):
    return lax.optimization_barrier(v.astype(jnp.bfloat16)).astype(jnp.float32)

@jax.custom_vjp
def low_back(v):
    return v

def low_keep(v):
    return (narrow_precision(v), None)

def low_pass(kept, grad):
    return (grad,)

def back_keep(v):
    return (v, None)

def back_low(kept, grad):
    return (narrow_precision(grad),)
narrow_precision.defvjp(low_keep, low_pass)
low_back.defvjp(back_keep, back_low)

def head_normalize(source, gain_row):
    scaling = lax.rsqrt(lax.optimization_barrier(jnp.mean(source * source, axis=-1, keepdims=True)) + EPS)
    return source * scaling * gain_row

def rotary(span_length):
    half_dim = HEAD_SIZE // 2
    frequency = jnp.power(ROTARY_BASE, -jnp.arange(half_dim, dtype=jnp.float32) * 2.0 / HEAD_SIZE)
    places = jnp.arange(span_length, dtype=jnp.int32).astype(jnp.float32)
    angles = places[:, None] * frequency[None, :]
    cosine_lookup = jnp.concatenate([jnp.cos(angles), jnp.cos(angles)], axis=-1)[:, None, :]
    sine_lookup = jnp.concatenate([jnp.sin(angles), jnp.sin(angles)], axis=-1)[:, None, :]
    return (cosine_lookup, sine_lookup)

def rotary_apply(source, cosine_lookup, sine_lookup):
    half_dim = source.shape[-1] // 2
    front_half = source[..., :half_dim]
    back_half = source[..., half_dim:]
    return source * cosine_lookup + jnp.concatenate([-back_half, front_half], axis=-1) * sine_lookup

def attend_sequence(query_sequence, key_sequence, value_sequence, prefix):
    span_length = key_sequence.shape[0]
    rows_per_block = TOK_DEV
    count_of_blocks = span_length // rows_per_block
    query_tiles = query_sequence.reshape(count_of_blocks, rows_per_block, KEY_VALUE_HEADS, QUERY_HEADS // KEY_VALUE_HEADS, HEAD_SIZE)
    starts = jnp.arange(count_of_blocks, dtype=jnp.int32) * rows_per_block
    key_place = jnp.arange(span_length, dtype=jnp.int32)

    def one_block(packed):
        query_block, block_start = packed
        scores = low_back(jnp.einsum('thgd,shd->hgts', query_block, key_sequence, precision=PRECISE) * HEAD_SIZE ** (-0.5))
        query_place = block_start + jnp.arange(rows_per_block, dtype=jnp.int32)
        allowed = (key_place[None, :] <= query_place[:, None]) | (key_place[None, :] < prefix)
        weights_low = narrow_precision(jax.nn.softmax(jnp.where(allowed, scores, VERY_NEGATIVE), axis=-1))
        return jnp.einsum('hgts,shd->thgd', weights_low, value_sequence, precision=PRECISE)
    block_list = lax.map(jax.checkpoint(one_block), (query_tiles, starts))
    return block_list.reshape(span_length, KEY_VALUE_HEADS, QUERY_HEADS // KEY_VALUE_HEADS, HEAD_SIZE)

def dispatch_slots(routes):
    devices = N_DP * N_EXPERT
    per_device = routes.reshape(devices, TOK_DEV * TOP)
    one_hot = (per_device[:, :, None] == jnp.arange(EXPERTS, dtype=jnp.int32)[None, None, :]).astype(jnp.int32)
    slot_rank = lax.optimization_barrier(jnp.sum(jnp.cumsum(one_hot, axis=1) * one_hot, axis=2)) - 1
    sources = jnp.arange(devices, dtype=jnp.int32)[:, None]
    return (per_device * (devices * CAP) + sources * CAP + slot_rank).reshape(-1)

def expert_rows(packed):
    rows_in, gate_matrix, up_matrix, down_matrix = packed
    gate_value = low_back(jnp.dot(rows_in, gate_matrix, precision=PRECISE))
    up_value = low_back(jnp.dot(rows_in, up_matrix, precision=PRECISE))
    activated = narrow_precision(jax.nn.silu(gate_value) * up_value)
    return narrow_precision(low_back(jnp.dot(activated, down_matrix, precision=PRECISE)))

def layer(tokens, query_weight, key_matrix, value_matrix, out_weight, router_weight, attention_gain, mixture_gain, query_gain, key_norm_gain, expert_gate, expert_up, expert_down, routes, prefix_len):
    head_groups = QUERY_HEADS // KEY_VALUE_HEADS
    devices = N_DP * N_EXPERT
    normed = narrow_precision(head_normalize(tokens, attention_gain))
    query_raw = low_back(jnp.dot(normed, query_weight, precision=PRECISE))
    key_unnormed = low_back(jnp.dot(normed, key_matrix, precision=PRECISE))
    value_narrow = narrow_precision(low_back(jnp.dot(normed, value_matrix, precision=PRECISE)))
    cosine_lookup, sine_lookup = rotary(SEQUENCE_LENGTH)
    query_sequence = head_normalize(query_raw.reshape(SEQUENCE_COUNT, SEQUENCE_LENGTH, QUERY_HEADS, HEAD_SIZE), query_gain)
    query_narrow = narrow_precision(rotary_apply(query_sequence, cosine_lookup, sine_lookup)).reshape(SEQUENCE_COUNT, SEQUENCE_LENGTH, KEY_VALUE_HEADS, head_groups, HEAD_SIZE)
    key_sequence = head_normalize(key_unnormed.reshape(SEQUENCE_COUNT, SEQUENCE_LENGTH, KEY_VALUE_HEADS, HEAD_SIZE), key_norm_gain)
    key_low = narrow_precision(rotary_apply(key_sequence, cosine_lookup, sine_lookup))
    value_sequence = value_narrow.reshape(SEQUENCE_COUNT, SEQUENCE_LENGTH, KEY_VALUE_HEADS, HEAD_SIZE)
    attended = lax.map(lambda packed: attend_sequence(packed[0], packed[1], packed[2], packed[3]), (query_narrow, key_low, value_sequence, prefix_len))
    attended_low = narrow_precision(low_back(attended.reshape(TOKENS, QUERY_HEADS * HEAD_SIZE)))
    after_attn = tokens + low_back(jnp.dot(attended_low, out_weight, precision=PRECISE))
    mixed_low = narrow_precision(head_normalize(after_attn, mixture_gain))
    logits = low_back(jnp.dot(mixed_low, router_weight, precision=PRECISE))
    chosen = jnp.take_along_axis(logits, routes, axis=1)
    route_weight = jax.nn.softmax(chosen, axis=-1)
    slot_index = dispatch_slots(routes)
    sent_rows = low_back(jnp.repeat(mixed_low, TOP, axis=0))
    buffer = jnp.zeros((EXPERTS * devices * CAP, MODEL_WIDTH), jnp.float32).at[slot_index].set(sent_rows)
    buffer = buffer.reshape(EXPERTS, devices * CAP, MODEL_WIDTH)
    produced = lax.map(jax.checkpoint(expert_rows), (buffer, expert_gate, expert_up, expert_down))
    picked = produced.reshape(EXPERTS * devices * CAP, MODEL_WIDTH)[slot_index].reshape(TOKENS, TOP, MODEL_WIDTH)
    return after_attn + lax.optimization_barrier(jnp.sum(picked * route_weight[:, :, None], axis=1))

def reference(tokens, routes, prefix_len, query_weight, key_matrix, value_matrix, out_weight, router_weight, attention_gain, mixture_gain, query_gain, key_norm_gain, expert_gate, expert_up, expert_down, cotangent):
    floats = (tokens.astype(jnp.float32), query_weight.astype(jnp.float32), key_matrix.astype(jnp.float32), value_matrix.astype(jnp.float32), out_weight.astype(jnp.float32), router_weight.astype(jnp.float32), attention_gain.astype(jnp.float32), mixture_gain.astype(jnp.float32), query_gain.astype(jnp.float32), key_norm_gain.astype(jnp.float32), expert_gate.astype(jnp.float32), expert_up.astype(jnp.float32), expert_down.astype(jnp.float32))

    def forward(*params):
        return layer(*params, routes, prefix_len)
    result, pullback = jax.vjp(forward, *floats)
    grads = pullback(cotangent.astype(jnp.float32))
    return (result.astype(jnp.bfloat16), grads[0], grads[1], grads[2], grads[3], grads[4], grads[5], grads[6], grads[7], grads[8], grads[9], grads[10], grads[11], grads[12])
```

```python
import functools
import math

import jax
import jax.numpy as jnp
from jax import lax
from jax.experimental import pallas as pl
from jax.experimental.pallas import tpu as pltpu
from jax.sharding import PartitionSpec as P

QUERY_HEADS = 32
KEY_VALUE_HEADS = 4
HEAD_SIZE = 128
TOP = 8
EPS = 1e-06
ROTARY_BASE = 1000000.0
VERY_NEGATIVE = -1e30
SOFTMAX_SCALE = HEAD_SIZE ** (-0.5)
LOG2_SCALE = SOFTMAX_SCALE * math.log2(math.e)
VMEM_BYTES = 56 * 1024 * 1024
F32 = jnp.float32
BF16 = jnp.bfloat16


def mm(a, b):
    return lax.dot_general(a, b, (((1,), (0,)), ((), ())), preferred_element_type=F32)


def mm_t(a, b):
    return lax.dot_general(a, b, (((1,), (1,)), ((), ())), preferred_element_type=F32)


def t_mm(a, b):
    return lax.dot_general(a, b, (((0,), (0,)), ((), ())), preferred_element_type=F32)


def row_scale(source):
    return lax.rsqrt(jnp.mean(source * source, axis=-1, keepdims=True) + EPS)


def normalize_back(upstream, source, scaling, gain_row):
    unit_rows = source * scaling
    weighted = upstream * gain_row
    inner_mean = jnp.mean(weighted * unit_rows, axis=-1, keepdims=True)
    return (scaling * (weighted - unit_rows * inner_mean), upstream * unit_rows)


def rotary_tables(span):
    half = HEAD_SIZE // 2
    frequency = jnp.power(ROTARY_BASE, -jnp.arange(half, dtype=F32) * 2.0 / HEAD_SIZE)
    angles = jnp.arange(span, dtype=jnp.int32).astype(F32)[:, None] * frequency[None, :]
    cosine, sine = jnp.cos(angles), jnp.sin(angles)
    return (
        jnp.concatenate([cosine, cosine], axis=-1),
        jnp.concatenate([-sine, sine], axis=-1),
    )


def project_kernel(x_ref, wq_ref, wkv_ref, cos_ref, sin_ref, qg_ref, kg_ref,
                   qraw_ref, kraw_ref, q_ref, k_ref, v_ref):
    x = x_ref[...]
    cosine, sine = cos_ref[...], sin_ref[...]
    q = mm(x, wq_ref[...])
    kv = mm(x, wkv_ref[...])
    qraw_ref[...] = q
    kraw_ref[...] = kv[:, :HEAD_SIZE]
    v_ref[...] = kv[:, HEAD_SIZE:].astype(BF16)

    def turned(u, gain):
        n = u * row_scale(u) * gain
        return (n * cosine + pltpu.roll(n, HEAD_SIZE // 2, 1) * sine).astype(BF16)

    for h in range(q.shape[1] // HEAD_SIZE):
        cols = slice(h * HEAD_SIZE, (h + 1) * HEAD_SIZE)
        q_ref[:, cols] = turned(q[:, cols], qg_ref[...])
    k_ref[...] = turned(kv[:, :HEAD_SIZE], kg_ref[...])


def project(x, wq, wkv, width, cosine, sine, q_gain, k_gain):
    span, model = x.shape
    tile = 256
    row = lambda w: pl.BlockSpec((tile, w), lambda i: (i, 0))
    whole = lambda a, b: pl.BlockSpec((a, b), lambda i: (0, 0))
    return pl.pallas_call(
        project_kernel,
        grid=(span // tile,),
        in_specs=[row(model), whole(model, width), whole(model, 2 * HEAD_SIZE), row(HEAD_SIZE), row(HEAD_SIZE),
                  whole(1, HEAD_SIZE), whole(1, HEAD_SIZE)],
        out_specs=[row(width), row(HEAD_SIZE), row(width), row(HEAD_SIZE), row(HEAD_SIZE)],
        out_shape=[
            jax.ShapeDtypeStruct((span, width), F32),
            jax.ShapeDtypeStruct((span, HEAD_SIZE), F32),
            jax.ShapeDtypeStruct((span, width), BF16),
            jax.ShapeDtypeStruct((span, HEAD_SIZE), BF16),
            jax.ShapeDtypeStruct((span, HEAD_SIZE), BF16),
        ],
        compiler_params=pltpu.CompilerParams(vmem_limit_bytes=VMEM_BYTES),
        cost_estimate=pl.CostEstimate(
            flops=2 * span * model * (width + 256), bytes_accessed=2 * model * (span + width + 256) + span * width * 6,
            transcendentals=0),
        name="project",
    )(x, wq, wkv, cosine, sine, q_gain[None], k_gain[None])


def block_limits(span, tile):
    return [(r0, max(r0 + tile, span // 2)) for r0 in range(0, span, tile)]


def masked(values, r0, limit, prefix):
    tile = values.shape[0]
    rows = r0 + lax.broadcasted_iota(jnp.int32, (tile, limit - r0), 0)
    cols = r0 + lax.broadcasted_iota(jnp.int32, (tile, limit - r0), 1)
    right = jnp.where((cols <= rows) | (cols < prefix), values[:, r0:], 0.0)
    return right if r0 == 0 else jnp.concatenate([values[:, :r0], right], axis=1)


def attend_kernel(tile, prefix_ref, q_ref, k_ref, v_ref, o_ref, l_ref, wide_ref):
    span = q_ref.shape[0]

    @pl.when(pl.program_id(0) == 0)
    def _():
        wide_ref[:, :HEAD_SIZE] = v_ref[...]
        wide_ref[:, HEAD_SIZE:] = jnp.ones((span, HEAD_SIZE), BF16)

    prefix = prefix_ref[0]
    for r0, limit in block_limits(span, tile):
        rows = slice(r0, r0 + tile)
        scores = mm_t(q_ref[rows, :], k_ref[:limit, :])
        weights = masked(jnp.exp2(scores * LOG2_SCALE), r0, limit, prefix)
        sums = mm(weights.astype(BF16), wide_ref[:limit, :])
        inverse = 1.0 / sums[:, HEAD_SIZE:]
        o_ref[rows, :] = (sums[:, :HEAD_SIZE] * inverse).astype(BF16)
        l_ref[rows, :] = inverse


def attend(prefix, q, k, v):
    span, width = q.shape
    heads = width // HEAD_SIZE
    head = pl.BlockSpec((span, HEAD_SIZE), lambda h: (0, h))
    shared = pl.BlockSpec((span, HEAD_SIZE), lambda h: (0, 0))
    return pl.pallas_call(
        functools.partial(attend_kernel, 256),
        grid=(heads,),
        in_specs=[pl.BlockSpec(memory_space=pltpu.SMEM), head, shared, shared],
        out_specs=[head, head],
        out_shape=[jax.ShapeDtypeStruct((span, width), BF16), jax.ShapeDtypeStruct((span, width), F32)],
        scratch_shapes=[pltpu.VMEM((span, 2 * HEAD_SIZE), BF16)],
        compiler_params=pltpu.CompilerParams(vmem_limit_bytes=VMEM_BYTES),
        cost_estimate=pl.CostEstimate(
            flops=8 * heads * span * span * HEAD_SIZE, bytes_accessed=8 * span * width,
            transcendentals=heads * span * span),
        name="attend",
    )(prefix, q, k, v)


def attend_back_kernel(tile, prefix_ref, q_ref, k_ref, v_ref, o_ref, l_ref, do_ref, qraw_ref, kraw_ref, cos_ref, sin_ref,
                       qg_ref, kg_ref, dq_ref, dk_ref, dv_ref, qgg_ref, kgg_ref, dk_sum, dv_sum):
    span = q_ref.shape[0]
    step = pl.program_id(0)

    @pl.when(step == 0)
    def _():
        dk_sum[...] = jnp.zeros_like(dk_sum)
        dv_sum[...] = jnp.zeros_like(dv_sum)
        qgg_ref[...] = jnp.zeros_like(qgg_ref)

    def unturned(grad, rows):
        return grad * cos_ref[rows, :] - pltpu.roll(grad, HEAD_SIZE // 2, 1) * sin_ref[rows, :]

    prefix = prefix_ref[0]
    for r0, limit in block_limits(span, tile):
        rows = slice(r0, r0 + tile)
        q, do = q_ref[rows, :], do_ref[rows, :]
        keys, values = k_ref[:limit, :], v_ref[:limit, :]
        weights = masked(jnp.exp2(mm_t(q, keys) * LOG2_SCALE), r0, limit, prefix)
        probs = weights * jnp.concatenate([l_ref[rows, :]] * (limit // HEAD_SIZE), axis=1)
        delta = jnp.sum(do.astype(F32) * o_ref[rows, :].astype(F32), axis=1, keepdims=True)
        score_grad = (probs * (mm_t(do, values) - delta)).astype(BF16)
        dv_sum[:limit, :] += t_mm(probs.astype(BF16), do)
        dk_sum[:limit, :] += t_mm(score_grad, q)
        turn = unturned(mm(score_grad, keys) * SOFTMAX_SCALE, rows)
        raw = qraw_ref[rows, :]
        back, terms = normalize_back(turn, raw, row_scale(raw), qg_ref[...])
        dq_ref[rows, :] = back.astype(BF16)
        qgg_ref[...] += jnp.sum(terms, axis=0, keepdims=True)

    @pl.when(step == pl.num_programs(0) - 1)
    def _():
        raw = kraw_ref[...]
        turn = unturned(dk_sum[...] * SOFTMAX_SCALE, slice(None))
        back, terms = normalize_back(turn, raw, row_scale(raw), kg_ref[...])
        dk_ref[...] = back.astype(BF16)
        dv_ref[...] = dv_sum[...].astype(BF16)
        kgg_ref[...] = jnp.sum(terms, axis=0, keepdims=True)


def attend_back(prefix, q, k, v, o, inverse, do, qraw, kraw, cosine, sine, q_gain, k_gain):
    span, width = q.shape
    heads = width // HEAD_SIZE
    head = pl.BlockSpec((span, HEAD_SIZE), lambda h: (0, h))
    shared = pl.BlockSpec((span, HEAD_SIZE), lambda h: (0, 0))
    gain = pl.BlockSpec((1, HEAD_SIZE), lambda h: (0, 0))
    return pl.pallas_call(
        functools.partial(attend_back_kernel, 256),
        grid=(heads,),
        in_specs=[pl.BlockSpec(memory_space=pltpu.SMEM), head, shared, shared, head, head, head, head, shared, shared,
                  shared, gain, gain],
        out_specs=[head, shared, shared, gain, gain],
        out_shape=[
            jax.ShapeDtypeStruct((span, width), BF16),
            jax.ShapeDtypeStruct((span, HEAD_SIZE), BF16),
            jax.ShapeDtypeStruct((span, HEAD_SIZE), BF16),
            jax.ShapeDtypeStruct((1, HEAD_SIZE), F32),
            jax.ShapeDtypeStruct((1, HEAD_SIZE), F32),
        ],
        scratch_shapes=[pltpu.VMEM((span, HEAD_SIZE), F32), pltpu.VMEM((span, HEAD_SIZE), F32)],
        compiler_params=pltpu.CompilerParams(vmem_limit_bytes=VMEM_BYTES),
        cost_estimate=pl.CostEstimate(
            flops=16 * heads * span * span * HEAD_SIZE, bytes_accessed=16 * span * width,
            transcendentals=heads * span * span),
        name="attend_back",
    )(prefix, q, k, v, o, inverse, do, qraw, kraw, cosine, sine, q_gain[None], k_gain[None])


def unproject_kernel(dq_ref, dk_ref, dv_ref, wq_ref, wkv_ref, x_ref, out_ref, sum_ref):
    total = mm_t(dq_ref[...], wq_ref[...])
    total += mm_t(dk_ref[...], wkv_ref[:, :HEAD_SIZE]) + mm_t(dv_ref[...], wkv_ref[:, HEAD_SIZE:])
    out_ref[...] = total.astype(BF16)
    part = jnp.sum(total * x_ref[...].astype(F32), axis=0, keepdims=True)

    @pl.when(pl.program_id(0) == 0)
    def _():
        sum_ref[...] = part

    @pl.when(pl.program_id(0) > 0)
    def _():
        sum_ref[...] += part


def unproject(dq, dk, dv, wq, wkv, x):
    span, model = x.shape
    width = dq.shape[1]
    tile = 256
    row = lambda w: pl.BlockSpec((tile, w), lambda i: (i, 0))
    whole = lambda a, b: pl.BlockSpec((a, b), lambda i: (0, 0))
    return pl.pallas_call(
        unproject_kernel,
        grid=(span // tile,),
        in_specs=[row(width), row(HEAD_SIZE), row(HEAD_SIZE), whole(model, width), whole(model, 2 * HEAD_SIZE), row(model)],
        out_specs=[row(model), whole(1, model)],
        out_shape=[jax.ShapeDtypeStruct((span, model), BF16), jax.ShapeDtypeStruct((1, model), F32)],
        compiler_params=pltpu.CompilerParams(vmem_limit_bytes=VMEM_BYTES),
        cost_estimate=pl.CostEstimate(
            flops=2 * span * model * (width + 256), bytes_accessed=2 * model * (2 * span + width + 256),
            transcendentals=0),
        name="unproject",
    )(dq, dk, dv, wq, wkv, x)


def shards(
    tokens,
    routes,
    prefix_len,
    query_weight,
    key_matrix,
    value_matrix,
    out_weight,
    router_weight,
    attention_gain,
    mixture_gain,
    query_gain,
    key_norm_gain,
    expert_gate,
    expert_up,
    expert_down,
    cotangent,
):
    planes, members = lax.axis_size("dp"), lax.axis_size("expert")
    devices = planes * members
    plane, member = lax.axis_index("dp"), lax.axis_index("expert")
    own_rows, model = tokens.shape
    span = own_rows * members
    column = own_rows * planes
    experts = devices
    width = query_weight.shape[1]
    piece = key_matrix.shape[1]
    group = HEAD_SIZE // piece
    block_slots = max(2, 6 * own_rows * TOP // (5 * experts))
    slots = planes * block_slots
    pad_experts = -(-experts // HEAD_SIZE) * HEAD_SIZE
    gate, up, down = expert_gate[0], expert_up[0], expert_down[0]

    def gather(array, axis, dimension=0):
        return lax.all_gather(array, axis, axis=dimension, tiled=True)

    def exchange(array, axis):
        return lax.all_to_all(array, axis, split_axis=0, concat_axis=0, tiled=True)

    qkv_part = jnp.concatenate([query_weight, key_matrix, value_matrix], axis=1)
    residual_in = tokens.astype(F32)
    scale_attention = row_scale(residual_in)
    normed_own = (residual_in * scale_attention * attention_gain).astype(BF16)
    normed = gather(normed_own, "expert")
    qkv_rows = gather(qkv_part, "dp")
    kv_own = qkv_rows[:, width:]
    place = member % group
    kv_parts = [kv_own]
    for shift in range(1, group):
        pairs = [(e - e % group + (e % group + shift) % group, e) for e in range(members)]
        kv_parts.append(lax.ppermute(kv_own, "expert", pairs))

    def kv_piece(j):
        value = kv_parts[0]
        for shift in range(1, group):
            value = jnp.where((place + shift) % group == j, kv_parts[shift], value)
        return value

    ordered = [kv_piece(j) for j in range(group)]
    kv_weight = jnp.concatenate([p[:, :piece] for p in ordered] + [p[:, piece:] for p in ordered], axis=1)

    cosine, sine = rotary_tables(span)
    qraw, kraw, query_low, key_low, value_low = project(
        normed, qkv_rows, kv_weight, width, cosine, sine, query_gain, key_norm_gain)
    attended_low, inverse = attend(prefix_len, query_low, key_low, value_low)

    out_columns = gather(out_weight, "dp")
    attended_all = gather(attended_low, "expert").reshape(members, span, width)
    out_by_member = out_columns.reshape(members, width, out_columns.shape[1])
    projected = sum(mm(attended_all[m], out_by_member[m]) for m in range(members))
    out_piece = out_columns.shape[1]
    projected = exchange(projected.astype(BF16), "expert").reshape(members, own_rows, out_piece)
    projected = jnp.transpose(projected, (1, 0, 2)).reshape(own_rows, model)
    out_heads = exchange(out_columns, "expert").reshape(members, width, out_piece)
    out_heads = jnp.transpose(out_heads, (1, 0, 2)).reshape(width, model)

    expert_ids = jnp.arange(experts, dtype=jnp.int32)
    mask_own = jnp.sum((routes[:, :, None] == expert_ids[None, None, :]).astype(F32), axis=1)
    mask_wide = jnp.pad(mask_own, ((0, 0), (0, pad_experts - experts))).astype(BF16)
    upstream_own = jnp.concatenate([cotangent, mask_wide], axis=1)
    upstream_column = gather(upstream_own, "dp")
    mask_plane = lax.dynamic_slice(upstream_column, (0, model + plane * members), (column, members))
    triangle = (jnp.arange(column)[:, None] >= jnp.arange(column)[None, :]).astype(BF16)
    rank = jnp.where(mask_plane > 0, mm(triangle, mask_plane) - 1.0, -1.0).astype(jnp.int32)
    pick = (rank.T[:, None, :] == jnp.arange(slots, dtype=jnp.int32)[None, :, None])
    pick = pick.reshape(members * slots, column).astype(BF16)

    upstream_rows = exchange(mm(pick, upstream_column).astype(BF16), "expert")
    upstream_arrived, mask_arrived = upstream_rows[:, :model], upstream_rows[:, model:model + experts].astype(F32)
    upstream_down = mm_t(upstream_arrived, down)

    router = gather(gather(router_weight.T, "expert"), "dp", 1)

    after_attn = residual_in + projected.astype(F32)
    scale_mixture = row_scale(after_attn)
    mixed_low = (after_attn * scale_mixture * mixture_gain).astype(BF16)
    mixed_column = gather(mixed_low, "dp")
    arrived = exchange(mm(pick, mixed_column).astype(BF16), "expert")

    def route_weights(rows, mask):
        logits = jnp.where(mask > 0, mm_t(rows, router), VERY_NEGATIVE)
        raised = jnp.where(mask > 0, jnp.exp(logits - jnp.max(logits, axis=-1, keepdims=True)), 0.0)
        return raised / jnp.maximum(jnp.sum(raised, axis=-1, keepdims=True), 1e-30)

    own_expert = plane * members + member
    weight_arrived = jnp.sum(
        jnp.where(expert_ids[None, :] == own_expert, route_weights(arrived, mask_arrived), 0.0), axis=-1, keepdims=True)
    weight_own = route_weights(mixed_low, mask_own)

    gate_raw = mm(arrived, gate)
    up_raw = mm(arrived, up)
    gate_sig = jax.nn.sigmoid(gate_raw)
    silu = gate_raw * gate_sig
    activated_full = silu * up_raw
    activated = activated_full.astype(BF16)
    activated_grad = weight_arrived * upstream_down
    gate_grad = (activated_grad * up_raw * gate_sig * (1.0 + gate_raw * (1.0 - gate_sig))).astype(BF16)
    up_grad = (activated_grad * silu).astype(BF16)
    route_grad = jnp.sum(activated.astype(F32) * upstream_down, axis=-1, keepdims=True)
    row_grad = (mm_t(gate_grad, gate) + mm_t(up_grad, up)).astype(BF16)
    here = (expert_ids[None, :] == own_expert).astype(F32)
    route_high = route_grad.astype(BF16)
    route_rest = (route_grad - route_high.astype(F32)).astype(BF16)
    pad_both = -(-2 * experts // HEAD_SIZE) * HEAD_SIZE
    route_columns = jnp.concatenate(
        [here * route_high.astype(F32), here * route_rest.astype(F32),
         jnp.zeros((row_grad.shape[0], pad_both - 2 * experts), F32)], axis=1).astype(BF16)
    back_rows = exchange(jnp.concatenate([row_grad, route_columns], axis=1), "expert")
    back_column = t_mm(pick, back_rows).astype(BF16)
    back_own = lax.psum_scatter(back_column, "dp", scatter_dimension=0, tiled=True).astype(F32)

    produced = (weight_arrived * mm(activated, down)).astype(BF16)
    mixture_rows = exchange(produced, "expert")
    mixture_column = t_mm(pick, mixture_rows).astype(BF16)
    mixture = lax.psum_scatter(mixture_column, "dp", scatter_dimension=0, tiled=True).astype(F32)
    layer_out = (after_attn + mixture).astype(BF16)

    produced_grad = (weight_arrived * upstream_arrived.astype(F32)).astype(BF16)
    down_gradient = t_mm(activated, produced_grad)
    gate_gradient = t_mm(arrived, gate_grad)
    up_gradient = t_mm(arrived, up_grad)

    upstream = cotangent.astype(F32)
    route_back = back_own[:, model:model + experts] + back_own[:, model + experts:model + 2 * experts]
    chosen_grad = weight_own * (route_back - jnp.sum(weight_own * route_back, axis=-1, keepdims=True))
    logit_grad = chosen_grad.astype(BF16)
    mixed_grad = mm(logit_grad, router) + back_own[:, :model]
    mixture_back, mixture_terms = normalize_back(mixed_grad, after_attn, scale_mixture, mixture_gain)
    after_grad = upstream + mixture_back
    after_low = after_grad.astype(BF16)
    router_part = t_mm(logit_grad, mixed_low).astype(BF16)

    after_all = gather(after_low, "expert")
    attended_grad = mm_t(after_all, out_heads).astype(BF16)
    after_columns = lax.dynamic_slice(after_all, (0, member * out_piece), (span, out_piece))
    out_partial = jnp.concatenate([t_mm(attended_all[m], after_columns) for m in range(members)], axis=0)
    out_share = lax.psum_scatter(out_partial.astype(BF16), "dp", scatter_dimension=0, tiled=True).astype(F32)
    dq, dk, dv, query_terms, key_terms = attend_back(
        prefix_len, query_low, key_low, value_low, attended_low, inverse, attended_grad, qraw, kraw, cosine, sine,
        query_gain, key_norm_gain)
    normed_partial, attention_terms = unproject(dq, dk, dv, qkv_rows, kv_weight, normed)
    normed_grad = lax.psum_scatter(normed_partial, "expert", scatter_dimension=0, tiled=True).astype(F32)
    input_back, _ = normalize_back(normed_grad, residual_in, scale_attention, attention_gain)
    input_grad = after_grad + input_back

    query_partial = t_mm(normed, dq).astype(BF16)
    kv_partial = jnp.concatenate([t_mm(normed, dk), t_mm(normed, dv)], axis=1)

    def kv_cols(j):
        start = j * piece
        return jnp.concatenate(
            [lax.dynamic_slice(kv_partial, (0, start), (model, piece)),
             lax.dynamic_slice(kv_partial, (0, HEAD_SIZE + start), (model, piece))], axis=1)

    kv_total = kv_cols(place)
    for shift in range(1, group):
        pairs = [(e, e - e % group + (e % group + shift) % group) for e in range(members)]
        kv_total += lax.ppermute(kv_cols((place + shift) % group).astype(BF16), "expert", pairs).astype(F32)
    qkv_partial = jnp.concatenate([query_partial, kv_total.astype(BF16)], axis=1)
    qkv_share = lax.psum_scatter(qkv_partial, "dp", scatter_dimension=0, tiled=True).astype(F32)
    query_share = qkv_share[:, :width]
    key_share = qkv_share[:, width:width + piece]
    value_share = qkv_share[:, width + piece:]

    router_share = lax.psum_scatter(router_part, "expert", scatter_dimension=0, tiled=True)
    router_share = lax.psum_scatter(router_share, "dp", scatter_dimension=1, tiled=True).astype(F32).T

    attention_total, mixture_total, query_total, key_total = lax.psum(
        (attention_terms[0] / attention_gain, jnp.sum(mixture_terms, axis=0), query_terms[0], key_terms[0]),
        ("dp", "expert"))
    return (
        layer_out,
        input_grad,
        query_share,
        key_share,
        value_share,
        out_share,
        router_share,
        attention_total,
        mixture_total,
        query_total,
        key_total,
        gate_gradient[None],
        up_gradient[None],
        down_gradient[None],
    )


def solution(mesh):
    rows = P(("dp", "expert"), None)
    grid = P("dp", "expert")
    experts = P(("dp", "expert"), None, None)
    in_specs = (rows, rows, P("dp"), grid, grid, grid, grid, grid, P(), P(), P(), P(), experts, experts, experts, rows)
    out_specs = (rows, rows, grid, grid, grid, grid, grid, P(), P(), P(), P(), experts, experts, experts)
    return jax.shard_map(shards, mesh=mesh, in_specs=in_specs, out_specs=out_specs, check_vma=False)
```

```python
import functools
import math

import jax
import jax.numpy as jnp
from jax import lax
from jax.experimental import pallas as pl
from jax.experimental.pallas import tpu as pltpu
from jax.sharding import PartitionSpec as P

QUERY_HEADS = 32
KEY_VALUE_HEADS = 4
HEAD_SIZE = 128
TOP = 8
EPS = 1e-06
ROTARY_BASE = 1000000.0
VERY_NEGATIVE = -1e30
SOFTMAX_SCALE = HEAD_SIZE ** (-0.5)
LOG2_SCALE = SOFTMAX_SCALE * math.log2(math.e)
VMEM_BYTES = 56 * 1024 * 1024
F32 = jnp.float32
BF16 = jnp.bfloat16


def cost(microseconds):
    return pl.CostEstimate(flops=int(microseconds * 1.1e9) + 1, bytes_accessed=1, transcendentals=0)


def mm(a, b):
    return lax.dot_general(a, b, (((1,), (0,)), ((), ())), preferred_element_type=F32)


def mm_t(a, b):
    return lax.dot_general(a, b, (((1,), (1,)), ((), ())), preferred_element_type=F32)


def t_mm(a, b):
    return lax.dot_general(a, b, (((0,), (0,)), ((), ())), preferred_element_type=F32)


def row_scale(source):
    return lax.rsqrt(jnp.mean(source * source, axis=-1, keepdims=True) + EPS)


def normalize_back(upstream, source, scaling, gain_row):
    unit_rows = source * scaling
    weighted = upstream * gain_row
    inner_mean = jnp.mean(weighted * unit_rows, axis=-1, keepdims=True)
    return (scaling * (weighted - unit_rows * inner_mean), upstream * unit_rows)


def rotary_tables(span):
    half = HEAD_SIZE // 2
    frequency = jnp.power(ROTARY_BASE, -jnp.arange(half, dtype=F32) * 2.0 / HEAD_SIZE)
    angles = jnp.arange(span, dtype=jnp.int32).astype(F32)[:, None] * frequency[None, :]
    cosine, sine = jnp.cos(angles), jnp.sin(angles)
    return (
        jnp.concatenate([cosine, cosine], axis=-1),
        jnp.concatenate([-sine, sine], axis=-1),
    )


def turned(u, gain, cosine, sine):
    n = u * row_scale(u) * gain
    return (n * cosine + pltpu.roll(n, HEAD_SIZE // 2, 1) * sine).astype(BF16)


def pieces_product(x, refs):
    size = refs[0].shape[0]
    total = mm(x[:, :size], refs[0][...])
    for s in range(1, len(refs)):
        total += mm(x[:, s * size:(s + 1) * size], refs[s][...])
    return total


def project_query_kernel(x_ref, cos_ref, sin_ref, gain_ref, *refs):
    raw_ref, low_ref = refs[-2:]
    q = pieces_product(x_ref[...], refs[:-2])
    raw_ref[...] = q
    for h in range(q.shape[1] // HEAD_SIZE):
        cols = slice(h * HEAD_SIZE, (h + 1) * HEAD_SIZE)
        low_ref[:, cols] = turned(q[:, cols], gain_ref[...], cos_ref[...], sin_ref[...])


def project_key_kernel(x_ref, cos_ref, sin_ref, gain_ref, w_ref, raw_ref, k_ref, v_ref):
    kv = mm(x_ref[...], w_ref[...])
    raw_ref[...] = kv[:, :HEAD_SIZE]
    v_ref[...] = kv[:, HEAD_SIZE:].astype(BF16)
    k_ref[...] = turned(kv[:, :HEAD_SIZE], gain_ref[...], cos_ref[...], sin_ref[...])


def project(kernel, x, weights, cosine, sine, gain, out):
    span, model = x.shape
    tile = 512
    row = lambda w: pl.BlockSpec((tile, w), lambda i: (i, 0))
    whole = lambda a, b: pl.BlockSpec((a, b), lambda i: (0, 0))
    return pl.pallas_call(
        kernel,
        grid=(span // tile,),
        in_specs=[row(model), row(HEAD_SIZE), row(HEAD_SIZE), whole(1, HEAD_SIZE)] + [whole(*w.shape) for w in weights],
        out_specs=[row(w) for w, _ in out],
        out_shape=[jax.ShapeDtypeStruct((span, w), t) for w, t in out],
        compiler_params=pltpu.CompilerParams(vmem_limit_bytes=VMEM_BYTES),
        cost_estimate=cost(0),
        name=kernel.__name__,
    )(x, cosine, sine, gain[None], *weights)


def block_limits(span, tile):
    return [(r0, max(r0 + tile, span // 2)) for r0 in range(0, span, tile)]


def masked(values, r0, limit, prefix):
    tile = values.shape[0]
    rows = r0 + lax.broadcasted_iota(jnp.int32, (tile, limit - r0), 0)
    cols = r0 + lax.broadcasted_iota(jnp.int32, (tile, limit - r0), 1)
    right = jnp.where((cols <= rows) | (cols < prefix), values[:, r0:], 0.0)
    return right if r0 == 0 else jnp.concatenate([values[:, :r0], right], axis=1)


def attend_kernel(tile, prefix_ref, q_ref, k_ref, v_ref, o_ref, l_ref, wide_ref):
    span = q_ref.shape[0]

    @pl.when(pl.program_id(0) == 0)
    def _():
        wide_ref[:, :HEAD_SIZE] = v_ref[...]
        wide_ref[:, HEAD_SIZE:] = jnp.ones((span, HEAD_SIZE), BF16)

    prefix = prefix_ref[0]
    for r0, limit in block_limits(span, tile):
        rows = slice(r0, r0 + tile)
        scores = mm_t(q_ref[rows, :], k_ref[:limit, :])
        weights = masked(jnp.exp2(scores * LOG2_SCALE), r0, limit, prefix)
        sums = mm(weights.astype(BF16), wide_ref[:limit, :])
        inverse = 1.0 / sums[:, HEAD_SIZE:]
        o_ref[rows, :] = (sums[:, :HEAD_SIZE] * inverse).astype(BF16)
        l_ref[rows, :] = inverse


def attend(prefix, q, k, v):
    span, width = q.shape
    heads = width // HEAD_SIZE
    head = pl.BlockSpec((span, HEAD_SIZE), lambda h: (0, h))
    shared = pl.BlockSpec((span, HEAD_SIZE), lambda h: (0, 0))
    return pl.pallas_call(
        functools.partial(attend_kernel, 256),
        grid=(heads,),
        in_specs=[pl.BlockSpec(memory_space=pltpu.SMEM), head, shared, shared],
        out_specs=[head, head],
        out_shape=[jax.ShapeDtypeStruct((span, width), BF16), jax.ShapeDtypeStruct((span, width), F32)],
        scratch_shapes=[pltpu.VMEM((span, 2 * HEAD_SIZE), BF16)],
        compiler_params=pltpu.CompilerParams(vmem_limit_bytes=VMEM_BYTES),
        cost_estimate=cost(0),
        name="attend",
    )(prefix, q, k, v)


def attend_back_kernel(tile, prefix_ref, q_ref, k_ref, v_ref, o_ref, l_ref, do_ref, qraw_ref, kraw_ref, cos_ref, sin_ref,
                       qg_ref, kg_ref, dq_ref, dk_ref, dv_ref, qgg_ref, kgg_ref, dk_sum, dv_sum):
    span = q_ref.shape[0]
    step = pl.program_id(0)

    @pl.when(step == 0)
    def _():
        dk_sum[...] = jnp.zeros_like(dk_sum)
        dv_sum[...] = jnp.zeros_like(dv_sum)
        qgg_ref[...] = jnp.zeros_like(qgg_ref)

    def unturned(grad, rows):
        return grad * cos_ref[rows, :] - pltpu.roll(grad, HEAD_SIZE // 2, 1) * sin_ref[rows, :]

    prefix = prefix_ref[0]
    for r0, limit in block_limits(span, tile):
        rows = slice(r0, r0 + tile)
        q, do = q_ref[rows, :], do_ref[rows, :]
        keys, values = k_ref[:limit, :], v_ref[:limit, :]
        weights = masked(jnp.exp2(mm_t(q, keys) * LOG2_SCALE), r0, limit, prefix)
        probs = weights * jnp.concatenate([l_ref[rows, :]] * (limit // HEAD_SIZE), axis=1)
        delta = jnp.sum(do.astype(F32) * o_ref[rows, :].astype(F32), axis=1, keepdims=True)
        score_grad = (probs * (mm_t(do, values) - delta)).astype(BF16)
        dv_sum[:limit, :] += t_mm(probs.astype(BF16), do)
        dk_sum[:limit, :] += t_mm(score_grad, q)
        turn = unturned(mm(score_grad, keys) * SOFTMAX_SCALE, rows)
        raw = qraw_ref[rows, :]
        back, terms = normalize_back(turn, raw, row_scale(raw), qg_ref[...])
        dq_ref[rows, :] = back.astype(BF16)
        qgg_ref[...] += jnp.sum(terms, axis=0, keepdims=True)

    @pl.when(step == pl.num_programs(0) - 1)
    def _():
        raw = kraw_ref[...]
        turn = unturned(dk_sum[...] * SOFTMAX_SCALE, slice(None))
        back, terms = normalize_back(turn, raw, row_scale(raw), kg_ref[...])
        dk_ref[...] = back.astype(BF16)
        dv_ref[...] = dv_sum[...].astype(BF16)
        kgg_ref[...] = jnp.sum(terms, axis=0, keepdims=True)


def attend_back(prefix, q, k, v, o, inverse, do, qraw, kraw, cosine, sine, q_gain, k_gain):
    span, width = q.shape
    heads = width // HEAD_SIZE
    head = pl.BlockSpec((span, HEAD_SIZE), lambda h: (0, h))
    shared = pl.BlockSpec((span, HEAD_SIZE), lambda h: (0, 0))
    gain = pl.BlockSpec((1, HEAD_SIZE), lambda h: (0, 0))
    return pl.pallas_call(
        functools.partial(attend_back_kernel, 256),
        grid=(heads,),
        in_specs=[pl.BlockSpec(memory_space=pltpu.SMEM), head, shared, shared, head, head, head, head, shared, shared,
                  shared, gain, gain],
        out_specs=[head, shared, shared, gain, gain],
        out_shape=[
            jax.ShapeDtypeStruct((span, width), BF16),
            jax.ShapeDtypeStruct((span, HEAD_SIZE), BF16),
            jax.ShapeDtypeStruct((span, HEAD_SIZE), BF16),
            jax.ShapeDtypeStruct((1, HEAD_SIZE), F32),
            jax.ShapeDtypeStruct((1, HEAD_SIZE), F32),
        ],
        scratch_shapes=[pltpu.VMEM((span, HEAD_SIZE), F32), pltpu.VMEM((span, HEAD_SIZE), F32)],
        compiler_params=pltpu.CompilerParams(vmem_limit_bytes=VMEM_BYTES),
        cost_estimate=cost(0),
        name="attend_back",
    )(prefix, q, k, v, o, inverse, do, qraw, kraw, cosine, sine, q_gain[None], k_gain[None])


def unproject_kernel(own_rows, dq_ref, dk_ref, dv_ref, wkv_ref, x_ref, gain_ref, router_ref, mix_ref, qg_ref, kg_ref,
                     *refs):
    weights, out_ref, sum_ref = refs[:-2], refs[-2], refs[-1]
    span, model = x_ref.shape
    size = weights[0].shape[0]
    tile = 512
    each = tile // own_rows
    for r in range(span // tile):
        rows = slice(r * tile, (r + 1) * tile)
        dq, dk, dv = dq_ref[rows, :], dk_ref[rows, :], dv_ref[rows, :]
        for s, weight in enumerate(weights):
            cols = slice(s * size, (s + 1) * size)
            total = mm_t(dq, weight[...])
            total += mm_t(dk, wkv_ref[cols, :HEAD_SIZE]) + mm_t(dv, wkv_ref[cols, HEAD_SIZE:])
            low = total.astype(BF16)
            for m in range(each):
                out_ref[r * each + m, :own_rows, cols] = low[m * own_rows:(m + 1) * own_rows]
            part = jnp.sum(total * x_ref[rows, cols].astype(F32), axis=0, keepdims=True)
            if r == 0:
                sum_ref[:, cols] = part
            else:
                sum_ref[:, cols] += part
    heads = jnp.concatenate([qg_ref[...], kg_ref[...], jnp.zeros((1, model - 2 * HEAD_SIZE), F32)], axis=1)
    place = lax.broadcasted_iota(jnp.int32, (8, model), 0)
    sums = jnp.zeros((8, model), F32)
    for n, values in enumerate((sum_ref[...] / gain_ref[...], mix_ref[...], heads)):
        high = values.astype(BF16).astype(F32)
        sums = jnp.where(place == 2 * n, high, jnp.where(place == 2 * n + 1, values - high, sums))
    sums = sums.astype(BF16)
    for m in range(out_ref.shape[0]):
        out_ref[m, own_rows:own_rows + 8, :] = router_ref[m]
        out_ref[m, own_rows + 8:, :] = sums


def unproject(own_rows, dq, dk, dv, pieces, wkv, x, gain, router_part, mixture_part, query_part, key_part):
    span, model = x.shape
    return pl.pallas_call(
        functools.partial(unproject_kernel, own_rows),
        out_shape=jax.ShapeDtypeStruct((span // own_rows, own_rows + 16, model), BF16),
        scratch_shapes=[pltpu.VMEM((1, model), F32)],
        compiler_params=pltpu.CompilerParams(vmem_limit_bytes=VMEM_BYTES),
        cost_estimate=cost(0),
        name="unproject",
    )(dq, dk, dv, wkv, x, gain[None], router_part, mixture_part, query_part, key_part, *pieces)


def out_project_kernel(a_ref, w_ref, out_ref):
    total = mm(a_ref[0], w_ref[0])
    for m in range(1, a_ref.shape[0]):
        total += mm(a_ref[m], w_ref[m])
    out_ref[...] = total.astype(BF16)


def out_project(attended_all, weight):
    members, span, width = attended_all.shape
    columns = weight.shape[2]
    tile = 512
    return pl.pallas_call(
        out_project_kernel,
        grid=(span // tile,),
        in_specs=[pl.BlockSpec((members, tile, width), lambda i: (0, i, 0)),
                  pl.BlockSpec((members, width, columns), lambda i: (0, 0, 0))],
        out_specs=pl.BlockSpec((tile, columns), lambda i: (i, 0)),
        out_shape=jax.ShapeDtypeStruct((span, columns), BF16),
        compiler_params=pltpu.CompilerParams(vmem_limit_bytes=VMEM_BYTES),
        cost_estimate=cost(0),
        name="out_project",
    )(attended_all, weight)


def out_back_kernel(g_ref, w_ref, out_ref):
    columns = w_ref.shape[2]
    total = mm_t(g_ref[:, :columns], w_ref[0])
    for m in range(1, w_ref.shape[0]):
        total += mm_t(g_ref[:, m * columns:(m + 1) * columns], w_ref[m])
    out_ref[...] = total.astype(BF16)


def out_back(after_all, heads):
    span, model = after_all.shape
    members, width, columns = heads.shape
    tile = 512
    return pl.pallas_call(
        out_back_kernel,
        grid=(span // tile,),
        in_specs=[pl.BlockSpec((tile, model), lambda i: (i, 0)),
                  pl.BlockSpec((members, width, columns), lambda i: (0, 0, 0))],
        out_specs=pl.BlockSpec((tile, width), lambda i: (i, 0)),
        out_shape=jax.ShapeDtypeStruct((span, width), BF16),
        compiler_params=pltpu.CompilerParams(vmem_limit_bytes=VMEM_BYTES),
        cost_estimate=cost(0),
        name="out_back",
    )(after_all, heads)


def out_gradient_kernel(member_ref, a_ref, g_ref, out_ref):
    out_ref[0] = t_mm(a_ref[0], g_ref[...]).astype(BF16)


def out_gradient(member, attended_all, after_all, columns):
    members, span, width = attended_all.shape
    return pl.pallas_call(
        out_gradient_kernel,
        grid_spec=pltpu.PrefetchScalarGridSpec(
            num_scalar_prefetch=1,
            grid=(members,),
            in_specs=[pl.BlockSpec((1, span, width), lambda m, me: (m, 0, 0)),
                      pl.BlockSpec((span, columns), lambda m, me: (0, me[0]))],
            out_specs=pl.BlockSpec((1, width, columns), lambda m, me: (m, 0, 0)),
        ),
        out_shape=jax.ShapeDtypeStruct((members, width, columns), BF16),
        compiler_params=pltpu.CompilerParams(vmem_limit_bytes=VMEM_BYTES),
        cost_estimate=cost(0),
        name="out_gradient",
    )(member, attended_all, after_all)


def expert_kernel(experts, own_ref, xa_ref, xb_ref, mask_ref, router_ref, gate_ref, up_ref, down_ref,
                  act_ref, gg_ref, ug_ref, w_ref, route_ref, sum_ref):
    half = xa_ref.shape[1]
    step = pl.program_id(0)
    own = own_ref[0]

    def product(left, right, weight):
        return mm(left[...], weight[:half, :]) + mm(right[...], weight[half:, :])

    @pl.when(step == 0)
    def _():
        mask = mask_ref[...].astype(F32)
        logits = mm_t(xa_ref[...], router_ref[:, :half]) + mm_t(xb_ref[...], router_ref[:, half:])
        logits = jnp.where(mask > 0, logits, VERY_NEGATIVE)
        raised = jnp.where(mask > 0, jnp.exp(logits - jnp.max(logits, axis=-1, keepdims=True)), 0.0)
        total = jnp.maximum(jnp.sum(raised, axis=-1, keepdims=True), 1e-30)
        lanes = lax.broadcasted_iota(jnp.int32, raised.shape, 1)
        weight = jnp.sum(jnp.where(lanes == own, raised, 0.0), axis=-1, keepdims=True) / total
        w_ref[...] = jnp.broadcast_to(weight, w_ref.shape)

    gate_raw, up_raw = product(xa_ref, xb_ref, gate_ref), product(xa_ref, xb_ref, up_ref)
    down = down_ref[...]
    weight = w_ref[:, :1]
    sig = 1.0 / (1.0 + jnp.exp(-gate_raw))
    silu = gate_raw * sig
    activated = (silu * up_raw).astype(BF16)
    act_ref[...] = activated
    route = jnp.sum(activated.astype(F32) * down, axis=-1, keepdims=True)
    grad = weight * down
    gg_ref[...] = (grad * up_raw * sig * (1.0 + gate_raw * (1.0 - sig))).astype(BF16)
    ug_ref[...] = (grad * silu).astype(BF16)
    route = jnp.broadcast_to(route, sum_ref.shape)

    @pl.when(step == 0)
    def _():
        sum_ref[...] = route

    @pl.when(step > 0)
    def _():
        sum_ref[...] += route

    @pl.when(step == pl.num_programs(0) - 1)
    def _():
        total = sum_ref[:, :1]
        high = total.astype(BF16).astype(F32)
        lanes = lax.broadcasted_iota(jnp.int32, route_ref.shape, 1)
        route_ref[...] = jnp.where(
            lanes == own, high, jnp.where(lanes == experts + own, total - high, 0.0)).astype(BF16)


def expert_forward(experts, own, xa, xb, masked_rows, router, gate, up, upstream_down):
    rows, half = xa.shape
    model, hidden = gate.shape
    padded = router.shape[0]
    route_width = -(-2 * experts // HEAD_SIZE) * HEAD_SIZE
    tile = 256
    whole = lambda a, b: pl.BlockSpec((a, b), lambda i: (0, 0))
    column = lambda a: pl.BlockSpec((a, tile), lambda i: (0, i))
    return pl.pallas_call(
        functools.partial(expert_kernel, experts),
        grid=(hidden // tile,),
        in_specs=[pl.BlockSpec(memory_space=pltpu.SMEM), whole(rows, half), whole(rows, half),
                  pl.BlockSpec((rows, padded), lambda i: (0, model // padded)), whole(padded, model), column(model),
                  column(model), column(rows)],
        out_specs=[column(rows), column(rows), column(rows), whole(rows, HEAD_SIZE), whole(rows, route_width)],
        out_shape=[
            jax.ShapeDtypeStruct((rows, hidden), BF16),
            jax.ShapeDtypeStruct((rows, hidden), BF16),
            jax.ShapeDtypeStruct((rows, hidden), BF16),
            jax.ShapeDtypeStruct((rows, HEAD_SIZE), F32),
            jax.ShapeDtypeStruct((rows, route_width), BF16),
        ],
        scratch_shapes=[pltpu.VMEM((rows, HEAD_SIZE), F32)],
        compiler_params=pltpu.CompilerParams(vmem_limit_bytes=VMEM_BYTES),
        cost_estimate=cost(18),
        name="expert_forward",
    )(own, xa, xb, masked_rows, router, gate, up, upstream_down)


def row_gradient_kernel(gg_ref, ug_ref, gate_ref, up_ref, *rest):
    total = (mm_t(gg_ref[...], gate_ref[...]) + mm_t(ug_ref[...], up_ref[...])).astype(BF16)
    out_ref = rest[-1]
    out_ref[:, :total.shape[1]] = total
    if len(rest) == 2:
        out_ref[:, total.shape[1]:] = rest[0][...]


def row_gradient(gg, ug, gate, up, part, route=None):
    rows, hidden = gg.shape
    half = gate.shape[0] // 2
    tile = rows // 4
    row = lambda w: pl.BlockSpec((tile, w), lambda i: (i, 0))
    weight = pl.BlockSpec((half, hidden), lambda i: (part, 0))
    extra = [] if route is None else [route]
    width = half + sum(e.shape[1] for e in extra)
    return pl.pallas_call(
        row_gradient_kernel,
        grid=(rows // tile,),
        in_specs=[row(hidden), row(hidden), weight, weight] + [row(e.shape[1]) for e in extra],
        out_specs=row(width),
        out_shape=jax.ShapeDtypeStruct((rows, width), BF16),
        compiler_params=pltpu.CompilerParams(vmem_limit_bytes=VMEM_BYTES),
        cost_estimate=cost(8),
        name="row_gradient",
    )(gg, ug, gate, up, *extra)


def down_back_kernel(c_ref, down_ref, out_ref):
    out_ref[...] = mm_t(c_ref[...], down_ref[...])


def down_back(upstream_rows, down):
    rows = upstream_rows.shape[0]
    hidden, model = down.shape
    tile = 256
    return pl.pallas_call(
        down_back_kernel,
        grid=(hidden // tile,),
        in_specs=[pl.BlockSpec((rows, model), lambda i: (0, 0)), pl.BlockSpec((tile, model), lambda i: (i, 0))],
        out_specs=pl.BlockSpec((rows, tile), lambda i: (0, i)),
        out_shape=jax.ShapeDtypeStruct((rows, hidden), F32),
        compiler_params=pltpu.CompilerParams(vmem_limit_bytes=VMEM_BYTES),
        cost_estimate=cost(8),
        name="down_back",
    )(upstream_rows, down)


def produce_kernel(act_ref, w_ref, down_ref, *outs):
    total = (w_ref[:, :1] * mm(act_ref[...], down_ref[...])).astype(BF16)
    half = total.shape[1] // 2
    outs[0][...] = total[:, :half]
    outs[1][...] = total[:, half:]


def produce(activated, weight, down):
    rows, hidden = activated.shape
    model = down.shape[1]
    tile = rows // 4
    row = lambda w: pl.BlockSpec((tile, w), lambda i: (i, 0))
    return pl.pallas_call(
        produce_kernel,
        grid=(rows // tile,),
        in_specs=[row(hidden), row(HEAD_SIZE), pl.BlockSpec((hidden, model), lambda i: (0, 0))],
        out_specs=[row(model // 2)] * 2,
        out_shape=[jax.ShapeDtypeStruct((rows, model // 2), BF16)] * 2,
        compiler_params=pltpu.CompilerParams(vmem_limit_bytes=VMEM_BYTES),
        cost_estimate=cost(0),
        name="produce",
    )(activated, weight, down)


def hidden_gradient_kernel(xa_ref, xb_ref, gg_ref, ug_ref, dg_ref, du_ref):
    in_first = pl.program_id(0) < pl.num_programs(0) // 2
    for x_ref, now in ((xa_ref, in_first), (xb_ref, jnp.logical_not(in_first))):
        @pl.when(now)
        def _():
            dg_ref[0] = t_mm(x_ref[...], gg_ref[...])
            du_ref[0] = t_mm(x_ref[...], ug_ref[...])


def hidden_gradient(xa, xb, gg, ug):
    rows, half = xa.shape
    hidden = gg.shape[1]
    tile = 256
    count = half // tile
    whole = pl.BlockSpec((rows, hidden), lambda i: (0, 0))
    out = pl.BlockSpec((1, tile, hidden), lambda i: (0, i, 0))
    return pl.pallas_call(
        hidden_gradient_kernel,
        grid=(2 * count,),
        in_specs=[pl.BlockSpec((rows, tile), lambda i: (0, jnp.minimum(i, count - 1))),
                  pl.BlockSpec((rows, tile), lambda i: (0, jnp.maximum(i - count, 0))), whole, whole],
        out_specs=[out, out],
        out_shape=[jax.ShapeDtypeStruct((1, 2 * half, hidden), F32)] * 2,
        compiler_params=pltpu.CompilerParams(vmem_limit_bytes=VMEM_BYTES),
        cost_estimate=cost(0),
        name="hidden_gradient",
    )(xa, xb, gg, ug)


def down_gradient_kernel(c_ref, w_ref, act_ref, out_ref):
    out_ref[0] = t_mm(act_ref[...], (w_ref[:, :1] * c_ref[...].astype(F32)).astype(BF16))


def down_gradient(upstream_rows, model, weight, activated):
    rows, hidden = activated.shape
    tile = 256
    return pl.pallas_call(
        down_gradient_kernel,
        grid=(model // tile,),
        in_specs=[pl.BlockSpec((rows, tile), lambda i: (0, i)), pl.BlockSpec((rows, HEAD_SIZE), lambda i: (0, 0)),
                  pl.BlockSpec((rows, hidden), lambda i: (0, 0))],
        out_specs=pl.BlockSpec((1, hidden, tile), lambda i: (0, 0, i)),
        out_shape=jax.ShapeDtypeStruct((1, hidden, model), F32),
        compiler_params=pltpu.CompilerParams(vmem_limit_bytes=VMEM_BYTES),
        cost_estimate=cost(0),
        name="down_gradient",
    )(upstream_rows, weight, activated)


def dispatch_kernel(pick_ref, *refs):
    out_ref, all_ref = refs[-2:]
    size = all_ref.shape[0] // (len(refs) - 2)

    @pl.when(pl.program_id(0) == 0)
    def _():
        for s, ref in enumerate(refs[:-2]):
            all_ref[s * size:(s + 1) * size, :] = ref[...]

    out_ref[...] = mm(pick_ref[...], all_ref[...]).astype(BF16)


def dispatch(pick, pieces):
    rows, column = pick.shape
    size, width = column // len(pieces), pieces[0].shape[1]
    tile = rows // 4
    return pl.pallas_call(
        dispatch_kernel,
        grid=(rows // tile,),
        in_specs=[pl.BlockSpec((tile, column), lambda i: (i, 0))]
        + [pl.BlockSpec((size, width), lambda i: (0, 0))] * len(pieces),
        out_specs=pl.BlockSpec((tile, width), lambda i: (i, 0)),
        out_shape=jax.ShapeDtypeStruct((rows, width), BF16),
        scratch_shapes=[pltpu.VMEM((column, width), BF16)],
        compiler_params=pltpu.CompilerParams(vmem_limit_bytes=VMEM_BYTES),
        cost_estimate=cost(0),
        name="dispatch",
    )(pick, *pieces)


def combine_kernel(pick_ref, rows_ref, *outs):
    total = mm(pick_ref[...], rows_ref[...]).astype(BF16)
    size = total.shape[0] // len(outs)
    for s, out in enumerate(outs):
        out[...] = total[s * size:(s + 1) * size]


def combine(pick, rows, count, microseconds=0):
    column, slots = pick.shape
    width = rows.shape[1]
    tile = math.gcd(width, 512)
    size = column // count
    out = pl.BlockSpec((size, tile), lambda i: (0, i))
    return pl.pallas_call(
        combine_kernel,
        grid=(width // tile,),
        in_specs=[pl.BlockSpec((column, slots), lambda i: (0, 0)), pl.BlockSpec((slots, tile), lambda i: (0, i))],
        out_specs=[out] * count,
        out_shape=[jax.ShapeDtypeStruct((size, width), BF16)] * count,
        compiler_params=pltpu.CompilerParams(vmem_limit_bytes=VMEM_BYTES),
        cost_estimate=cost(microseconds),
        name="combine",
    )(pick, rows)


def after(array, *earlier):
    return lax.optimization_barrier((array, *earlier))[0]


def shards(
    tokens,
    routes,
    prefix_len,
    query_weight,
    key_matrix,
    value_matrix,
    out_weight,
    router_weight,
    attention_gain,
    mixture_gain,
    query_gain,
    key_norm_gain,
    expert_gate,
    expert_up,
    expert_down,
    cotangent,
):
    planes, members = lax.axis_size("dp"), lax.axis_size("expert")
    devices = planes * members
    plane, member = lax.axis_index("dp"), lax.axis_index("expert")
    own_rows, model = tokens.shape
    span = own_rows * members
    column = own_rows * planes
    experts = devices
    width = query_weight.shape[1]
    piece = key_matrix.shape[1]
    group = HEAD_SIZE // piece
    block_slots = max(2, 6 * own_rows * TOP // (5 * experts))
    slots = planes * block_slots
    padded = -(-experts // HEAD_SIZE) * HEAD_SIZE
    half = model // 2
    part_rows = model // planes
    gate, up, down = expert_gate[0], expert_up[0], expert_down[0]

    def gather(array, axis, dimension=0):
        return lax.all_gather(array, axis, axis=dimension, tiled=True)

    def exchange(array, axis):
        return lax.all_to_all(array, axis, split_axis=0, concat_axis=0, tiled=True)

    def plane_pieces(array):
        def shift(value, by):
            return lax.ppermute(value, "dp", [(i, (i + by) % planes) for i in range(planes)])

        pieces = [array] + [None] * (planes - 1)
        for s in range(1, planes // 2 + 1):
            pieces[s] = shift(pieces[s - 1], 1)
            if planes - s > s:
                pieces[planes - s] = shift(pieces[(planes - s + 1) % planes], -1)
        return pieces

    def plane_sum(pieces):
        total = pieces[0].astype(F32)
        for s in range(1, planes):
            total += lax.ppermute(pieces[s], "dp", [(i, (i - s) % planes) for i in range(planes)]).astype(F32)
        return total

    def reorder(array, dimension):
        size = array.shape[dimension] // planes
        return jnp.concatenate(
            [lax.dynamic_slice_in_dim(array, (plane - s) % planes * size, size, dimension) for s in range(planes)],
            axis=dimension)

    def cut(array):
        return [array[s * (array.shape[0] // planes):(s + 1) * (array.shape[0] // planes)] for s in range(planes)]

    residual_in = tokens.astype(F32)
    scale_attention = row_scale(residual_in)
    normed_own = (residual_in * scale_attention * attention_gain).astype(BF16)
    normed = gather(reorder(normed_own, 1), "expert")

    kv_pieces = plane_pieces(jnp.concatenate([key_matrix, value_matrix], axis=1))
    wq_pieces = plane_pieces(query_weight)
    out_piece = out_weight.shape[1]
    out_columns = gather(after(out_weight, *kv_pieces[1:]), "dp").reshape(members, width, out_piece)

    expert_ids = jnp.arange(experts, dtype=jnp.int32)
    mask_own = jnp.sum((routes[:, :, None] == expert_ids[None, None, :]).astype(F32), axis=1)
    mask_wide = jnp.pad(mask_own, ((0, 0), (0, padded - experts))).astype(BF16)
    router_rows = gather(after(router_weight.T, wq_pieces[1], wq_pieces[-1]), "expert").reshape(members, model)
    upstream_own = jnp.concatenate(
        [jnp.concatenate([cotangent, mask_wide], axis=1), jnp.pad(router_rows, ((0, 0), (0, padded)))], axis=0)
    upstream_pieces = plane_pieces(after(upstream_own, *wq_pieces[1:]))
    cosine, sine = rotary_tables(span)

    kv_own = jnp.concatenate(kv_pieces, axis=0)
    place = member % group
    kv_parts = [kv_own]
    for shift in range(1, group):
        pairs = [(e - e % group + (e % group + shift) % group, e) for e in range(members)]
        kv_parts.append(lax.ppermute(kv_own, "expert", pairs))

    def kv_piece(j):
        value = kv_parts[0]
        for shift in range(1, group):
            value = jnp.where((place + shift) % group == j, kv_parts[shift], value)
        return value

    ordered = [kv_piece(j) for j in range(group)]
    kv_weight = jnp.concatenate([p[:, :piece] for p in ordered] + [p[:, piece:] for p in ordered], axis=1)

    kraw, key_low, value_low = project(
        project_key_kernel, after(normed, cosine, sine, upstream_own), [kv_weight], cosine, sine, key_norm_gain,
        [(HEAD_SIZE, F32), (HEAD_SIZE, BF16), (HEAD_SIZE, BF16)])
    qraw, query_low = project(
        project_query_kernel, normed, wq_pieces, cosine, sine, query_gain, [(width, F32), (width, BF16)])
    attended_low, inverse = attend(prefix_len, after(query_low, out_columns), key_low, value_low)
    attended_all = gather(attended_low, "expert").reshape(members, span, width)

    out_rows = out_project(after(attended_all, *upstream_pieces), out_columns)
    projected = exchange(out_rows, "expert").reshape(members, own_rows, out_piece)
    projected = jnp.transpose(projected, (1, 0, 2)).reshape(own_rows, model)

    upstream_pieces = after(upstream_pieces, out_rows)
    mask_plane = jnp.concatenate(
        [lax.dynamic_slice(p, (0, model + plane * members), (own_rows, members)) for p in upstream_pieces], axis=0)
    triangle = (jnp.arange(column)[:, None] >= jnp.arange(column)[None, :]).astype(BF16)
    rank = jnp.where(mask_plane > 0, mm(triangle, mask_plane) - 1.0, -1.0).astype(jnp.int32)
    pick = (rank.T[:, None, :] == jnp.arange(slots, dtype=jnp.int32)[None, :, None])
    pick = pick.reshape(members * slots, column).astype(BF16)
    unpick = rank[:, :, None] == jnp.arange(slots, dtype=jnp.int32)[None, None, :]
    unpick = unpick.reshape(column, members * slots).astype(BF16)
    upstream_sent = dispatch(pick, upstream_pieces)
    upstream_rows = exchange(upstream_sent, "expert")
    pick = after(pick, upstream_sent)
    router = jnp.concatenate([p[own_rows:, :model].reshape(experts, part_rows) for p in upstream_pieces], axis=1)
    router = jnp.pad(reorder(router, 1), ((0, padded - experts), (0, 0)))

    after_attn = residual_in + projected.astype(F32)
    scale_mixture = row_scale(after_attn)
    mixed_low = (after_attn * scale_mixture * mixture_gain).astype(BF16)
    arrived = []
    for columns in (slice(0, half), slice(half, model)):
        sent = dispatch(pick, plane_pieces(mixed_low[:, columns]))
        arrived.append(exchange(after(sent, upstream_rows), "expert"))

    out_heads = exchange(after(out_columns, arrived[1]), "expert")
    upstream_down = down_back(upstream_rows, down)
    own_expert = (plane * members + member).astype(jnp.int32).reshape(1)
    activated, gate_grad, up_grad, weight_wide, route_columns = expert_forward(
        experts, own_expert, arrived[0], arrived[1], upstream_rows, router, gate, up, upstream_down)
    back_first = exchange(row_gradient(gate_grad, up_grad, gate, up, 0), "expert")
    back_second = exchange(row_gradient(gate_grad, up_grad, gate, up, 1, route_columns), "expert")
    produced = produce(activated, weight_wide, down)
    back_first = after(back_first, out_heads, *produced)
    mixed_first = plane_sum(combine(unpick, back_first, planes, 40))
    mixed_second = plane_sum(combine(unpick, back_second, planes, 40))
    mixture_rows = exchange(after(produced[0], back_second), "expert")

    upstream = cotangent.astype(F32)
    mask = mask_own > 0
    logits = jnp.where(mask, mm_t(mixed_low, router[:experts]), VERY_NEGATIVE)
    raised = jnp.where(mask, jnp.exp(logits - jnp.max(logits, axis=-1, keepdims=True)), 0.0)
    weight_own = raised / jnp.sum(raised, axis=-1, keepdims=True)
    route_back = mixed_second[:, half:half + experts] + mixed_second[:, half + experts:half + 2 * experts]
    chosen_grad = weight_own * (route_back - jnp.sum(weight_own * route_back, axis=-1, keepdims=True))
    logit_grad = chosen_grad.astype(BF16)
    mixed_first = after(mixed_first, mixture_rows)
    mixed_grad = mm(logit_grad, router[:experts]) + jnp.concatenate([mixed_first, mixed_second[:, :half]], axis=1)
    mixture_back, mixture_terms = normalize_back(mixed_grad, after_attn, scale_mixture, mixture_gain)
    after_grad = upstream + mixture_back
    after_low = after_grad.astype(BF16)

    router_part = t_mm(logit_grad, mixed_low).astype(BF16).reshape(members, planes, model)
    router_part = jnp.pad(router_part, ((0, 0), (0, 8 - planes), (0, 0)))
    mixture_part = jnp.sum(mixture_terms, axis=0, keepdims=True)

    after_all = gather(after_low, "expert")
    mixture_parts = combine(unpick, after(mixture_rows, after_low), planes)
    mixture_first = plane_sum(mixture_parts)
    gate_gradient, up_gradient = hidden_gradient(
        arrived[0], arrived[1], *after((gate_grad, up_grad), after_low, *mixture_parts))
    after_all = after(after_all, gate_gradient, router_part, mixture_part, mixture_first)
    mixture_rows = exchange(after(produced[1], after_all), "expert")
    out_partial = out_gradient(member.astype(jnp.int32).reshape(1), attended_all, after_all, out_piece)
    out_share = lax.psum_scatter(
        after(out_partial, mixture_first).reshape(members * width, out_piece), "dp", scatter_dimension=0, tiled=True).astype(F32)
    attended_grad = out_back(after(after_all, out_partial), out_heads)
    dq, dk, dv, query_terms, key_terms = attend_back(
        prefix_len, query_low, key_low, value_low, attended_low, inverse, attended_grad, qraw, kraw, cosine, sine,
        query_gain, key_norm_gain)
    normed_partial = unproject(
        own_rows, dq, dk, dv, wq_pieces, kv_weight, normed, reorder(attention_gain, 0), router_part, mixture_part,
        query_terms, key_terms)
    mixture_parts = combine(unpick, after(mixture_rows, normed_partial), planes)
    arrived_sums = exchange(after(normed_partial, out_share, *mixture_parts), "expert")
    normed_sums = jnp.sum(arrived_sums.astype(F32), axis=0)
    input_back, _ = normalize_back(
        reorder(normed_sums[:own_rows], 1), residual_in, scale_attention, attention_gain)
    input_grad = after_grad + input_back
    mixture_second = plane_sum(mixture_parts)
    layer_out = (after_attn + jnp.concatenate([mixture_first, mixture_second], axis=1)).astype(BF16)

    query_partial = t_mm(normed, dq).astype(BF16)
    query_share = plane_sum(cut(after(query_partial, mixture_second)))
    down_grad = down_gradient(upstream_rows, model, weight_wide, after(activated, query_partial))
    kv_partial = jnp.concatenate([t_mm(normed, dk), t_mm(normed, dv)], axis=1)

    def kv_cols(j):
        start = j * piece
        return jnp.concatenate(
            [lax.dynamic_slice(kv_partial, (0, start), (model, piece)),
             lax.dynamic_slice(kv_partial, (0, HEAD_SIZE + start), (model, piece))], axis=1)

    kv_total = kv_cols(place)
    for shift in range(1, group):
        pairs = [(e, e - e % group + (e % group + shift) % group) for e in range(members)]
        kv_total += lax.ppermute(kv_cols((place + shift) % group).astype(BF16), "expert", pairs).astype(F32)
    kv_share = plane_sum(cut(kv_total.astype(BF16)))
    key_share = kv_share[:, :piece]
    value_share = kv_share[:, piece:]

    last = normed_sums[own_rows:]
    attention_sum, mixture_sum, head_sum = (last[8 + 2 * n] + last[9 + 2 * n] for n in range(3))
    gains = jnp.concatenate([reorder(attention_sum, 0), mixture_sum, head_sum[:2 * HEAD_SIZE]])
    total = jnp.concatenate([gains, last[:planes].reshape(-1)]).reshape(-1, HEAD_SIZE)
    step = 1
    while step < planes:
        total = total + lax.ppermute(total, "dp", [(i, i ^ step) for i in range(planes)])
        step *= 2
    total = total.reshape(-1)
    gains, router_total = total[:gains.shape[0]], total[gains.shape[0]:].reshape(planes, model)
    router_share = lax.dynamic_slice(router_total, (0, plane * part_rows), (planes, part_rows)).T
    attention_total, mixture_total = gains[:model], gains[model:2 * model]
    query_total, key_total = gains[2 * model:2 * model + HEAD_SIZE], gains[2 * model + HEAD_SIZE:]
    return (
        layer_out,
        input_grad,
        query_share,
        key_share,
        value_share,
        out_share,
        router_share,
        attention_total,
        mixture_total,
        query_total,
        key_total,
        gate_gradient,
        up_gradient,
        down_grad,
    )


def solution(mesh):
    rows = P(("dp", "expert"), None)
    grid = P("dp", "expert")
    experts = P(("dp", "expert"), None, None)
    in_specs = (rows, rows, P("dp"), grid, grid, grid, grid, grid, P(), P(), P(), P(), experts, experts, experts, rows)
    out_specs = (rows, rows, grid, grid, grid, grid, grid, P(), P(), P(), P(), experts, experts, experts)
    return jax.shard_map(shards, mesh=mesh, in_specs=in_specs, out_specs=out_specs, check_vma=False)
```

```python
import functools
import math

import jax
import jax.numpy as jnp
from jax import lax
from jax.experimental import pallas as pl
from jax.experimental.pallas import tpu as pltpu
from jax.sharding import PartitionSpec as P

QUERY_HEADS = 32
KEY_VALUE_HEADS = 4
HEAD_SIZE = 128
TOP = 8
EPS = 1e-06
ROTARY_BASE = 1000000.0
VERY_NEGATIVE = -1e30
SOFTMAX_SCALE = HEAD_SIZE ** (-0.5)
LOG2_SCALE = SOFTMAX_SCALE * math.log2(math.e)
VMEM_BYTES = 24 * 1024 * 1024
F32 = jnp.float32
BF16 = jnp.bfloat16


def cost(microseconds):
    return pl.CostEstimate(flops=int(microseconds * 1.1e9) + 1, bytes_accessed=1, transcendentals=0)


def mm(a, b):
    return lax.dot_general(a, b, (((1,), (0,)), ((), ())), preferred_element_type=F32)


def mm_t(a, b):
    return lax.dot_general(a, b, (((1,), (1,)), ((), ())), preferred_element_type=F32)


def t_mm(a, b):
    return lax.dot_general(a, b, (((0,), (0,)), ((), ())), preferred_element_type=F32)


def row_scale(source):
    return lax.rsqrt(jnp.mean(source * source, axis=-1, keepdims=True) + EPS)


def normalize_back(upstream, source, scaling, gain_row):
    unit_rows = source * scaling
    weighted = upstream * gain_row
    inner_mean = jnp.mean(weighted * unit_rows, axis=-1, keepdims=True)
    return (scaling * (weighted - unit_rows * inner_mean), upstream * unit_rows)


def rotary_tables(span):
    half = HEAD_SIZE // 2
    frequency = jnp.power(ROTARY_BASE, -jnp.arange(half, dtype=F32) * 2.0 / HEAD_SIZE)
    angles = jnp.arange(span, dtype=jnp.int32).astype(F32)[:, None] * frequency[None, :]
    cosine, sine = jnp.cos(angles), jnp.sin(angles)
    return (
        jnp.concatenate([cosine, cosine], axis=-1),
        jnp.concatenate([-sine, sine], axis=-1),
    )


def turned(u, gain, cosine, sine):
    n = u * row_scale(u) * gain
    return (n * cosine + pltpu.roll(n, HEAD_SIZE // 2, 1) * sine).astype(BF16)


def pieces_product(x, refs):
    size = refs[0].shape[0]
    total = mm(x[:, :size], refs[0][...])
    for s in range(1, len(refs)):
        total += mm(x[:, s * size:(s + 1) * size], refs[s][...])
    return total


def project_query_kernel(x_ref, cos_ref, sin_ref, gain_ref, *refs):
    raw_ref, low_ref = refs[-2:]
    q = pieces_product(x_ref[...], refs[:-2])
    raw_ref[...] = q
    for h in range(q.shape[1] // HEAD_SIZE):
        cols = slice(h * HEAD_SIZE, (h + 1) * HEAD_SIZE)
        low_ref[:, cols] = turned(q[:, cols], gain_ref[...], cos_ref[...], sin_ref[...])


def project_key_kernel(x_ref, cos_ref, sin_ref, gain_ref, w_ref, raw_ref, k_ref, v_ref):
    kv = mm(x_ref[...], w_ref[...])
    raw_ref[...] = kv[:, :HEAD_SIZE]
    v_ref[...] = kv[:, HEAD_SIZE:].astype(BF16)
    k_ref[...] = turned(kv[:, :HEAD_SIZE], gain_ref[...], cos_ref[...], sin_ref[...])


def project(kernel, x, weights, cosine, sine, gain, out):
    span, model = x.shape
    tile = 512
    row = lambda w: pl.BlockSpec((tile, w), lambda i: (i, 0))
    whole = lambda a, b: pl.BlockSpec((a, b), lambda i: (0, 0))
    return pl.pallas_call(
        kernel,
        grid=(span // tile,),
        in_specs=[row(model), row(HEAD_SIZE), row(HEAD_SIZE), whole(1, HEAD_SIZE)] + [whole(*w.shape) for w in weights],
        out_specs=[row(w) for w, _ in out],
        out_shape=[jax.ShapeDtypeStruct((span, w), t) for w, t in out],
        compiler_params=pltpu.CompilerParams(vmem_limit_bytes=VMEM_BYTES),
        cost_estimate=cost(0),
        name=kernel.__name__,
    )(x, cosine, sine, gain[None], *weights)


def block_limits(span, tile):
    return [(r0, max(r0 + tile, span // 2)) for r0 in range(0, span, tile)]


def masked(values, r0, limit, prefix):
    tile = values.shape[0]
    rows = r0 + lax.broadcasted_iota(jnp.int32, (tile, limit - r0), 0)
    cols = r0 + lax.broadcasted_iota(jnp.int32, (tile, limit - r0), 1)
    right = jnp.where((cols <= rows) | (cols < prefix), values[:, r0:], 0.0)
    return right if r0 == 0 else jnp.concatenate([values[:, :r0], right], axis=1)


def attend_kernel(tile, prefix_ref, q_ref, k_ref, v_ref, o_ref, l_ref, wide_ref):
    span = q_ref.shape[0]

    @pl.when(pl.program_id(0) == 0)
    def _():
        wide_ref[:, :HEAD_SIZE] = v_ref[...]
        wide_ref[:, HEAD_SIZE:] = jnp.ones((span, HEAD_SIZE), BF16)

    prefix = prefix_ref[0]
    for r0, limit in block_limits(span, tile):
        rows = slice(r0, r0 + tile)
        scores = mm_t(q_ref[rows, :], k_ref[:limit, :])
        weights = masked(jnp.exp2(scores * LOG2_SCALE), r0, limit, prefix)
        sums = mm(weights.astype(BF16), wide_ref[:limit, :])
        inverse = 1.0 / sums[:, HEAD_SIZE:]
        o_ref[rows, :] = (sums[:, :HEAD_SIZE] * inverse).astype(BF16)
        l_ref[rows, :] = inverse


def attend(prefix, q, k, v):
    span, width = q.shape
    heads = width // HEAD_SIZE
    head = pl.BlockSpec((span, HEAD_SIZE), lambda h: (0, h))
    shared = pl.BlockSpec((span, HEAD_SIZE), lambda h: (0, 0))
    return pl.pallas_call(
        functools.partial(attend_kernel, 256),
        grid=(heads,),
        in_specs=[pl.BlockSpec(memory_space=pltpu.SMEM), head, shared, shared],
        out_specs=[head, head],
        out_shape=[jax.ShapeDtypeStruct((span, width), BF16), jax.ShapeDtypeStruct((span, width), F32)],
        scratch_shapes=[pltpu.VMEM((span, 2 * HEAD_SIZE), BF16)],
        compiler_params=pltpu.CompilerParams(vmem_limit_bytes=VMEM_BYTES),
        cost_estimate=cost(0),
        name="attend",
    )(prefix, q, k, v)


def attend_back_kernel(tile, prefix_ref, q_ref, k_ref, v_ref, o_ref, l_ref, do_ref, qraw_ref, kraw_ref, cos_ref, sin_ref,
                       qg_ref, kg_ref, dq_ref, dk_ref, dv_ref, qgg_ref, kgg_ref, dk_sum, dv_sum):
    span = q_ref.shape[0]
    step = pl.program_id(0)

    @pl.when(step == 0)
    def _():
        dk_sum[...] = jnp.zeros_like(dk_sum)
        dv_sum[...] = jnp.zeros_like(dv_sum)
        qgg_ref[...] = jnp.zeros_like(qgg_ref)

    def unturned(grad, rows):
        return grad * cos_ref[rows, :] - pltpu.roll(grad, HEAD_SIZE // 2, 1) * sin_ref[rows, :]

    prefix = prefix_ref[0]
    for r0, limit in block_limits(span, tile):
        rows = slice(r0, r0 + tile)
        q, do = q_ref[rows, :], do_ref[rows, :]
        keys, values = k_ref[:limit, :], v_ref[:limit, :]
        weights = masked(jnp.exp2(mm_t(q, keys) * LOG2_SCALE), r0, limit, prefix)
        probs = weights * jnp.concatenate([l_ref[rows, :]] * (limit // HEAD_SIZE), axis=1)
        delta = jnp.sum(do.astype(F32) * o_ref[rows, :].astype(F32), axis=1, keepdims=True)
        score_grad = (probs * (mm_t(do, values) - delta)).astype(BF16)
        dv_sum[:limit, :] += t_mm(probs.astype(BF16), do)
        dk_sum[:limit, :] += t_mm(score_grad, q)
        turn = unturned(mm(score_grad, keys) * SOFTMAX_SCALE, rows)
        raw = qraw_ref[rows, :]
        back, terms = normalize_back(turn, raw, row_scale(raw), qg_ref[...])
        dq_ref[rows, :] = back.astype(BF16)
        qgg_ref[...] += jnp.sum(terms, axis=0, keepdims=True)

    @pl.when(step == pl.num_programs(0) - 1)
    def _():
        raw = kraw_ref[...]
        turn = unturned(dk_sum[...] * SOFTMAX_SCALE, slice(None))
        back, terms = normalize_back(turn, raw, row_scale(raw), kg_ref[...])
        dk_ref[...] = back.astype(BF16)
        dv_ref[...] = dv_sum[...].astype(BF16)
        kgg_ref[...] = jnp.sum(terms, axis=0, keepdims=True)


def attend_back(prefix, q, k, v, o, inverse, do, qraw, kraw, cosine, sine, q_gain, k_gain):
    span, width = q.shape
    heads = width // HEAD_SIZE
    head = pl.BlockSpec((span, HEAD_SIZE), lambda h: (0, h))
    shared = pl.BlockSpec((span, HEAD_SIZE), lambda h: (0, 0))
    gain = pl.BlockSpec((1, HEAD_SIZE), lambda h: (0, 0))
    return pl.pallas_call(
        functools.partial(attend_back_kernel, 256),
        grid=(heads,),
        in_specs=[pl.BlockSpec(memory_space=pltpu.SMEM), head, shared, shared, head, head, head, head, shared, shared,
                  shared, gain, gain],
        out_specs=[head, shared, shared, gain, gain],
        out_shape=[
            jax.ShapeDtypeStruct((span, width), BF16),
            jax.ShapeDtypeStruct((span, HEAD_SIZE), BF16),
            jax.ShapeDtypeStruct((span, HEAD_SIZE), BF16),
            jax.ShapeDtypeStruct((1, HEAD_SIZE), F32),
            jax.ShapeDtypeStruct((1, HEAD_SIZE), F32),
        ],
        scratch_shapes=[pltpu.VMEM((span, HEAD_SIZE), F32), pltpu.VMEM((span, HEAD_SIZE), F32)],
        compiler_params=pltpu.CompilerParams(vmem_limit_bytes=VMEM_BYTES),
        cost_estimate=cost(0),
        name="attend_back",
    )(prefix, q, k, v, o, inverse, do, qraw, kraw, cosine, sine, q_gain[None], k_gain[None])


def unproject_kernel(own_rows, dq_ref, dk_ref, dv_ref, wkv_ref, x_ref, gain_ref, router_ref, mix_ref, qg_ref, kg_ref,
                     *refs):
    weights, out_ref, sum_ref = refs[:-2], refs[-2], refs[-1]
    span, model = x_ref.shape
    size = weights[0].shape[0]
    tile = 512
    each = tile // own_rows
    for r in range(span // tile):
        rows = slice(r * tile, (r + 1) * tile)
        dq, dk, dv = dq_ref[rows, :], dk_ref[rows, :], dv_ref[rows, :]
        for s, weight in enumerate(weights):
            cols = slice(s * size, (s + 1) * size)
            total = mm_t(dq, weight[...])
            total += mm_t(dk, wkv_ref[cols, :HEAD_SIZE]) + mm_t(dv, wkv_ref[cols, HEAD_SIZE:])
            low = total.astype(BF16)
            for m in range(each):
                out_ref[r * each + m, :own_rows, cols] = low[m * own_rows:(m + 1) * own_rows]
            part = jnp.sum(total * x_ref[rows, cols].astype(F32), axis=0, keepdims=True)
            if r == 0:
                sum_ref[:, cols] = part
            else:
                sum_ref[:, cols] += part
    heads = jnp.concatenate([qg_ref[...], kg_ref[...], jnp.zeros((1, model - 2 * HEAD_SIZE), F32)], axis=1)
    place = lax.broadcasted_iota(jnp.int32, (8, model), 0)
    sums = jnp.zeros((8, model), F32)
    for n, values in enumerate((sum_ref[...] / gain_ref[...], mix_ref[...], heads)):
        high = values.astype(BF16).astype(F32)
        sums = jnp.where(place == 2 * n, high, jnp.where(place == 2 * n + 1, values - high, sums))
    sums = sums.astype(BF16)
    for m in range(out_ref.shape[0]):
        out_ref[m, own_rows:own_rows + 8, :] = router_ref[m]
        out_ref[m, own_rows + 8:, :] = sums


def unproject(own_rows, dq, dk, dv, pieces, wkv, x, gain, router_part, mixture_part, query_part, key_part):
    span, model = x.shape
    return pl.pallas_call(
        functools.partial(unproject_kernel, own_rows),
        out_shape=jax.ShapeDtypeStruct((span // own_rows, own_rows + 16, model), BF16),
        scratch_shapes=[pltpu.VMEM((1, model), F32)],
        compiler_params=pltpu.CompilerParams(vmem_limit_bytes=44 * 1024 * 1024),
        cost_estimate=cost(0),
        name="unproject",
    )(dq, dk, dv, wkv, x, gain[None], router_part, mixture_part, query_part, key_part, *pieces)


def out_project_kernel(plane_ref, a_ref, *refs):
    out_ref = refs[-1]
    pieces = refs[:-1]
    members, _, width = a_ref.shape
    planes, each = len(pieces), members // len(pieces)
    total = None
    for s, piece in enumerate(pieces):
        block = lax.rem(plane_ref[0] + planes - s, planes) * each
        for i in range(each):
            part = mm(a_ref[block + i], piece[i * width:(i + 1) * width, :])
            total = part if total is None else total + part
    out_ref[...] = total.astype(BF16)


def out_project(plane, attended_all, pieces):
    members, span, width = attended_all.shape
    size, columns = pieces[0].shape
    tile = 256
    return pl.pallas_call(
        out_project_kernel,
        grid=(span // tile,),
        in_specs=[pl.BlockSpec(memory_space=pltpu.SMEM), pl.BlockSpec((members, tile, width), lambda i: (0, i, 0))]
        + [pl.BlockSpec((size, columns), lambda i: (0, 0))] * len(pieces),
        out_specs=pl.BlockSpec((tile, columns), lambda i: (i, 0)),
        out_shape=jax.ShapeDtypeStruct((span, columns), BF16),
        compiler_params=pltpu.CompilerParams(vmem_limit_bytes=VMEM_BYTES),
        cost_estimate=cost(0),
        name="out_project",
    )(plane, attended_all, *pieces)


def out_back_kernel(g_ref, w_ref, out_ref):
    columns = w_ref.shape[2]
    total = mm_t(g_ref[:, :columns], w_ref[0])
    for m in range(1, w_ref.shape[0]):
        total += mm_t(g_ref[:, m * columns:(m + 1) * columns], w_ref[m])
    out_ref[...] = total.astype(BF16)


def out_back(after_all, heads):
    span, model = after_all.shape
    members, width, columns = heads.shape
    tile = 512
    return pl.pallas_call(
        out_back_kernel,
        grid=(span // tile,),
        in_specs=[pl.BlockSpec((tile, model), lambda i: (i, 0)),
                  pl.BlockSpec((members, width, columns), lambda i: (0, 0, 0))],
        out_specs=pl.BlockSpec((tile, width), lambda i: (i, 0)),
        out_shape=jax.ShapeDtypeStruct((span, width), BF16),
        compiler_params=pltpu.CompilerParams(vmem_limit_bytes=VMEM_BYTES),
        cost_estimate=cost(0),
        name="out_back",
    )(after_all, heads)


def out_gradient_kernel(member_ref, a_ref, g_ref, out_ref):
    out_ref[0] = t_mm(a_ref[0], g_ref[...]).astype(BF16)


def out_gradient(member, attended_all, after_all, columns):
    members, span, width = attended_all.shape
    return pl.pallas_call(
        out_gradient_kernel,
        grid_spec=pltpu.PrefetchScalarGridSpec(
            num_scalar_prefetch=1,
            grid=(members,),
            in_specs=[pl.BlockSpec((1, span, width), lambda m, me: (m, 0, 0)),
                      pl.BlockSpec((span, columns), lambda m, me: (0, me[0]))],
            out_specs=pl.BlockSpec((1, width, columns), lambda m, me: (m, 0, 0)),
        ),
        out_shape=jax.ShapeDtypeStruct((members, width, columns), BF16),
        compiler_params=pltpu.CompilerParams(vmem_limit_bytes=VMEM_BYTES),
        cost_estimate=cost(0),
        name="out_gradient",
    )(member, attended_all, after_all)


def expert_kernel(experts, own_ref, xa_ref, xb_ref, mask_ref, router_ref, gate_ref, up_ref, down_ref,
                  act_ref, gg_ref, ug_ref, w_ref, route_ref, sum_ref):
    half = xa_ref.shape[1]
    step = pl.program_id(0)
    own = own_ref[0]

    def product(left, right, weight):
        return mm(left[...], weight[:half, :]) + mm(right[...], weight[half:, :])

    @pl.when(step == 0)
    def _():
        mask = mask_ref[...].astype(F32)
        logits = mm_t(xa_ref[...], router_ref[:, :half]) + mm_t(xb_ref[...], router_ref[:, half:])
        logits = jnp.where(mask > 0, logits, VERY_NEGATIVE)
        raised = jnp.where(mask > 0, jnp.exp(logits - jnp.max(logits, axis=-1, keepdims=True)), 0.0)
        total = jnp.maximum(jnp.sum(raised, axis=-1, keepdims=True), 1e-30)
        lanes = lax.broadcasted_iota(jnp.int32, raised.shape, 1)
        weight = jnp.sum(jnp.where(lanes == own, raised, 0.0), axis=-1, keepdims=True) / total
        w_ref[...] = jnp.broadcast_to(weight, w_ref.shape)

    gate_raw, up_raw = product(xa_ref, xb_ref, gate_ref), product(xa_ref, xb_ref, up_ref)
    down = down_ref[...]
    weight = w_ref[:, :1]
    sig = 1.0 / (1.0 + jnp.exp(-gate_raw))
    silu = gate_raw * sig
    activated = (silu * up_raw).astype(BF16)
    act_ref[...] = activated
    route = jnp.sum(activated.astype(F32) * down, axis=-1, keepdims=True)
    grad = weight * down
    gg_ref[...] = (grad * up_raw * sig * (1.0 + gate_raw * (1.0 - sig))).astype(BF16)
    ug_ref[...] = (grad * silu).astype(BF16)
    route = jnp.broadcast_to(route, sum_ref.shape)

    @pl.when(step == 0)
    def _():
        sum_ref[...] = route

    @pl.when(step > 0)
    def _():
        sum_ref[...] += route

    @pl.when(step == pl.num_programs(0) - 1)
    def _():
        total = sum_ref[:, :1]
        high = total.astype(BF16).astype(F32)
        lanes = lax.broadcasted_iota(jnp.int32, route_ref.shape, 1)
        route_ref[...] = jnp.where(
            lanes == own, high, jnp.where(lanes == experts + own, total - high, 0.0)).astype(BF16)


def expert_forward(experts, own, xa, xb, masked_rows, router, gate, up, upstream_down):
    rows, half = xa.shape
    model, hidden = gate.shape
    padded = router.shape[0]
    route_width = -(-2 * experts // HEAD_SIZE) * HEAD_SIZE
    tile = 256
    whole = lambda a, b: pl.BlockSpec((a, b), lambda i: (0, 0))
    column = lambda a: pl.BlockSpec((a, tile), lambda i: (0, i))
    return pl.pallas_call(
        functools.partial(expert_kernel, experts),
        grid=(hidden // tile,),
        in_specs=[pl.BlockSpec(memory_space=pltpu.SMEM), whole(rows, half), whole(rows, half),
                  pl.BlockSpec((rows, padded), lambda i: (0, half // padded)), whole(padded, model), column(model),
                  column(model), column(rows)],
        out_specs=[column(rows), column(rows), column(rows), whole(rows, HEAD_SIZE), whole(rows, route_width)],
        out_shape=[
            jax.ShapeDtypeStruct((rows, hidden), BF16),
            jax.ShapeDtypeStruct((rows, hidden), BF16),
            jax.ShapeDtypeStruct((rows, hidden), BF16),
            jax.ShapeDtypeStruct((rows, HEAD_SIZE), F32),
            jax.ShapeDtypeStruct((rows, route_width), BF16),
        ],
        scratch_shapes=[pltpu.VMEM((rows, HEAD_SIZE), F32)],
        compiler_params=pltpu.CompilerParams(vmem_limit_bytes=40 * 1024 * 1024),
        cost_estimate=cost(18),
        name="expert_forward",
    )(own, xa, xb, masked_rows, router, gate, up, upstream_down)


def row_gradient_kernel(gg_ref, ug_ref, gate_ref, up_ref, *rest):
    total = (mm_t(gg_ref[...], gate_ref[...]) + mm_t(ug_ref[...], up_ref[...])).astype(BF16)
    out_ref = rest[-1]
    out_ref[:, :total.shape[1]] = total
    if len(rest) == 2:
        out_ref[:, total.shape[1]:] = rest[0][...]


def row_gradient(gg, ug, gate, up, part, route=None):
    rows, hidden = gg.shape
    half = gate.shape[0] // 2
    tile = rows // 4
    row = lambda w: pl.BlockSpec((tile, w), lambda i: (i, 0))
    weight = pl.BlockSpec((half, hidden), lambda i: (part, 0))
    extra = [] if route is None else [route]
    width = half + sum(e.shape[1] for e in extra)
    return pl.pallas_call(
        row_gradient_kernel,
        grid=(rows // tile,),
        in_specs=[row(hidden), row(hidden), weight, weight] + [row(e.shape[1]) for e in extra],
        out_specs=row(width),
        out_shape=jax.ShapeDtypeStruct((rows, width), BF16),
        compiler_params=pltpu.CompilerParams(vmem_limit_bytes=VMEM_BYTES),
        cost_estimate=cost(8),
        name="row_gradient",
    )(gg, ug, gate, up, *extra)


def down_back_kernel(ca_ref, cb_ref, down_ref, out_ref):
    half = cb_ref.shape[1]
    out_ref[...] = mm_t(ca_ref[...], down_ref[:, :half]) + mm_t(cb_ref[...], down_ref[:, half:])


def down_back(ca, cb, down):
    rows, half = cb.shape
    hidden, model = down.shape
    tile = 256
    whole = pl.BlockSpec((rows, half), lambda i: (0, 0))
    return pl.pallas_call(
        down_back_kernel,
        grid=(hidden // tile,),
        in_specs=[whole, whole, pl.BlockSpec((tile, model), lambda i: (i, 0))],
        out_specs=pl.BlockSpec((rows, tile), lambda i: (0, i)),
        out_shape=jax.ShapeDtypeStruct((rows, hidden), F32),
        compiler_params=pltpu.CompilerParams(vmem_limit_bytes=VMEM_BYTES),
        cost_estimate=cost(0),
        name="down_back",
    )(ca, cb, down)


def produce_kernel(act_ref, w_ref, down_ref, *outs):
    total = (w_ref[:, :1] * mm(act_ref[...], down_ref[...])).astype(BF16)
    half = total.shape[1] // 2
    outs[0][...] = total[:, :half]
    outs[1][...] = total[:, half:]


def produce(activated, weight, down):
    rows, hidden = activated.shape
    model = down.shape[1]
    tile = rows // 4
    row = lambda w: pl.BlockSpec((tile, w), lambda i: (i, 0))
    return pl.pallas_call(
        produce_kernel,
        grid=(rows // tile,),
        in_specs=[row(hidden), row(HEAD_SIZE), pl.BlockSpec((hidden, model), lambda i: (0, 0))],
        out_specs=[row(model // 2)] * 2,
        out_shape=[jax.ShapeDtypeStruct((rows, model // 2), BF16)] * 2,
        compiler_params=pltpu.CompilerParams(vmem_limit_bytes=VMEM_BYTES),
        cost_estimate=cost(0),
        name="produce",
    )(activated, weight, down)


def hidden_gradient_kernel(xa_ref, xb_ref, gg_ref, ug_ref, dg_ref, du_ref):
    in_first = pl.program_id(0) < pl.num_programs(0) // 2
    for x_ref, now in ((xa_ref, in_first), (xb_ref, jnp.logical_not(in_first))):
        @pl.when(now)
        def _():
            dg_ref[0] = t_mm(x_ref[...], gg_ref[...])
            du_ref[0] = t_mm(x_ref[...], ug_ref[...])


def hidden_gradient(xa, xb, gg, ug):
    rows, half = xa.shape
    hidden = gg.shape[1]
    tile = 256
    count = half // tile
    whole = pl.BlockSpec((rows, hidden), lambda i: (0, 0))
    out = pl.BlockSpec((1, tile, hidden), lambda i: (0, i, 0))
    return pl.pallas_call(
        hidden_gradient_kernel,
        grid=(2 * count,),
        in_specs=[pl.BlockSpec((rows, tile), lambda i: (0, jnp.minimum(i, count - 1))),
                  pl.BlockSpec((rows, tile), lambda i: (0, jnp.maximum(i - count, 0))), whole, whole],
        out_specs=[out, out],
        out_shape=[jax.ShapeDtypeStruct((1, 2 * half, hidden), F32)] * 2,
        compiler_params=pltpu.CompilerParams(vmem_limit_bytes=VMEM_BYTES),
        cost_estimate=cost(0),
        name="hidden_gradient",
    )(xa, xb, gg, ug)


def down_gradient_kernel(ca_ref, cb_ref, w_ref, act_ref, out_ref):
    in_first = pl.program_id(0) < pl.num_programs(0) // 2
    for c_ref, now in ((ca_ref, in_first), (cb_ref, jnp.logical_not(in_first))):
        @pl.when(now)
        def _():
            out_ref[0] = t_mm(act_ref[...], (w_ref[:, :1] * c_ref[...].astype(F32)).astype(BF16))


def down_gradient(ca, cb, weight, activated):
    rows, half = cb.shape
    hidden = activated.shape[1]
    tile = 256
    count = half // tile
    return pl.pallas_call(
        down_gradient_kernel,
        grid=(2 * count,),
        in_specs=[pl.BlockSpec((rows, tile), lambda i: (0, jnp.minimum(i, count - 1))),
                  pl.BlockSpec((rows, tile), lambda i: (0, jnp.maximum(i - count, 0))),
                  pl.BlockSpec((rows, HEAD_SIZE), lambda i: (0, 0)), pl.BlockSpec((rows, hidden), lambda i: (0, 0))],
        out_specs=pl.BlockSpec((1, hidden, tile), lambda i: (0, 0, i)),
        out_shape=jax.ShapeDtypeStruct((1, hidden, 2 * half), F32),
        compiler_params=pltpu.CompilerParams(vmem_limit_bytes=VMEM_BYTES),
        cost_estimate=cost(0),
        name="down_gradient",
    )(ca, cb, weight, activated)


def dispatch_kernel(pick_ref, *refs):
    out_ref, all_ref = refs[-2:]
    size = all_ref.shape[0] // (len(refs) - 2)

    @pl.when(pl.program_id(0) == 0)
    def _():
        for s, ref in enumerate(refs[:-2]):
            all_ref[s * size:(s + 1) * size, :] = ref[...]

    out_ref[...] = mm(pick_ref[...], all_ref[...]).astype(BF16)


def dispatch(pick, pieces):
    rows, column = pick.shape
    size, width = column // len(pieces), pieces[0].shape[1]
    tile = rows // 4
    return pl.pallas_call(
        dispatch_kernel,
        grid=(rows // tile,),
        in_specs=[pl.BlockSpec((tile, column), lambda i: (i, 0))]
        + [pl.BlockSpec((size, width), lambda i: (0, 0))] * len(pieces),
        out_specs=pl.BlockSpec((tile, width), lambda i: (i, 0)),
        out_shape=jax.ShapeDtypeStruct((rows, width), BF16),
        scratch_shapes=[pltpu.VMEM((column, width), BF16)],
        compiler_params=pltpu.CompilerParams(vmem_limit_bytes=VMEM_BYTES),
        cost_estimate=cost(0),
        name="dispatch",
    )(pick, *pieces)


def combine_kernel(pick_ref, rows_ref, *outs):
    total = mm(pick_ref[...], rows_ref[...]).astype(BF16)
    size = total.shape[0] // len(outs)
    for s, out in enumerate(outs):
        out[...] = total[s * size:(s + 1) * size]


def combine(pick, rows, count, microseconds=0):
    column, slots = pick.shape
    width = rows.shape[1]
    tile = max(t for t in range(HEAD_SIZE, 513, HEAD_SIZE) if width % t == 0)
    size = column // count
    out = pl.BlockSpec((size, tile), lambda i: (0, i))
    return pl.pallas_call(
        combine_kernel,
        grid=(width // tile,),
        in_specs=[pl.BlockSpec((column, slots), lambda i: (0, 0)), pl.BlockSpec((slots, tile), lambda i: (0, i))],
        out_specs=[out] * count,
        out_shape=[jax.ShapeDtypeStruct((size, width), BF16)] * count,
        compiler_params=pltpu.CompilerParams(vmem_limit_bytes=VMEM_BYTES),
        cost_estimate=cost(microseconds),
        name="combine",
    )(pick, rows)


def after(array, *earlier):
    return lax.optimization_barrier((array, *earlier))[0]


def shards(
    tokens,
    routes,
    prefix_len,
    query_weight,
    key_matrix,
    value_matrix,
    out_weight,
    router_weight,
    attention_gain,
    mixture_gain,
    query_gain,
    key_norm_gain,
    expert_gate,
    expert_up,
    expert_down,
    cotangent,
):
    planes, members = lax.axis_size("dp"), lax.axis_size("expert")
    devices = planes * members
    plane, member = lax.axis_index("dp"), lax.axis_index("expert")
    own_rows, model = tokens.shape
    span = own_rows * members
    column = own_rows * planes
    experts = devices
    width = query_weight.shape[1]
    piece = key_matrix.shape[1]
    group = HEAD_SIZE // piece
    block_slots = max(2, 6 * own_rows * TOP // (5 * experts))
    slots = planes * block_slots
    padded = -(-experts // HEAD_SIZE) * HEAD_SIZE
    half = model // 2
    part_rows = model // planes
    gate, up, down = expert_gate[0], expert_up[0], expert_down[0]

    def gather(array, axis, dimension=0):
        return lax.all_gather(array, axis, axis=dimension, tiled=True)

    def exchange(array, axis):
        return lax.all_to_all(array, axis, split_axis=0, concat_axis=0, tiled=True)

    def plane_pieces(array):
        def shift(value, by):
            return lax.ppermute(value, "dp", [(i, (i + by) % planes) for i in range(planes)])

        pieces = [array] + [None] * (planes - 1)
        for s in range(1, planes // 2 + 1):
            pieces[s] = shift(pieces[s - 1], 1)
            if planes - s > s:
                pieces[planes - s] = shift(pieces[(planes - s + 1) % planes], -1)
        return pieces

    def plane_sum(pieces):
        def shift(value, by):
            return lax.ppermute(value, "dp", [(i, (i + by) % planes) for i in range(planes)]).astype(F32)

        total = pieces[0].astype(F32)
        middle = planes // 2
        for order, by in ((range(middle, 0, -1), -1), (range(middle + 1, planes), 1)):
            running = None
            for s in order:
                running = pieces[s] if running is None else (shift(running, by) + pieces[s].astype(F32)).astype(BF16)
            if running is not None:
                total += shift(running, by)
        return total

    def reorder(array, dimension):
        size = array.shape[dimension] // planes
        return jnp.concatenate(
            [lax.dynamic_slice_in_dim(array, (plane - s) % planes * size, size, dimension) for s in range(planes)],
            axis=dimension)

    def cut(array):
        return [array[s * (array.shape[0] // planes):(s + 1) * (array.shape[0] // planes)] for s in range(planes)]

    residual_in = tokens.astype(F32)
    scale_attention = row_scale(residual_in)
    normed_own = (residual_in * scale_attention * attention_gain).astype(BF16)
    normed = gather(reorder(normed_own, 1), "expert")

    expert_ids = jnp.arange(experts, dtype=jnp.int32)
    mask_own = jnp.sum((routes[:, :, None] == expert_ids[None, None, :]).astype(F32), axis=1)
    mask_wide = jnp.pad(mask_own, ((0, 0), (0, padded - experts))).astype(BF16)
    upstream_pieces = plane_pieces(jnp.concatenate([cotangent[:, :half], mask_wide], axis=1))
    first_hop = (upstream_pieces[1], upstream_pieces[-1])
    kv_pieces = plane_pieces(after(jnp.concatenate([key_matrix, value_matrix], axis=1), *first_hop))
    wq_pieces = plane_pieces(after(query_weight, *first_hop))
    out_piece = out_weight.shape[1]
    out_pieces = plane_pieces(after(out_weight, *wq_pieces[1:]))
    cosine, sine = rotary_tables(span)

    mask_plane = jnp.concatenate(
        [lax.dynamic_slice(p, (0, half + plane * members), (own_rows, members)) for p in upstream_pieces], axis=0)
    triangle = (jnp.arange(column)[:, None] >= jnp.arange(column)[None, :]).astype(BF16)
    rank = jnp.where(mask_plane > 0, mm(triangle, mask_plane) - 1.0, -1.0).astype(jnp.int32)
    pick = (rank.T[:, None, :] == jnp.arange(slots, dtype=jnp.int32)[None, :, None])
    pick = pick.reshape(members * slots, column).astype(BF16)
    unpick = rank[:, :, None] == jnp.arange(slots, dtype=jnp.int32)[None, None, :]
    unpick = unpick.reshape(column, members * slots).astype(BF16)
    upstream_sent = dispatch(pick, upstream_pieces)
    upstream_a = exchange(upstream_sent, "expert")

    kv_own = jnp.concatenate(kv_pieces, axis=0)
    place = member % group
    kv_parts = [kv_own]
    for shift in range(1, group):
        pairs = [(e - e % group + (e % group + shift) % group, e) for e in range(members)]
        kv_parts.append(lax.ppermute(kv_own, "expert", pairs))

    def kv_piece(j):
        value = kv_parts[0]
        for shift in range(1, group):
            value = jnp.where((place + shift) % group == j, kv_parts[shift], value)
        return value

    ordered = [kv_piece(j) for j in range(group)]
    kv_weight = jnp.concatenate([p[:, :piece] for p in ordered] + [p[:, piece:] for p in ordered], axis=1)

    kraw, key_low, value_low = project(
        project_key_kernel, after(normed, cosine, sine, upstream_sent), [kv_weight], cosine, sine, key_norm_gain,
        [(HEAD_SIZE, F32), (HEAD_SIZE, BF16), (HEAD_SIZE, BF16)])
    qraw, query_low = project(
        project_query_kernel, normed, wq_pieces, cosine, sine, query_gain, [(width, F32), (width, BF16)])
    attended_low, inverse = attend(prefix_len, after(query_low, upstream_a), key_low, value_low)
    attended_all = gather(attended_low, "expert").reshape(members, span, width)

    router_rows = gather(after(router_weight.T, attended_low), "expert").reshape(2 * members, half)
    upstream_pieces = plane_pieces(after(jnp.concatenate([cotangent[:, half:], router_rows], axis=0), *out_pieces[1:]))

    out_rows = out_project(plane.astype(jnp.int32).reshape(1), attended_all, out_pieces)
    projected = exchange(out_rows, "expert").reshape(members, own_rows, out_piece)
    projected = jnp.transpose(projected, (1, 0, 2)).reshape(own_rows, model)

    upstream_sent = dispatch(after(pick, out_rows), upstream_pieces)
    upstream_b = exchange(upstream_sent, "expert")
    pick = after(pick, upstream_sent)
    router = jnp.concatenate([p[own_rows:].reshape(experts, part_rows) for p in upstream_pieces], axis=1)
    router = jnp.pad(reorder(router, 1), ((0, padded - experts), (0, 0)))

    after_attn = residual_in + projected.astype(F32)
    scale_mixture = row_scale(after_attn)
    mixed_low = (after_attn * scale_mixture * mixture_gain).astype(BF16)
    arrived = []
    for columns in (slice(0, half), slice(half, model)):
        sent = dispatch(pick, plane_pieces(mixed_low[:, columns]))
        arrived.append(exchange(after(sent, upstream_b), "expert"))

    out_columns = reorder(jnp.concatenate(after(out_pieces, arrived[0]), axis=0), 0)
    out_heads = exchange(after(out_columns, arrived[1]).reshape(members, width, out_piece), "expert")
    upstream_down = down_back(upstream_a, upstream_b, down)
    own_expert = (plane * members + member).astype(jnp.int32).reshape(1)
    activated, gate_grad, up_grad, weight_wide, route_columns = expert_forward(
        experts, own_expert, arrived[0], arrived[1], upstream_a, router, gate, up, upstream_down)
    back_first = exchange(row_gradient(gate_grad, up_grad, gate, up, 0), "expert")
    back_second = exchange(row_gradient(gate_grad, up_grad, gate, up, 1, route_columns), "expert")
    produced = produce(activated, weight_wide, down)
    back_first = after(back_first, out_heads, *produced)
    mixed_first = plane_sum(combine(unpick, back_first, planes, 40))
    mixed_second = plane_sum(combine(unpick, back_second, planes, 40))
    mixture_rows = exchange(after(produced[0], back_second), "expert")

    upstream = cotangent.astype(F32)
    mask = mask_own > 0
    logits = jnp.where(mask, mm_t(mixed_low, router[:experts]), VERY_NEGATIVE)
    raised = jnp.where(mask, jnp.exp(logits - jnp.max(logits, axis=-1, keepdims=True)), 0.0)
    weight_own = raised / jnp.sum(raised, axis=-1, keepdims=True)
    route_back = mixed_second[:, half:half + experts] + mixed_second[:, half + experts:half + 2 * experts]
    chosen_grad = weight_own * (route_back - jnp.sum(weight_own * route_back, axis=-1, keepdims=True))
    logit_grad = chosen_grad.astype(BF16)
    mixed_first = after(mixed_first, mixture_rows)
    mixed_grad = mm(logit_grad, router[:experts]) + jnp.concatenate([mixed_first, mixed_second[:, :half]], axis=1)
    mixture_back, mixture_terms = normalize_back(mixed_grad, after_attn, scale_mixture, mixture_gain)
    after_grad = upstream + mixture_back
    after_low = after_grad.astype(BF16)

    router_part = t_mm(logit_grad, mixed_low).astype(BF16).reshape(members, planes, model)
    router_part = jnp.pad(router_part, ((0, 0), (0, 8 - planes), (0, 0)))
    mixture_part = jnp.sum(mixture_terms, axis=0, keepdims=True)

    after_all = gather(after_low, "expert")
    mixture_parts = combine(unpick, after(mixture_rows, after_low), planes)
    mixture_first = plane_sum(mixture_parts)
    gate_gradient, up_gradient = hidden_gradient(
        arrived[0], arrived[1], *after((gate_grad, up_grad), after_low, *mixture_parts))
    after_all = after(after_all, gate_gradient, router_part, mixture_part, mixture_first)
    mixture_rows = exchange(after(produced[1], after_all), "expert")
    out_partial = out_gradient(member.astype(jnp.int32).reshape(1), attended_all, after_all, out_piece)
    out_share = lax.psum_scatter(
        after(out_partial, mixture_first).reshape(members * width, out_piece), "dp", scatter_dimension=0, tiled=True).astype(F32)
    attended_grad = out_back(after(after_all, out_partial), out_heads)
    dq, dk, dv, query_terms, key_terms = attend_back(
        prefix_len, query_low, key_low, value_low, attended_low, inverse, attended_grad, qraw, kraw, cosine, sine,
        query_gain, key_norm_gain)
    normed_partial = unproject(
        own_rows, dq, dk, dv, wq_pieces, kv_weight, normed, reorder(attention_gain, 0), router_part, mixture_part,
        query_terms, key_terms)
    query_partial = t_mm(normed, dq).astype(BF16)
    mixture_parts = combine(unpick, after(mixture_rows, normed_partial), planes)
    mixture_second = plane_sum(mixture_parts)
    arrived_sums = exchange(after(normed_partial, out_share, query_partial, *mixture_parts), "expert")
    normed_sums = jnp.sum(arrived_sums.astype(F32), axis=0)
    input_back, _ = normalize_back(
        reorder(normed_sums[:own_rows], 1), residual_in, scale_attention, attention_gain)
    input_grad = after_grad + input_back
    layer_out = (after_attn + jnp.concatenate([mixture_first, mixture_second], axis=1)).astype(BF16)

    query_share = plane_sum(cut(after(query_partial, mixture_second)))
    down_grad = down_gradient(upstream_a, upstream_b, weight_wide, after(activated, query_partial))
    kv_partial = jnp.concatenate([t_mm(normed, dk), t_mm(normed, dv)], axis=1)

    def kv_cols(j):
        start = j * piece
        return jnp.concatenate(
            [lax.dynamic_slice(kv_partial, (0, start), (model, piece)),
             lax.dynamic_slice(kv_partial, (0, HEAD_SIZE + start), (model, piece))], axis=1)

    kv_total = kv_cols(place)
    for shift in range(1, group):
        pairs = [(e, e - e % group + (e % group + shift) % group) for e in range(members)]
        kv_total += lax.ppermute(kv_cols((place + shift) % group).astype(BF16), "expert", pairs).astype(F32)
    kv_share = plane_sum(cut(kv_total.astype(BF16)))
    key_share = kv_share[:, :piece]
    value_share = kv_share[:, piece:]

    last = normed_sums[own_rows:]
    attention_sum, mixture_sum, head_sum = (last[8 + 2 * n] + last[9 + 2 * n] for n in range(3))
    gains = jnp.concatenate([reorder(attention_sum, 0), mixture_sum, head_sum[:2 * HEAD_SIZE]])
    total = jnp.concatenate([gains, last[:planes].reshape(-1)]).reshape(-1, HEAD_SIZE)
    step = 1
    while step < planes:
        total = total + lax.ppermute(total, "dp", [(i, i ^ step) for i in range(planes)])
        step *= 2
    total = total.reshape(-1)
    gains, router_total = total[:gains.shape[0]], total[gains.shape[0]:].reshape(planes, model)
    router_share = lax.dynamic_slice(router_total, (0, plane * part_rows), (planes, part_rows)).T
    attention_total, mixture_total = gains[:model], gains[model:2 * model]
    query_total, key_total = gains[2 * model:2 * model + HEAD_SIZE], gains[2 * model + HEAD_SIZE:]
    return (
        layer_out,
        input_grad,
        query_share,
        key_share,
        value_share,
        out_share,
        router_share,
        attention_total,
        mixture_total,
        query_total,
        key_total,
        gate_gradient,
        up_gradient,
        down_grad,
    )


def solution(mesh):
    rows = P(("dp", "expert"), None)
    grid = P("dp", "expert")
    experts = P(("dp", "expert"), None, None)
    in_specs = (rows, rows, P("dp"), grid, grid, grid, grid, grid, P(), P(), P(), P(), experts, experts, experts, rows)
    out_specs = (rows, rows, grid, grid, grid, grid, grid, P(), P(), P(), P(), experts, experts, experts)
    return jax.shard_map(shards, mesh=mesh, in_specs=in_specs, out_specs=out_specs, check_vma=False)
```

```python
import functools
import math

import jax
import jax.numpy as jnp
from jax import lax
from jax.experimental import pallas as pl
from jax.experimental.pallas import tpu as pltpu
from jax.sharding import PartitionSpec as P

QUERY_HEADS = 32
KEY_VALUE_HEADS = 4
HEAD_SIZE = 128
TOP = 8
EPS = 1e-06
ROTARY_BASE = 1000000.0
VERY_NEGATIVE = -1e30
SOFTMAX_SCALE = HEAD_SIZE ** (-0.5)
LOG2_SCALE = SOFTMAX_SCALE * math.log2(math.e)
VMEM_BYTES = 24 * 1024 * 1024
F32 = jnp.float32
BF16 = jnp.bfloat16


def cost(microseconds):
    return pl.CostEstimate(flops=int(microseconds * 1.1e9) + 1, bytes_accessed=1, transcendentals=0)


def mm(a, b):
    return lax.dot_general(a, b, (((1,), (0,)), ((), ())), preferred_element_type=F32)


def mm_t(a, b):
    return lax.dot_general(a, b, (((1,), (1,)), ((), ())), preferred_element_type=F32)


def t_mm(a, b):
    return lax.dot_general(a, b, (((0,), (0,)), ((), ())), preferred_element_type=F32)


def row_scale(source):
    return lax.rsqrt(jnp.mean(source * source, axis=-1, keepdims=True) + EPS)


def normalize_back(upstream, source, scaling, gain_row):
    unit_rows = source * scaling
    weighted = upstream * gain_row
    inner_mean = jnp.mean(weighted * unit_rows, axis=-1, keepdims=True)
    return (scaling * (weighted - unit_rows * inner_mean), upstream * unit_rows)


def rotary_tables(span):
    half = HEAD_SIZE // 2
    frequency = jnp.power(ROTARY_BASE, -jnp.arange(half, dtype=F32) * 2.0 / HEAD_SIZE)
    angles = jnp.arange(span, dtype=jnp.int32).astype(F32)[:, None] * frequency[None, :]
    cosine, sine = jnp.cos(angles), jnp.sin(angles)
    return (
        jnp.concatenate([cosine, cosine], axis=-1),
        jnp.concatenate([-sine, sine], axis=-1),
    )


def turned(u, gain, cosine, sine):
    n = u * row_scale(u) * gain
    return (n * cosine + pltpu.roll(n, HEAD_SIZE // 2, 1) * sine).astype(BF16)


def pieces_product(x, refs):
    size = refs[0].shape[0]
    total = mm(x[:, :size], refs[0][...])
    for s in range(1, len(refs)):
        total += mm(x[:, s * size:(s + 1) * size], refs[s][...])
    return total


def project_kernel(x_ref, cos_ref, sin_ref, qg_ref, kg_ref, *refs):
    weights, (qraw_ref, kraw_ref, q_ref, k_ref, v_ref) = refs[:-5], refs[-5:]
    total = pieces_product(x_ref[...], weights)
    width = q_ref.shape[1]
    cosine, sine = cos_ref[...], sin_ref[...]
    qraw_ref[...] = total[:, :width]
    for h in range(width // HEAD_SIZE):
        cols = slice(h * HEAD_SIZE, (h + 1) * HEAD_SIZE)
        q_ref[:, cols] = turned(total[:, cols], qg_ref[...], cosine, sine)
    key = total[:, width:width + HEAD_SIZE]
    kraw_ref[...] = key
    k_ref[...] = turned(key, kg_ref[...], cosine, sine)
    v_ref[...] = total[:, width + HEAD_SIZE:].astype(BF16)


def project(x, weights, cosine, sine, q_gain, k_gain):
    span, model = x.shape
    width = weights[0].shape[1] - 2 * HEAD_SIZE
    tile = 512
    row = lambda w: pl.BlockSpec((tile, w), lambda i: (i, 0))
    whole = lambda a, b: pl.BlockSpec((a, b), lambda i: (0, 0))
    out = [(width, F32), (HEAD_SIZE, F32), (width, BF16), (HEAD_SIZE, BF16), (HEAD_SIZE, BF16)]
    return pl.pallas_call(
        project_kernel,
        grid=(span // tile,),
        in_specs=[row(model), row(HEAD_SIZE), row(HEAD_SIZE), whole(1, HEAD_SIZE), whole(1, HEAD_SIZE)]
        + [whole(*w.shape) for w in weights],
        out_specs=[row(w) for w, _ in out],
        out_shape=[jax.ShapeDtypeStruct((span, w), t) for w, t in out],
        compiler_params=pltpu.CompilerParams(vmem_limit_bytes=VMEM_BYTES),
        cost_estimate=cost(0),
        name="project",
    )(x, cosine, sine, q_gain[None], k_gain[None], *weights)


def block_limits(span, tile):
    return [(r0, max(r0 + tile, span // 2)) for r0 in range(0, span, tile)]


def masked(values, r0, limit, prefix):
    tile = values.shape[0]
    rows = r0 + lax.broadcasted_iota(jnp.int32, (tile, limit - r0), 0)
    cols = r0 + lax.broadcasted_iota(jnp.int32, (tile, limit - r0), 1)
    right = jnp.where((cols <= rows) | (cols < prefix), values[:, r0:], 0.0)
    return right if r0 == 0 else jnp.concatenate([values[:, :r0], right], axis=1)


def attend_kernel(tile, prefix_ref, q_ref, k_ref, v_ref, o_ref, l_ref, wide_ref):
    span = q_ref.shape[0]

    @pl.when(pl.program_id(0) == 0)
    def _():
        wide_ref[:, :HEAD_SIZE] = v_ref[...]
        wide_ref[:, HEAD_SIZE:] = jnp.ones((span, HEAD_SIZE), BF16)

    prefix = prefix_ref[0]
    for r0, limit in block_limits(span, tile):
        rows = slice(r0, r0 + tile)
        scores = mm_t(q_ref[rows, :], k_ref[:limit, :])
        weights = masked(jnp.exp2(scores * LOG2_SCALE), r0, limit, prefix)
        sums = mm(weights.astype(BF16), wide_ref[:limit, :])
        inverse = 1.0 / sums[:, HEAD_SIZE:]
        o_ref[rows, :] = (sums[:, :HEAD_SIZE] * inverse).astype(BF16)
        l_ref[rows, :] = inverse


def attend(prefix, q, k, v):
    span, width = q.shape
    heads = width // HEAD_SIZE
    head = pl.BlockSpec((span, HEAD_SIZE), lambda h: (0, h))
    shared = pl.BlockSpec((span, HEAD_SIZE), lambda h: (0, 0))
    return pl.pallas_call(
        functools.partial(attend_kernel, 256),
        grid=(heads,),
        in_specs=[pl.BlockSpec(memory_space=pltpu.SMEM), head, shared, shared],
        out_specs=[head, head],
        out_shape=[jax.ShapeDtypeStruct((span, width), BF16), jax.ShapeDtypeStruct((span, width), F32)],
        scratch_shapes=[pltpu.VMEM((span, 2 * HEAD_SIZE), BF16)],
        compiler_params=pltpu.CompilerParams(vmem_limit_bytes=VMEM_BYTES),
        cost_estimate=cost(0),
        name="attend",
    )(prefix, q, k, v)


def attend_back_kernel(tile, prefix_ref, q_ref, k_ref, v_ref, o_ref, l_ref, do_ref, qraw_ref, kraw_ref, cos_ref, sin_ref,
                       qg_ref, kg_ref, dq_ref, dk_ref, dv_ref, qgg_ref, kgg_ref, dk_sum, dv_sum):
    span = q_ref.shape[0]
    step = pl.program_id(0)

    @pl.when(step == 0)
    def _():
        dk_sum[...] = jnp.zeros_like(dk_sum)
        dv_sum[...] = jnp.zeros_like(dv_sum)
        qgg_ref[...] = jnp.zeros_like(qgg_ref)

    def unturned(grad, rows):
        return grad * cos_ref[rows, :] - pltpu.roll(grad, HEAD_SIZE // 2, 1) * sin_ref[rows, :]

    prefix = prefix_ref[0]
    for r0, limit in block_limits(span, tile):
        rows = slice(r0, r0 + tile)
        q, do = q_ref[rows, :], do_ref[rows, :]
        keys, values = k_ref[:limit, :], v_ref[:limit, :]
        weights = masked(jnp.exp2(mm_t(q, keys) * LOG2_SCALE), r0, limit, prefix)
        probs = weights * jnp.concatenate([l_ref[rows, :]] * (limit // HEAD_SIZE), axis=1)
        delta = jnp.sum(do.astype(F32) * o_ref[rows, :].astype(F32), axis=1, keepdims=True)
        score_grad = (probs * (mm_t(do, values) - delta)).astype(BF16)
        dv_sum[:limit, :] += t_mm(probs.astype(BF16), do)
        dk_sum[:limit, :] += t_mm(score_grad, q)
        turn = unturned(mm(score_grad, keys) * SOFTMAX_SCALE, rows)
        raw = qraw_ref[rows, :]
        back, terms = normalize_back(turn, raw, row_scale(raw), qg_ref[...])
        dq_ref[rows, :] = back.astype(BF16)
        qgg_ref[...] += jnp.sum(terms, axis=0, keepdims=True)

    @pl.when(step == pl.num_programs(0) - 1)
    def _():
        raw = kraw_ref[...]
        turn = unturned(dk_sum[...] * SOFTMAX_SCALE, slice(None))
        back, terms = normalize_back(turn, raw, row_scale(raw), kg_ref[...])
        dk_ref[...] = back.astype(BF16)
        dv_ref[...] = dv_sum[...].astype(BF16)
        kgg_ref[...] = jnp.sum(terms, axis=0, keepdims=True)


def attend_back(prefix, q, k, v, o, inverse, do, qraw, kraw, cosine, sine, q_gain, k_gain):
    span, width = q.shape
    heads = width // HEAD_SIZE
    head = pl.BlockSpec((span, HEAD_SIZE), lambda h: (0, h))
    shared = pl.BlockSpec((span, HEAD_SIZE), lambda h: (0, 0))
    gain = pl.BlockSpec((1, HEAD_SIZE), lambda h: (0, 0))
    return pl.pallas_call(
        functools.partial(attend_back_kernel, 256),
        grid=(heads,),
        in_specs=[pl.BlockSpec(memory_space=pltpu.SMEM), head, shared, shared, head, head, head, head, shared, shared,
                  shared, gain, gain],
        out_specs=[head, shared, shared, gain, gain],
        out_shape=[
            jax.ShapeDtypeStruct((span, width), BF16),
            jax.ShapeDtypeStruct((span, HEAD_SIZE), BF16),
            jax.ShapeDtypeStruct((span, HEAD_SIZE), BF16),
            jax.ShapeDtypeStruct((1, HEAD_SIZE), F32),
            jax.ShapeDtypeStruct((1, HEAD_SIZE), F32),
        ],
        scratch_shapes=[pltpu.VMEM((span, HEAD_SIZE), F32), pltpu.VMEM((span, HEAD_SIZE), F32)],
        compiler_params=pltpu.CompilerParams(vmem_limit_bytes=VMEM_BYTES),
        cost_estimate=cost(0),
        name="attend_back",
    )(prefix, q, k, v, o, inverse, do, qraw, kraw, cosine, sine, q_gain[None], k_gain[None])


def unproject_kernel(own_rows, dq_ref, dk_ref, dv_ref, x_ref, gain_ref, router_ref, mix_ref, qg_ref, kg_ref,
                     *refs):
    weights, out_ref, sum_ref = refs[:-2], refs[-2], refs[-1]
    span, model = x_ref.shape
    size = weights[0].shape[0]
    tile = 512
    each = tile // own_rows
    for r in range(span // tile):
        rows = slice(r * tile, (r + 1) * tile)
        grads = jnp.concatenate([dq_ref[rows, :], dk_ref[rows, :], dv_ref[rows, :]], axis=1)
        for s, weight in enumerate(weights):
            cols = slice(s * size, (s + 1) * size)
            total = mm_t(grads, weight[...])
            low = total.astype(BF16)
            for m in range(each):
                out_ref[r * each + m, :own_rows, cols] = low[m * own_rows:(m + 1) * own_rows]
            part = jnp.sum(total * x_ref[rows, cols].astype(F32), axis=0, keepdims=True)
            if r == 0:
                sum_ref[:, cols] = part
            else:
                sum_ref[:, cols] += part
    heads = jnp.concatenate([qg_ref[...], kg_ref[...], jnp.zeros((1, model - 2 * HEAD_SIZE), F32)], axis=1)
    place = lax.broadcasted_iota(jnp.int32, (8, model), 0)
    sums = jnp.zeros((8, model), F32)
    for n, values in enumerate((sum_ref[...] / gain_ref[...], mix_ref[...], heads)):
        high = values.astype(BF16).astype(F32)
        sums = jnp.where(place == 2 * n, high, jnp.where(place == 2 * n + 1, values - high, sums))
    sums = sums.astype(BF16)
    for m in range(out_ref.shape[0]):
        out_ref[m, own_rows:own_rows + 8, :] = router_ref[m]
        out_ref[m, own_rows + 8:, :] = sums


def unproject(own_rows, dq, dk, dv, pieces, x, gain, router_part, mixture_part, query_part, key_part):
    span, model = x.shape
    return pl.pallas_call(
        functools.partial(unproject_kernel, own_rows),
        out_shape=jax.ShapeDtypeStruct((span // own_rows, own_rows + 16, model), BF16),
        scratch_shapes=[pltpu.VMEM((1, model), F32)],
        compiler_params=pltpu.CompilerParams(vmem_limit_bytes=44 * 1024 * 1024),
        cost_estimate=cost(0),
        name="unproject",
    )(dq, dk, dv, x, gain[None], router_part, mixture_part, query_part, key_part, *pieces)


def out_project_kernel(plane_ref, a_ref, *refs):
    out_ref = refs[-1]
    pieces = refs[:-1]
    members, _, width = a_ref.shape
    planes, each = len(pieces), members // len(pieces)
    total = None
    for s, piece in enumerate(pieces):
        block = lax.rem(plane_ref[0] + planes - s, planes) * each
        for i in range(each):
            part = mm(a_ref[block + i], piece[i * width:(i + 1) * width, :])
            total = part if total is None else total + part
    out_ref[...] = total.astype(BF16)


def out_project(plane, attended_all, pieces):
    members, span, width = attended_all.shape
    size, columns = pieces[0].shape
    tile = 256
    return pl.pallas_call(
        out_project_kernel,
        grid=(span // tile,),
        in_specs=[pl.BlockSpec(memory_space=pltpu.SMEM), pl.BlockSpec((members, tile, width), lambda i: (0, i, 0))]
        + [pl.BlockSpec((size, columns), lambda i: (0, 0))] * len(pieces),
        out_specs=pl.BlockSpec((tile, columns), lambda i: (i, 0)),
        out_shape=jax.ShapeDtypeStruct((span, columns), BF16),
        compiler_params=pltpu.CompilerParams(vmem_limit_bytes=VMEM_BYTES),
        cost_estimate=cost(0),
        name="out_project",
    )(plane, attended_all, *pieces)


def out_back_kernel(g_ref, w_ref, out_ref):
    columns = w_ref.shape[2]
    total = mm_t(g_ref[:, :columns], w_ref[0])
    for m in range(1, w_ref.shape[0]):
        total += mm_t(g_ref[:, m * columns:(m + 1) * columns], w_ref[m])
    out_ref[...] = total.astype(BF16)


def out_back(after_all, heads):
    span, model = after_all.shape
    members, width, columns = heads.shape
    tile = 512
    return pl.pallas_call(
        out_back_kernel,
        grid=(span // tile,),
        in_specs=[pl.BlockSpec((tile, model), lambda i: (i, 0)),
                  pl.BlockSpec((members, width, columns), lambda i: (0, 0, 0))],
        out_specs=pl.BlockSpec((tile, width), lambda i: (i, 0)),
        out_shape=jax.ShapeDtypeStruct((span, width), BF16),
        compiler_params=pltpu.CompilerParams(vmem_limit_bytes=VMEM_BYTES),
        cost_estimate=cost(0),
        name="out_back",
    )(after_all, heads)


def out_gradient_kernel(member_ref, a_ref, g_ref, out_ref):
    out_ref[0] = t_mm(a_ref[0], g_ref[...]).astype(BF16)


def out_gradient(member, attended_all, after_all, columns):
    members, span, width = attended_all.shape
    return pl.pallas_call(
        out_gradient_kernel,
        grid_spec=pltpu.PrefetchScalarGridSpec(
            num_scalar_prefetch=1,
            grid=(members,),
            in_specs=[pl.BlockSpec((1, span, width), lambda m, me: (m, 0, 0)),
                      pl.BlockSpec((span, columns), lambda m, me: (0, me[0]))],
            out_specs=pl.BlockSpec((1, width, columns), lambda m, me: (m, 0, 0)),
        ),
        out_shape=jax.ShapeDtypeStruct((members, width, columns), BF16),
        compiler_params=pltpu.CompilerParams(vmem_limit_bytes=VMEM_BYTES),
        cost_estimate=cost(0),
        name="out_gradient",
    )(member, attended_all, after_all)


def expert_kernel(experts, own_ref, xa_ref, xb_ref, mask_ref, router_ref, gate_ref, up_ref, down_ref,
                  act_ref, gg_ref, ug_ref, w_ref, route_ref, sum_ref):
    half = xa_ref.shape[1]
    step = pl.program_id(0)
    own = own_ref[0]

    def product(left, right, weight):
        return mm(left[...], weight[:half, :]) + mm(right[...], weight[half:, :])

    @pl.when(step == 0)
    def _():
        mask = mask_ref[...].astype(F32)
        logits = mm_t(xa_ref[...], router_ref[:, :half]) + mm_t(xb_ref[...], router_ref[:, half:])
        logits = jnp.where(mask > 0, logits, VERY_NEGATIVE)
        raised = jnp.where(mask > 0, jnp.exp(logits - jnp.max(logits, axis=-1, keepdims=True)), 0.0)
        total = jnp.maximum(jnp.sum(raised, axis=-1, keepdims=True), 1e-30)
        lanes = lax.broadcasted_iota(jnp.int32, raised.shape, 1)
        weight = jnp.sum(jnp.where(lanes == own, raised, 0.0), axis=-1, keepdims=True) / total
        w_ref[...] = jnp.broadcast_to(weight, w_ref.shape)

    gate_raw, up_raw = product(xa_ref, xb_ref, gate_ref), product(xa_ref, xb_ref, up_ref)
    down = down_ref[...]
    weight = w_ref[:, :1]
    sig = 1.0 / (1.0 + jnp.exp(-gate_raw))
    silu = gate_raw * sig
    activated = (silu * up_raw).astype(BF16)
    act_ref[...] = activated
    route = jnp.sum(activated.astype(F32) * down, axis=-1, keepdims=True)
    grad = weight * down
    gg_ref[...] = (grad * up_raw * sig * (1.0 + gate_raw * (1.0 - sig))).astype(BF16)
    ug_ref[...] = (grad * silu).astype(BF16)
    route = jnp.broadcast_to(route, sum_ref.shape)

    @pl.when(step == 0)
    def _():
        sum_ref[...] = route

    @pl.when(step > 0)
    def _():
        sum_ref[...] += route

    @pl.when(step == pl.num_programs(0) - 1)
    def _():
        total = sum_ref[:, :1]
        high = total.astype(BF16).astype(F32)
        lanes = lax.broadcasted_iota(jnp.int32, route_ref.shape, 1)
        route_ref[...] = jnp.where(
            lanes == own, high, jnp.where(lanes == experts + own, total - high, 0.0)).astype(BF16)


def expert_forward(experts, own, xa, xb, masked_rows, router, gate, up, upstream_down):
    rows, half = xa.shape
    model, hidden = gate.shape
    padded = router.shape[0]
    route_width = -(-2 * experts // HEAD_SIZE) * HEAD_SIZE
    tile = 256
    whole = lambda a, b: pl.BlockSpec((a, b), lambda i: (0, 0))
    column = lambda a: pl.BlockSpec((a, tile), lambda i: (0, i))
    return pl.pallas_call(
        functools.partial(expert_kernel, experts),
        grid=(hidden // tile,),
        in_specs=[pl.BlockSpec(memory_space=pltpu.SMEM), whole(rows, half), whole(rows, half),
                  pl.BlockSpec((rows, padded), lambda i: (0, half // padded)), whole(padded, model), column(model),
                  column(model), column(rows)],
        out_specs=[column(rows), column(rows), column(rows), whole(rows, HEAD_SIZE), whole(rows, route_width)],
        out_shape=[
            jax.ShapeDtypeStruct((rows, hidden), BF16),
            jax.ShapeDtypeStruct((rows, hidden), BF16),
            jax.ShapeDtypeStruct((rows, hidden), BF16),
            jax.ShapeDtypeStruct((rows, HEAD_SIZE), F32),
            jax.ShapeDtypeStruct((rows, route_width), BF16),
        ],
        scratch_shapes=[pltpu.VMEM((rows, HEAD_SIZE), F32)],
        compiler_params=pltpu.CompilerParams(vmem_limit_bytes=40 * 1024 * 1024),
        cost_estimate=cost(18),
        name="expert_forward",
    )(own, xa, xb, masked_rows, router, gate, up, upstream_down)


def row_gradient_kernel(start, stop, gg_ref, ug_ref, gate_ref, up_ref, *rest):
    part = slice(start, stop)
    total = (mm_t(gg_ref[...], gate_ref[part, :]) + mm_t(ug_ref[...], up_ref[part, :])).astype(BF16)
    out_ref = rest[-1]
    out_ref[:, :total.shape[1]] = total
    if len(rest) == 2:
        out_ref[:, total.shape[1]:] = rest[0][...]


def row_gradient(gg, ug, gate, up, start, stop, route=None):
    rows, hidden = gg.shape
    tile = rows // 4
    row = lambda w: pl.BlockSpec((tile, w), lambda i: (i, 0))
    weight = pl.BlockSpec(gate.shape, lambda i: (0, 0))
    extra = [] if route is None else [route]
    width = stop - start + sum(e.shape[1] for e in extra)
    return pl.pallas_call(
        functools.partial(row_gradient_kernel, start, stop),
        grid=(rows // tile,),
        in_specs=[row(hidden), row(hidden), weight, weight] + [row(e.shape[1]) for e in extra],
        out_specs=row(width),
        out_shape=jax.ShapeDtypeStruct((rows, width), BF16),
        compiler_params=pltpu.CompilerParams(vmem_limit_bytes=VMEM_BYTES),
        cost_estimate=cost(8),
        name="row_gradient",
    )(gg, ug, gate, up, *extra)


def down_back_kernel(ca_ref, cb_ref, down_ref, out_ref):
    half = cb_ref.shape[1]
    out_ref[...] = mm_t(ca_ref[...], down_ref[:, :half]) + mm_t(cb_ref[...], down_ref[:, half:])


def down_back(ca, cb, down):
    rows, half = cb.shape
    hidden, model = down.shape
    tile = 256
    whole = pl.BlockSpec((rows, half), lambda i: (0, 0))
    return pl.pallas_call(
        down_back_kernel,
        grid=(hidden // tile,),
        in_specs=[whole, whole, pl.BlockSpec((tile, model), lambda i: (i, 0))],
        out_specs=pl.BlockSpec((rows, tile), lambda i: (0, i)),
        out_shape=jax.ShapeDtypeStruct((rows, hidden), F32),
        compiler_params=pltpu.CompilerParams(vmem_limit_bytes=VMEM_BYTES),
        cost_estimate=cost(0),
        name="down_back",
    )(ca, cb, down)


def produce_kernel(act_ref, w_ref, down_ref, *outs):
    total = (w_ref[:, :1] * mm(act_ref[...], down_ref[...])).astype(BF16)
    first = outs[0].shape[1]
    outs[0][...] = total[:, :first]
    outs[1][...] = total[:, first:]


def produce(activated, weight, down, first):
    rows, hidden = activated.shape
    model = down.shape[1]
    tile = rows // 4
    row = lambda w: pl.BlockSpec((tile, w), lambda i: (i, 0))
    return pl.pallas_call(
        produce_kernel,
        grid=(rows // tile,),
        in_specs=[row(hidden), row(HEAD_SIZE), pl.BlockSpec((hidden, model), lambda i: (0, 0))],
        out_specs=[row(first), row(model - first)],
        out_shape=[jax.ShapeDtypeStruct((rows, w), BF16) for w in (first, model - first)],
        compiler_params=pltpu.CompilerParams(vmem_limit_bytes=VMEM_BYTES),
        cost_estimate=cost(0),
        name="produce",
    )(activated, weight, down)


def hidden_gradient_kernel(xa_ref, xb_ref, gg_ref, ug_ref, dg_ref, du_ref):
    in_first = pl.program_id(0) < pl.num_programs(0) // 2
    for x_ref, now in ((xa_ref, in_first), (xb_ref, jnp.logical_not(in_first))):
        @pl.when(now)
        def _():
            dg_ref[0] = t_mm(x_ref[...], gg_ref[...])
            du_ref[0] = t_mm(x_ref[...], ug_ref[...])


def hidden_gradient(xa, xb, gg, ug):
    rows, half = xa.shape
    hidden = gg.shape[1]
    tile = 256
    count = half // tile
    whole = pl.BlockSpec((rows, hidden), lambda i: (0, 0))
    out = pl.BlockSpec((1, tile, hidden), lambda i: (0, i, 0))
    return pl.pallas_call(
        hidden_gradient_kernel,
        grid=(2 * count,),
        in_specs=[pl.BlockSpec((rows, tile), lambda i: (0, jnp.minimum(i, count - 1))),
                  pl.BlockSpec((rows, tile), lambda i: (0, jnp.maximum(i - count, 0))), whole, whole],
        out_specs=[out, out],
        out_shape=[jax.ShapeDtypeStruct((1, 2 * half, hidden), F32)] * 2,
        compiler_params=pltpu.CompilerParams(vmem_limit_bytes=VMEM_BYTES),
        cost_estimate=cost(0),
        name="hidden_gradient",
    )(xa, xb, gg, ug)


def down_gradient_kernel(ca_ref, cb_ref, w_ref, act_ref, out_ref):
    in_first = pl.program_id(0) < pl.num_programs(0) // 2
    for c_ref, now in ((ca_ref, in_first), (cb_ref, jnp.logical_not(in_first))):
        @pl.when(now)
        def _():
            out_ref[0] = t_mm(act_ref[...], (w_ref[:, :1] * c_ref[...].astype(F32)).astype(BF16))


def down_gradient(ca, cb, weight, activated):
    rows, half = cb.shape
    hidden = activated.shape[1]
    tile = 256
    count = half // tile
    return pl.pallas_call(
        down_gradient_kernel,
        grid=(2 * count,),
        in_specs=[pl.BlockSpec((rows, tile), lambda i: (0, jnp.minimum(i, count - 1))),
                  pl.BlockSpec((rows, tile), lambda i: (0, jnp.maximum(i - count, 0))),
                  pl.BlockSpec((rows, HEAD_SIZE), lambda i: (0, 0)), pl.BlockSpec((rows, hidden), lambda i: (0, 0))],
        out_specs=pl.BlockSpec((1, hidden, tile), lambda i: (0, 0, i)),
        out_shape=jax.ShapeDtypeStruct((1, hidden, 2 * half), F32),
        compiler_params=pltpu.CompilerParams(vmem_limit_bytes=VMEM_BYTES),
        cost_estimate=cost(0),
        name="down_gradient",
    )(ca, cb, weight, activated)


def dispatch_kernel(pick_ref, *refs):
    out_ref, all_ref = refs[-2:]
    size = all_ref.shape[0] // (len(refs) - 2)

    @pl.when(pl.program_id(0) == 0)
    def _():
        for s, ref in enumerate(refs[:-2]):
            all_ref[s * size:(s + 1) * size, :] = ref[...]

    out_ref[...] = mm(pick_ref[...], all_ref[...]).astype(BF16)


def dispatch(pick, pieces):
    rows, column = pick.shape
    size, width = column // len(pieces), pieces[0].shape[1]
    tile = rows // 4
    return pl.pallas_call(
        dispatch_kernel,
        grid=(rows // tile,),
        in_specs=[pl.BlockSpec((tile, column), lambda i: (i, 0))]
        + [pl.BlockSpec((size, width), lambda i: (0, 0))] * len(pieces),
        out_specs=pl.BlockSpec((tile, width), lambda i: (i, 0)),
        out_shape=jax.ShapeDtypeStruct((rows, width), BF16),
        scratch_shapes=[pltpu.VMEM((column, width), BF16)],
        compiler_params=pltpu.CompilerParams(vmem_limit_bytes=VMEM_BYTES),
        cost_estimate=cost(0),
        name="dispatch",
    )(pick, *pieces)


def combine_kernel(pick_ref, rows_ref, *outs):
    total = mm(pick_ref[...], rows_ref[...]).astype(BF16)
    size = total.shape[0] // len(outs)
    for s, out in enumerate(outs):
        out[...] = total[s * size:(s + 1) * size]


def combine(pick, rows, count, microseconds=0):
    column, slots = pick.shape
    width = rows.shape[1]
    tile = max(t for t in range(HEAD_SIZE, 513, HEAD_SIZE) if width % t == 0)
    size = column // count
    out = pl.BlockSpec((size, tile), lambda i: (0, i))
    return pl.pallas_call(
        combine_kernel,
        grid=(width // tile,),
        in_specs=[pl.BlockSpec((column, slots), lambda i: (0, 0)), pl.BlockSpec((slots, tile), lambda i: (0, i))],
        out_specs=[out] * count,
        out_shape=[jax.ShapeDtypeStruct((size, width), BF16)] * count,
        compiler_params=pltpu.CompilerParams(vmem_limit_bytes=VMEM_BYTES),
        cost_estimate=cost(microseconds),
        name="combine",
    )(pick, rows)


def after(array, *earlier):
    return lax.optimization_barrier((array, *earlier))[0]


def shards(
    tokens,
    routes,
    prefix_len,
    query_weight,
    key_matrix,
    value_matrix,
    out_weight,
    router_weight,
    attention_gain,
    mixture_gain,
    query_gain,
    key_norm_gain,
    expert_gate,
    expert_up,
    expert_down,
    cotangent,
):
    planes, members = lax.axis_size("dp"), lax.axis_size("expert")
    devices = planes * members
    plane, member = lax.axis_index("dp"), lax.axis_index("expert")
    own_rows, model = tokens.shape
    span = own_rows * members
    column = own_rows * planes
    experts = devices
    width = query_weight.shape[1]
    piece = key_matrix.shape[1]
    group = HEAD_SIZE // piece
    block_slots = max(2, 6 * own_rows * TOP // (5 * experts))
    slots = planes * block_slots
    padded = -(-experts // HEAD_SIZE) * HEAD_SIZE
    half = model // 2
    first = 5 * model // 8
    rest = model - first
    part_rows = model // planes
    gate, up, down = expert_gate[0], expert_up[0], expert_down[0]

    def gather(array, axis, dimension=0):
        return lax.all_gather(array, axis, axis=dimension, tiled=True)

    def exchange(array, axis):
        return lax.all_to_all(array, axis, split_axis=0, concat_axis=0, tiled=True)

    def plane_pieces(array):
        def shift(value, by):
            return lax.ppermute(value, "dp", [(i, (i + by) % planes) for i in range(planes)])

        pieces = [array] + [None] * (planes - 1)
        for s in range(1, planes // 2 + 1):
            pieces[s] = shift(pieces[s - 1], 1)
            if planes - s > s:
                pieces[planes - s] = shift(pieces[(planes - s + 1) % planes], -1)
        return pieces

    def plane_sum_direct(pieces):
        total = pieces[0].astype(F32)
        for s in range(1, planes):
            total += lax.ppermute(pieces[s], "dp", [(i, (i - s) % planes) for i in range(planes)]).astype(F32)
        return total

    def plane_sum(pieces, between=(), last=()):
        def shift(value, by):
            return lax.ppermute(value, "dp", [(i, (i + by) % planes) for i in range(planes)]).astype(F32)

        total = pieces[0].astype(F32)
        middle = planes // 2
        for order, by in ((range(middle, 0, -1), -1), (range(middle + 1, planes), 1)):
            running = None
            for s in order:
                if running is None:
                    running = pieces[s]
                else:
                    running = (after(shift(running, by), *between) + pieces[s].astype(F32)).astype(BF16)
            if running is not None:
                total += after(shift(running, by), *last)
        return total

    def reorder(array, dimension):
        size = array.shape[dimension] // planes
        return jnp.concatenate(
            [lax.dynamic_slice_in_dim(array, (plane - s) % planes * size, size, dimension) for s in range(planes)],
            axis=dimension)

    def cut(array):
        return [array[s * (array.shape[0] // planes):(s + 1) * (array.shape[0] // planes)] for s in range(planes)]

    residual_in = tokens.astype(F32)
    scale_attention = row_scale(residual_in)
    normed_own = (residual_in * scale_attention * attention_gain).astype(BF16)
    normed = gather(reorder(normed_own, 1), "expert")

    kv_own = jnp.concatenate([key_matrix, value_matrix], axis=1)
    place = member % group
    kv_parts = [kv_own]
    for shift in range(1, group):
        pairs = [(e - e % group + (e % group + shift) % group, e) for e in range(members)]
        kv_parts.append(lax.ppermute(kv_own, "expert", pairs))

    def kv_piece(j):
        value = kv_parts[0]
        for shift in range(1, group):
            value = jnp.where((place + shift) % group == j, kv_parts[shift], value)
        return value

    ordered = [kv_piece(j) for j in range(group)]
    qkv_part = jnp.concatenate(
        [query_weight] + [p[:, :piece] for p in ordered] + [p[:, piece:] for p in ordered], axis=1)

    expert_ids = jnp.arange(experts, dtype=jnp.int32)
    mask_own = jnp.sum((routes[:, :, None] == expert_ids[None, None, :]).astype(F32), axis=1)
    mask_wide = jnp.pad(mask_own, ((0, 0), (0, padded - experts))).astype(BF16)
    qkv_pieces = plane_pieces(qkv_part)
    upstream_pieces = plane_pieces(
        after(jnp.concatenate([cotangent[:, :half], mask_wide], axis=1), *qkv_pieces[1:]))
    router_rows = gather(after(router_weight.T, normed), "expert").reshape(2 * members, half)
    out_piece = out_weight.shape[1]
    out_pieces = plane_pieces(after(out_weight, *upstream_pieces[1:]))
    cosine, sine = rotary_tables(span)

    mask_plane = jnp.concatenate(
        [lax.dynamic_slice(p, (0, half + plane * members), (own_rows, members)) for p in upstream_pieces], axis=0)
    triangle = (jnp.arange(column)[:, None] >= jnp.arange(column)[None, :]).astype(BF16)
    rank = jnp.where(mask_plane > 0, mm(triangle, mask_plane) - 1.0, -1.0).astype(jnp.int32)
    pick = (rank.T[:, None, :] == jnp.arange(slots, dtype=jnp.int32)[None, :, None])
    pick = pick.reshape(members * slots, column).astype(BF16)
    unpick = rank[:, :, None] == jnp.arange(slots, dtype=jnp.int32)[None, None, :]
    unpick = unpick.reshape(column, members * slots).astype(BF16)
    upstream_sent = dispatch(pick, upstream_pieces)
    upstream_a = exchange(upstream_sent, "expert")

    qraw, kraw, query_low, key_low, value_low = project(
        after(normed, cosine, sine, router_rows), qkv_pieces, cosine, sine, query_gain, key_norm_gain)
    attended_low, inverse = attend(prefix_len, query_low, key_low, value_low)
    attended_all = gather(attended_low, "expert").reshape(members, span, width)

    upstream_pieces = plane_pieces(after(jnp.concatenate([cotangent[:, half:], router_rows], axis=0), *out_pieces[1:]))

    out_rows = out_project(
        plane.astype(jnp.int32).reshape(1),
        after(attended_all, upstream_a, upstream_pieces[1], upstream_pieces[-1]), out_pieces)
    projected = exchange(after(out_rows, *upstream_pieces[2:-1]), "expert").reshape(members, own_rows, out_piece)
    projected = jnp.transpose(projected, (1, 0, 2)).reshape(own_rows, model)

    upstream_sent = dispatch(after(pick, out_rows), upstream_pieces)
    upstream_b = exchange(upstream_sent, "expert")
    pick = after(pick, upstream_sent)
    router = jnp.concatenate([p[own_rows:].reshape(experts, part_rows) for p in upstream_pieces], axis=1)
    router = jnp.pad(reorder(router, 1), ((0, padded - experts), (0, 0)))

    after_attn = residual_in + projected.astype(F32)
    scale_mixture = row_scale(after_attn)
    mixed_low = (after_attn * scale_mixture * mixture_gain).astype(BF16)
    arrived = []
    for columns in (slice(0, half), slice(half, model)):
        sent = dispatch(pick, plane_pieces(mixed_low[:, columns]))
        arrived.append(exchange(after(sent, upstream_b), "expert"))

    out_columns = reorder(jnp.concatenate(after(out_pieces, arrived[0]), axis=0), 0)
    out_heads = exchange(after(out_columns, arrived[1]).reshape(members, width, out_piece), "expert")
    upstream_down = down_back(upstream_a, upstream_b, down)
    own_expert = (plane * members + member).astype(jnp.int32).reshape(1)
    activated, gate_grad, up_grad, weight_wide, route_columns = expert_forward(
        experts, own_expert, arrived[0], arrived[1], upstream_a, router, gate, up, upstream_down)
    back_first = exchange(row_gradient(gate_grad, up_grad, gate, up, 0, first), "expert")
    back_second = exchange(row_gradient(gate_grad, up_grad, gate, up, first, model, route_columns), "expert")
    produced = produce(activated, weight_wide, down, first)
    back_first = after(back_first, out_heads, *produced)
    mixed_first = plane_sum_direct(combine(unpick, back_first, planes, 40))
    mixed_second = plane_sum_direct(combine(unpick, back_second, planes, 40))
    mixture_rows = exchange(after(produced[0], back_second), "expert")

    upstream = cotangent.astype(F32)
    mask = mask_own > 0
    logits = jnp.where(mask, mm_t(mixed_low, router[:experts]), VERY_NEGATIVE)
    raised = jnp.where(mask, jnp.exp(logits - jnp.max(logits, axis=-1, keepdims=True)), 0.0)
    weight_own = raised / jnp.sum(raised, axis=-1, keepdims=True)
    route_back = mixed_second[:, rest:rest + experts] + mixed_second[:, rest + experts:rest + 2 * experts]
    chosen_grad = weight_own * (route_back - jnp.sum(weight_own * route_back, axis=-1, keepdims=True))
    logit_grad = chosen_grad.astype(BF16)
    mixed_first = after(mixed_first, mixture_rows)
    mixed_grad = mm(logit_grad, router[:experts]) + jnp.concatenate([mixed_first, mixed_second[:, :rest]], axis=1)
    mixture_back, mixture_terms = normalize_back(mixed_grad, after_attn, scale_mixture, mixture_gain)
    after_grad = upstream + mixture_back
    after_low = after_grad.astype(BF16)

    router_part = t_mm(logit_grad, mixed_low).astype(BF16).reshape(members, planes, model)
    router_part = jnp.pad(router_part, ((0, 0), (0, 8 - planes), (0, 0)))
    mixture_part = jnp.sum(mixture_terms, axis=0, keepdims=True)

    after_all = gather(after_low, "expert")
    mixture_parts = combine(unpick, after(mixture_rows, after_low), planes)
    mixture_first = plane_sum(mixture_parts)
    gate_gradient, up_gradient = hidden_gradient(
        arrived[0], arrived[1], *after((gate_grad, up_grad), after_low, *mixture_parts))
    after_all = after(after_all, gate_gradient, router_part, mixture_part, mixture_first)
    mixture_rows = exchange(after(produced[1], gate_gradient), "expert")
    out_partial = out_gradient(member.astype(jnp.int32).reshape(1), attended_all, after_all, out_piece)
    out_share = lax.psum_scatter(
        after(out_partial, mixture_first).reshape(members * width, out_piece), "dp", scatter_dimension=0, tiled=True).astype(F32)
    attended_grad = out_back(after(after_all, out_partial), out_heads)
    dq, dk, dv, query_terms, key_terms = attend_back(
        prefix_len, query_low, key_low, value_low, attended_low, inverse, attended_grad, qraw, kraw, cosine, sine,
        query_gain, key_norm_gain)
    normed_partial = unproject(
        own_rows, dq, dk, dv, qkv_pieces, normed, reorder(attention_gain, 0), router_part, mixture_part,
        query_terms, key_terms)
    query_partial = t_mm(normed, dq).astype(BF16)
    mixture_parts = combine(unpick, after(mixture_rows, normed_partial), planes)
    mixture_second = plane_sum(mixture_parts)
    arrived_sums = exchange(after(normed_partial, out_share, query_partial, *mixture_parts), "expert")
    normed_sums = jnp.sum(arrived_sums.astype(F32), axis=0)
    input_back, _ = normalize_back(
        reorder(normed_sums[:own_rows], 1), residual_in, scale_attention, attention_gain)
    input_grad = after_grad + input_back
    layer_out = (after_attn + jnp.concatenate([mixture_first, mixture_second], axis=1)).astype(BF16)

    kv_partial = jnp.concatenate([t_mm(normed, dk), t_mm(normed, dv)], axis=1)

    def kv_cols(j):
        start = j * piece
        return jnp.concatenate(
            [lax.dynamic_slice(kv_partial, (0, start), (model, piece)),
             lax.dynamic_slice(kv_partial, (0, HEAD_SIZE + start), (model, piece))], axis=1)

    kv_total = kv_cols(place)
    for shift in range(1, group):
        pairs = [(e, e - e % group + (e % group + shift) % group) for e in range(members)]
        kv_total += lax.ppermute(kv_cols((place + shift) % group).astype(BF16), "expert", pairs).astype(F32)
    kv_share = plane_sum(cut(kv_total.astype(BF16)))
    down_grad = down_gradient(upstream_a, upstream_b, weight_wide, after(activated, normed_partial))
    query_share = plane_sum(cut(after(query_partial, mixture_second, kv_share)), [down_grad], [normed_sums])
    key_share = kv_share[:, :piece]
    value_share = kv_share[:, piece:]

    last = normed_sums[own_rows:]
    attention_sum, mixture_sum, head_sum = (last[8 + 2 * n] + last[9 + 2 * n] for n in range(3))
    gains = jnp.concatenate([reorder(attention_sum, 0), mixture_sum, head_sum[:2 * HEAD_SIZE]])
    total = jnp.concatenate([gains, last[:planes].reshape(-1)]).reshape(-1, HEAD_SIZE)
    step = 1
    while step < planes:
        total = total + lax.ppermute(total, "dp", [(i, i ^ step) for i in range(planes)])
        step *= 2
    total = total.reshape(-1)
    gains, router_total = total[:gains.shape[0]], total[gains.shape[0]:].reshape(planes, model)
    router_share = lax.dynamic_slice(router_total, (0, plane * part_rows), (planes, part_rows)).T
    attention_total, mixture_total = gains[:model], gains[model:2 * model]
    query_total, key_total = gains[2 * model:2 * model + HEAD_SIZE], gains[2 * model + HEAD_SIZE:]
    return (
        layer_out,
        input_grad,
        query_share,
        key_share,
        value_share,
        out_share,
        router_share,
        attention_total,
        mixture_total,
        query_total,
        key_total,
        gate_gradient,
        up_gradient,
        down_grad,
    )


def solution(mesh):
    rows = P(("dp", "expert"), None)
    grid = P("dp", "expert")
    experts = P(("dp", "expert"), None, None)
    in_specs = (rows, rows, P("dp"), grid, grid, grid, grid, grid, P(), P(), P(), P(), experts, experts, experts, rows)
    out_specs = (rows, rows, grid, grid, grid, grid, grid, P(), P(), P(), P(), experts, experts, experts)
    return jax.shard_map(shards, mesh=mesh, in_specs=in_specs, out_specs=out_specs, check_vma=False)
```

```python
import functools
import math

import jax
import jax.numpy as jnp
from jax import lax
from jax.experimental import pallas as pl
from jax.experimental.pallas import tpu as pltpu
from jax.sharding import PartitionSpec as P

QUERY_HEADS = 32
KEY_VALUE_HEADS = 4
HEAD_SIZE = 128
TOP = 8
EPS = 1e-06
ROTARY_BASE = 1000000.0
VERY_NEGATIVE = -1e30
SOFTMAX_SCALE = HEAD_SIZE ** (-0.5)
LOG2_SCALE = SOFTMAX_SCALE * math.log2(math.e)
VMEM_BYTES = 24 * 1024 * 1024
F32 = jnp.float32
BF16 = jnp.bfloat16


def cost(microseconds):
    return pl.CostEstimate(flops=int(microseconds * 1.1e9) + 1, bytes_accessed=1, transcendentals=0)


def mm(a, b):
    return lax.dot_general(a, b, (((1,), (0,)), ((), ())), preferred_element_type=F32)


def mm_t(a, b):
    return lax.dot_general(a, b, (((1,), (1,)), ((), ())), preferred_element_type=F32)


def t_mm(a, b):
    return lax.dot_general(a, b, (((0,), (0,)), ((), ())), preferred_element_type=F32)


def row_scale(source):
    return lax.rsqrt(jnp.mean(source * source, axis=-1, keepdims=True) + EPS)


def normalize_back(upstream, source, scaling, gain_row):
    unit_rows = source * scaling
    weighted = upstream * gain_row
    inner_mean = jnp.mean(weighted * unit_rows, axis=-1, keepdims=True)
    return (scaling * (weighted - unit_rows * inner_mean), upstream * unit_rows)


def rotary_tables(span):
    half = HEAD_SIZE // 2
    frequency = jnp.power(ROTARY_BASE, -jnp.arange(half, dtype=F32) * 2.0 / HEAD_SIZE)
    angles = jnp.arange(span, dtype=jnp.int32).astype(F32)[:, None] * frequency[None, :]
    cosine, sine = jnp.cos(angles), jnp.sin(angles)
    return (
        jnp.concatenate([cosine, cosine], axis=-1),
        jnp.concatenate([-sine, sine], axis=-1),
    )


def turned(u, gain, cosine, sine):
    n = u * row_scale(u) * gain
    return (n * cosine + pltpu.roll(n, HEAD_SIZE // 2, 1) * sine).astype(BF16)


def pieces_product(x, refs):
    size = refs[0].shape[0]
    total = mm(x[:, :size], refs[0][...])
    for s in range(1, len(refs)):
        total += mm(x[:, s * size:(s + 1) * size], refs[s][...])
    return total


def project_kernel(x_ref, cos_ref, sin_ref, qg_ref, kg_ref, *refs):
    weights, (qraw_ref, kraw_ref, q_ref, k_ref, v_ref) = refs[:-5], refs[-5:]
    total = pieces_product(x_ref[...], weights)
    width = q_ref.shape[1]
    cosine, sine = cos_ref[...], sin_ref[...]
    qraw_ref[...] = total[:, :width]
    for h in range(width // HEAD_SIZE):
        cols = slice(h * HEAD_SIZE, (h + 1) * HEAD_SIZE)
        q_ref[:, cols] = turned(total[:, cols], qg_ref[...], cosine, sine)
    key = total[:, width:width + HEAD_SIZE]
    kraw_ref[...] = key
    k_ref[...] = turned(key, kg_ref[...], cosine, sine)
    v_ref[...] = total[:, width + HEAD_SIZE:].astype(BF16)


def project(x, weights, cosine, sine, q_gain, k_gain):
    span, model = x.shape
    width = weights[0].shape[1] - 2 * HEAD_SIZE
    tile = 256
    row = lambda w: pl.BlockSpec((tile, w), lambda i: (i, 0))
    whole = lambda a, b: pl.BlockSpec((a, b), lambda i: (0, 0))
    out = [(width, F32), (HEAD_SIZE, F32), (width, BF16), (HEAD_SIZE, BF16), (HEAD_SIZE, BF16)]
    return pl.pallas_call(
        project_kernel,
        grid=(span // tile,),
        in_specs=[row(model), row(HEAD_SIZE), row(HEAD_SIZE), whole(1, HEAD_SIZE), whole(1, HEAD_SIZE)]
        + [whole(*w.shape) for w in weights],
        out_specs=[row(w) for w, _ in out],
        out_shape=[jax.ShapeDtypeStruct((span, w), t) for w, t in out],
        compiler_params=pltpu.CompilerParams(vmem_limit_bytes=VMEM_BYTES),
        cost_estimate=cost(0),
        name="project",
    )(x, cosine, sine, q_gain[None], k_gain[None], *weights)


def block_limits(span, tile):
    return [(r0, max(r0 + tile, span // 2)) for r0 in range(0, span, tile)]


def masked(values, r0, limit, prefix):
    tile = values.shape[0]
    rows = r0 + lax.broadcasted_iota(jnp.int32, (tile, limit - r0), 0)
    cols = r0 + lax.broadcasted_iota(jnp.int32, (tile, limit - r0), 1)
    right = jnp.where((cols <= rows) | (cols < prefix), values[:, r0:], 0.0)
    return right if r0 == 0 else jnp.concatenate([values[:, :r0], right], axis=1)


def attend_kernel(tile, prefix_ref, q_ref, k_ref, v_ref, o_ref, l_ref, wide_ref):
    span = q_ref.shape[0]

    @pl.when(pl.program_id(0) == 0)
    def _():
        wide_ref[:, :HEAD_SIZE] = v_ref[...]
        wide_ref[:, HEAD_SIZE:] = jnp.ones((span, HEAD_SIZE), BF16)

    prefix = prefix_ref[0]
    for r0, limit in block_limits(span, tile):
        rows = slice(r0, r0 + tile)
        scores = mm_t(q_ref[rows, :], k_ref[:limit, :])
        weights = masked(jnp.exp2(scores * LOG2_SCALE), r0, limit, prefix)
        sums = mm(weights.astype(BF16), wide_ref[:limit, :])
        inverse = 1.0 / sums[:, HEAD_SIZE:]
        o_ref[rows, :] = (sums[:, :HEAD_SIZE] * inverse).astype(BF16)
        l_ref[rows, :] = inverse


def attend(prefix, q, k, v):
    span, width = q.shape
    heads = width // HEAD_SIZE
    head = pl.BlockSpec((span, HEAD_SIZE), lambda h: (0, h))
    shared = pl.BlockSpec((span, HEAD_SIZE), lambda h: (0, 0))
    return pl.pallas_call(
        functools.partial(attend_kernel, 256),
        grid=(heads,),
        in_specs=[pl.BlockSpec(memory_space=pltpu.SMEM), head, shared, shared],
        out_specs=[head, head],
        out_shape=[jax.ShapeDtypeStruct((span, width), BF16), jax.ShapeDtypeStruct((span, width), F32)],
        scratch_shapes=[pltpu.VMEM((span, 2 * HEAD_SIZE), BF16)],
        compiler_params=pltpu.CompilerParams(vmem_limit_bytes=VMEM_BYTES),
        cost_estimate=cost(0),
        name="attend",
    )(prefix, q, k, v)


def attend_back_kernel(tile, prefix_ref, q_ref, k_ref, v_ref, o_ref, l_ref, do_ref, qraw_ref, kraw_ref, cos_ref, sin_ref,
                       qg_ref, kg_ref, dq_ref, dk_ref, dv_ref, qgg_ref, kgg_ref, dk_sum, dv_sum):
    span = q_ref.shape[0]
    step = pl.program_id(0)

    @pl.when(step == 0)
    def _():
        dk_sum[...] = jnp.zeros_like(dk_sum)
        dv_sum[...] = jnp.zeros_like(dv_sum)
        qgg_ref[...] = jnp.zeros_like(qgg_ref)

    def unturned(grad, rows):
        return grad * cos_ref[rows, :] - pltpu.roll(grad, HEAD_SIZE // 2, 1) * sin_ref[rows, :]

    prefix = prefix_ref[0]
    for r0, limit in block_limits(span, tile):
        rows = slice(r0, r0 + tile)
        q, do = q_ref[rows, :], do_ref[rows, :]
        keys, values = k_ref[:limit, :], v_ref[:limit, :]
        weights = masked(jnp.exp2(mm_t(q, keys) * LOG2_SCALE), r0, limit, prefix)
        probs = weights * jnp.concatenate([l_ref[rows, :]] * (limit // HEAD_SIZE), axis=1)
        delta = jnp.sum(do.astype(F32) * o_ref[rows, :].astype(F32), axis=1, keepdims=True)
        score_grad = (probs * (mm_t(do, values) - delta)).astype(BF16)
        dv_sum[:limit, :] += t_mm(probs.astype(BF16), do)
        dk_sum[:limit, :] += t_mm(score_grad, q)
        turn = unturned(mm(score_grad, keys) * SOFTMAX_SCALE, rows)
        raw = qraw_ref[rows, :]
        back, terms = normalize_back(turn, raw, row_scale(raw), qg_ref[...])
        dq_ref[rows, :] = back.astype(BF16)
        qgg_ref[...] += jnp.sum(terms, axis=0, keepdims=True)

    @pl.when(step == pl.num_programs(0) - 1)
    def _():
        raw = kraw_ref[...]
        turn = unturned(dk_sum[...] * SOFTMAX_SCALE, slice(None))
        back, terms = normalize_back(turn, raw, row_scale(raw), kg_ref[...])
        dk_ref[...] = back.astype(BF16)
        dv_ref[...] = dv_sum[...].astype(BF16)
        kgg_ref[...] = jnp.sum(terms, axis=0, keepdims=True)


def attend_back(prefix, q, k, v, o, inverse, do, qraw, kraw, cosine, sine, q_gain, k_gain):
    span, width = q.shape
    heads = width // HEAD_SIZE
    head = pl.BlockSpec((span, HEAD_SIZE), lambda h: (0, h))
    shared = pl.BlockSpec((span, HEAD_SIZE), lambda h: (0, 0))
    gain = pl.BlockSpec((1, HEAD_SIZE), lambda h: (0, 0))
    return pl.pallas_call(
        functools.partial(attend_back_kernel, 256),
        grid=(heads,),
        in_specs=[pl.BlockSpec(memory_space=pltpu.SMEM), head, shared, shared, head, head, head, head, shared, shared,
                  shared, gain, gain],
        out_specs=[head, shared, shared, gain, gain],
        out_shape=[
            jax.ShapeDtypeStruct((span, width), BF16),
            jax.ShapeDtypeStruct((span, HEAD_SIZE), BF16),
            jax.ShapeDtypeStruct((span, HEAD_SIZE), BF16),
            jax.ShapeDtypeStruct((1, HEAD_SIZE), F32),
            jax.ShapeDtypeStruct((1, HEAD_SIZE), F32),
        ],
        scratch_shapes=[pltpu.VMEM((span, HEAD_SIZE), F32), pltpu.VMEM((span, HEAD_SIZE), F32)],
        compiler_params=pltpu.CompilerParams(vmem_limit_bytes=VMEM_BYTES),
        cost_estimate=cost(0),
        name="attend_back",
    )(prefix, q, k, v, o, inverse, do, qraw, kraw, cosine, sine, q_gain[None], k_gain[None])


def unproject_kernel(own_rows, dq_ref, dk_ref, dv_ref, x_ref, gain_ref, router_ref, mix_ref, qg_ref, kg_ref,
                     *refs):
    weights, out_ref, sum_ref = refs[:-2], refs[-2], refs[-1]
    span, model = x_ref.shape
    size = weights[0].shape[0]
    tile = 512
    each = tile // own_rows
    for r in range(span // tile):
        rows = slice(r * tile, (r + 1) * tile)
        grads = jnp.concatenate([dq_ref[rows, :], dk_ref[rows, :], dv_ref[rows, :]], axis=1)
        for s, weight in enumerate(weights):
            cols = slice(s * size, (s + 1) * size)
            total = mm_t(grads, weight[...])
            low = total.astype(BF16)
            for m in range(each):
                out_ref[r * each + m, :own_rows, cols] = low[m * own_rows:(m + 1) * own_rows]
            part = jnp.sum(total * x_ref[rows, cols].astype(F32), axis=0, keepdims=True)
            if r == 0:
                sum_ref[:, cols] = part
            else:
                sum_ref[:, cols] += part
    heads = jnp.concatenate([qg_ref[...], kg_ref[...], jnp.zeros((1, model - 2 * HEAD_SIZE), F32)], axis=1)
    place = lax.broadcasted_iota(jnp.int32, (8, model), 0)
    sums = jnp.zeros((8, model), F32)
    for n, values in enumerate((sum_ref[...] / gain_ref[...], mix_ref[...], heads)):
        high = values.astype(BF16).astype(F32)
        sums = jnp.where(place == 2 * n, high, jnp.where(place == 2 * n + 1, values - high, sums))
    sums = sums.astype(BF16)
    for m in range(out_ref.shape[0]):
        out_ref[m, own_rows:own_rows + 8, :] = router_ref[m]
        out_ref[m, own_rows + 8:, :] = sums


def unproject(own_rows, dq, dk, dv, pieces, x, gain, router_part, mixture_part, query_part, key_part):
    span, model = x.shape
    return pl.pallas_call(
        functools.partial(unproject_kernel, own_rows),
        out_shape=jax.ShapeDtypeStruct((span // own_rows, own_rows + 16, model), BF16),
        scratch_shapes=[pltpu.VMEM((1, model), F32)],
        compiler_params=pltpu.CompilerParams(vmem_limit_bytes=44 * 1024 * 1024),
        cost_estimate=cost(0),
        name="unproject",
    )(dq, dk, dv, x, gain[None], router_part, mixture_part, query_part, key_part, *pieces)


def out_project_kernel(plane_ref, a_ref, *refs):
    out_ref = refs[-1]
    pieces = refs[:-1]
    members, _, width = a_ref.shape
    planes, each = len(pieces), members // len(pieces)
    total = None
    for s, piece in enumerate(pieces):
        block = lax.rem(plane_ref[0] + planes - s, planes) * each
        for i in range(each):
            part = mm(a_ref[block + i], piece[i * width:(i + 1) * width, :])
            total = part if total is None else total + part
    out_ref[...] = total.astype(BF16)


def out_project(plane, attended_all, pieces):
    members, span, width = attended_all.shape
    size, columns = pieces[0].shape
    tile = 256
    return pl.pallas_call(
        out_project_kernel,
        grid=(span // tile,),
        in_specs=[pl.BlockSpec(memory_space=pltpu.SMEM), pl.BlockSpec((members, tile, width), lambda i: (0, i, 0))]
        + [pl.BlockSpec((size, columns), lambda i: (0, 0))] * len(pieces),
        out_specs=pl.BlockSpec((tile, columns), lambda i: (i, 0)),
        out_shape=jax.ShapeDtypeStruct((span, columns), BF16),
        compiler_params=pltpu.CompilerParams(vmem_limit_bytes=VMEM_BYTES),
        cost_estimate=cost(0),
        name="out_project",
    )(plane, attended_all, *pieces)


def out_back_kernel(g_ref, w_ref, out_ref):
    columns = w_ref.shape[2]
    total = mm_t(g_ref[:, :columns], w_ref[0])
    for m in range(1, w_ref.shape[0]):
        total += mm_t(g_ref[:, m * columns:(m + 1) * columns], w_ref[m])
    out_ref[...] = total.astype(BF16)


def out_back(after_all, heads):
    span, model = after_all.shape
    members, width, columns = heads.shape
    tile = 512
    return pl.pallas_call(
        out_back_kernel,
        grid=(span // tile,),
        in_specs=[pl.BlockSpec((tile, model), lambda i: (i, 0)),
                  pl.BlockSpec((members, width, columns), lambda i: (0, 0, 0))],
        out_specs=pl.BlockSpec((tile, width), lambda i: (i, 0)),
        out_shape=jax.ShapeDtypeStruct((span, width), BF16),
        compiler_params=pltpu.CompilerParams(vmem_limit_bytes=56 * 1024 * 1024),
        cost_estimate=cost(0),
        name="out_back",
    )(after_all, heads)


def out_gradient_kernel(member_ref, a_ref, g_ref, out_ref):
    out_ref[0] = t_mm(a_ref[0], g_ref[...]).astype(BF16)


def out_gradient(member, attended_all, after_all, columns):
    members, span, width = attended_all.shape
    return pl.pallas_call(
        out_gradient_kernel,
        grid_spec=pltpu.PrefetchScalarGridSpec(
            num_scalar_prefetch=1,
            grid=(members,),
            in_specs=[pl.BlockSpec((1, span, width), lambda m, me: (m, 0, 0)),
                      pl.BlockSpec((span, columns), lambda m, me: (0, me[0]))],
            out_specs=pl.BlockSpec((1, width, columns), lambda m, me: (m, 0, 0)),
        ),
        out_shape=jax.ShapeDtypeStruct((members, width, columns), BF16),
        compiler_params=pltpu.CompilerParams(vmem_limit_bytes=56 * 1024 * 1024),
        cost_estimate=cost(0),
        name="out_gradient",
    )(member, attended_all, after_all)


def expert_kernel(experts, own_ref, xa_ref, xb_ref, mask_ref, router_ref, gate_ref, up_ref, down_ref,
                  act_ref, gg_ref, ug_ref, w_ref, route_ref):
    half = xa_ref.shape[1]
    own = own_ref[0]
    xa, xb = xa_ref[...], xb_ref[...]

    def product(weight):
        return mm(xa, weight[:half, :]) + mm(xb, weight[half:, :])

    gate_raw, up_raw = product(gate_ref), product(up_ref)
    mask = mask_ref[...].astype(F32)
    logits = mm_t(xa, router_ref[:, :half]) + mm_t(xb, router_ref[:, half:])
    logits = jnp.where(mask > 0, logits, VERY_NEGATIVE)
    raised = jnp.where(mask > 0, jnp.exp(logits - jnp.max(logits, axis=-1, keepdims=True)), 0.0)
    total = jnp.maximum(jnp.sum(raised, axis=-1, keepdims=True), 1e-30)
    lanes = lax.broadcasted_iota(jnp.int32, raised.shape, 1)
    weight = jnp.sum(jnp.where(lanes == own, raised, 0.0), axis=-1, keepdims=True) / total
    w_ref[...] = jnp.broadcast_to(weight, w_ref.shape)

    sig = 1.0 / (1.0 + jnp.exp(-gate_raw))
    silu = gate_raw * sig
    activated = (silu * up_raw).astype(BF16)
    act_ref[...] = activated
    down = down_ref[...]
    route = jnp.sum(activated.astype(F32) * down, axis=-1, keepdims=True)
    grad = weight * down
    gg_ref[...] = (grad * up_raw * sig * (1.0 + gate_raw * (1.0 - sig))).astype(BF16)
    ug_ref[...] = (grad * silu).astype(BF16)
    high = route.astype(BF16).astype(F32)
    lanes = lax.broadcasted_iota(jnp.int32, route_ref.shape, 1)
    route_ref[...] = jnp.where(
        lanes == own, high, jnp.where(lanes == experts + own, route - high, 0.0)).astype(BF16)


def expert_forward(experts, own, xa, xb, masked_rows, router, gate, up, upstream_down):
    rows, half = xa.shape
    model, hidden = gate.shape
    padded = router.shape[0]
    route_width = -(-2 * experts // HEAD_SIZE) * HEAD_SIZE
    tile = rows // 4
    row = lambda w: pl.BlockSpec((tile, w), lambda i: (i, 0))
    whole = lambda a, b: pl.BlockSpec((a, b), lambda i: (0, 0))
    out = [(hidden, BF16), (hidden, BF16), (hidden, BF16), (HEAD_SIZE, F32), (route_width, BF16)]
    return pl.pallas_call(
        functools.partial(expert_kernel, experts),
        grid=(rows // tile,),
        in_specs=[pl.BlockSpec(memory_space=pltpu.SMEM), row(half), row(half),
                  pl.BlockSpec((tile, padded), lambda i: (i, half // padded)), whole(padded, model),
                  whole(model, hidden), whole(model, hidden), row(hidden)],
        out_specs=[row(w) for w, _ in out],
        out_shape=[jax.ShapeDtypeStruct((rows, w), t) for w, t in out],
        compiler_params=pltpu.CompilerParams(vmem_limit_bytes=32 * 1024 * 1024),
        cost_estimate=cost(18),
        name="expert_forward",
    )(own, xa, xb, masked_rows, router, gate, up, upstream_down)


def row_gradient_kernel(start, stop, gg_ref, ug_ref, gate_ref, up_ref, *rest):
    part = slice(start, stop)
    total = (mm_t(gg_ref[...], gate_ref[part, :]) + mm_t(ug_ref[...], up_ref[part, :])).astype(BF16)
    out_ref = rest[-1]
    out_ref[:, :total.shape[1]] = total
    if len(rest) == 2:
        out_ref[:, total.shape[1]:] = rest[0][...]


def row_gradient(gg, ug, gate, up, start, stop, route=None):
    rows, hidden = gg.shape
    tile = rows // 4
    row = lambda w: pl.BlockSpec((tile, w), lambda i: (i, 0))
    weight = pl.BlockSpec(gate.shape, lambda i: (0, 0))
    extra = [] if route is None else [route]
    width = stop - start + sum(e.shape[1] for e in extra)
    return pl.pallas_call(
        functools.partial(row_gradient_kernel, start, stop),
        grid=(rows // tile,),
        in_specs=[row(hidden), row(hidden), weight, weight] + [row(e.shape[1]) for e in extra],
        out_specs=row(width),
        out_shape=jax.ShapeDtypeStruct((rows, width), BF16),
        compiler_params=pltpu.CompilerParams(vmem_limit_bytes=VMEM_BYTES),
        cost_estimate=cost(8),
        name="row_gradient",
    )(gg, ug, gate, up, *extra)


def down_back_kernel(ca_ref, cb_ref, down_ref, out_ref):
    half = cb_ref.shape[1]
    out_ref[...] = mm_t(ca_ref[...], down_ref[:, :half]) + mm_t(cb_ref[...], down_ref[:, half:])


def down_back(ca, cb, down):
    rows, half = cb.shape
    hidden, model = down.shape
    tile = 256
    whole = pl.BlockSpec((rows, half), lambda i: (0, 0))
    return pl.pallas_call(
        down_back_kernel,
        grid=(hidden // tile,),
        in_specs=[whole, whole, pl.BlockSpec((tile, model), lambda i: (i, 0))],
        out_specs=pl.BlockSpec((rows, tile), lambda i: (0, i)),
        out_shape=jax.ShapeDtypeStruct((rows, hidden), F32),
        compiler_params=pltpu.CompilerParams(vmem_limit_bytes=VMEM_BYTES),
        cost_estimate=cost(0),
        name="down_back",
    )(ca, cb, down)


def produce_kernel(act_ref, w_ref, down_ref, *outs):
    total = (w_ref[:, :1] * mm(act_ref[...], down_ref[...])).astype(BF16)
    first = outs[0].shape[1]
    outs[0][...] = total[:, :first]
    outs[1][...] = total[:, first:]


def produce(activated, weight, down, first):
    rows, hidden = activated.shape
    model = down.shape[1]
    tile = rows // 4
    row = lambda w: pl.BlockSpec((tile, w), lambda i: (i, 0))
    return pl.pallas_call(
        produce_kernel,
        grid=(rows // tile,),
        in_specs=[row(hidden), row(HEAD_SIZE), pl.BlockSpec((hidden, model), lambda i: (0, 0))],
        out_specs=[row(first), row(model - first)],
        out_shape=[jax.ShapeDtypeStruct((rows, w), BF16) for w in (first, model - first)],
        compiler_params=pltpu.CompilerParams(vmem_limit_bytes=VMEM_BYTES),
        cost_estimate=cost(0),
        name="produce",
    )(activated, weight, down)


def hidden_gradient_kernel(xa_ref, xb_ref, gg_ref, ug_ref, dg_ref, du_ref):
    in_first = pl.program_id(0) < pl.num_programs(0) // 2
    for x_ref, now in ((xa_ref, in_first), (xb_ref, jnp.logical_not(in_first))):
        @pl.when(now)
        def _():
            dg_ref[0] = t_mm(x_ref[...], gg_ref[...])
            du_ref[0] = t_mm(x_ref[...], ug_ref[...])


def hidden_gradient(xa, xb, gg, ug):
    rows, half = xa.shape
    hidden = gg.shape[1]
    tile = 256
    count = half // tile
    whole = pl.BlockSpec((rows, hidden), lambda i: (0, 0))
    out = pl.BlockSpec((1, tile, hidden), lambda i: (0, i, 0))
    return pl.pallas_call(
        hidden_gradient_kernel,
        grid=(2 * count,),
        in_specs=[pl.BlockSpec((rows, tile), lambda i: (0, jnp.minimum(i, count - 1))),
                  pl.BlockSpec((rows, tile), lambda i: (0, jnp.maximum(i - count, 0))), whole, whole],
        out_specs=[out, out],
        out_shape=[jax.ShapeDtypeStruct((1, 2 * half, hidden), F32)] * 2,
        compiler_params=pltpu.CompilerParams(vmem_limit_bytes=VMEM_BYTES),
        cost_estimate=cost(0),
        name="hidden_gradient",
    )(xa, xb, gg, ug)


def down_gradient_kernel(ca_ref, cb_ref, w_ref, act_ref, out_ref):
    in_first = pl.program_id(0) < pl.num_programs(0) // 2
    for c_ref, now in ((ca_ref, in_first), (cb_ref, jnp.logical_not(in_first))):
        @pl.when(now)
        def _():
            out_ref[0] = t_mm(act_ref[...], (w_ref[:, :1] * c_ref[...].astype(F32)).astype(BF16))


def down_gradient(ca, cb, weight, activated):
    rows, half = cb.shape
    hidden = activated.shape[1]
    tile = 256
    count = half // tile
    return pl.pallas_call(
        down_gradient_kernel,
        grid=(2 * count,),
        in_specs=[pl.BlockSpec((rows, tile), lambda i: (0, jnp.minimum(i, count - 1))),
                  pl.BlockSpec((rows, tile), lambda i: (0, jnp.maximum(i - count, 0))),
                  pl.BlockSpec((rows, HEAD_SIZE), lambda i: (0, 0)), pl.BlockSpec((rows, hidden), lambda i: (0, 0))],
        out_specs=pl.BlockSpec((1, hidden, tile), lambda i: (0, 0, i)),
        out_shape=jax.ShapeDtypeStruct((1, hidden, 2 * half), F32),
        compiler_params=pltpu.CompilerParams(vmem_limit_bytes=VMEM_BYTES),
        cost_estimate=cost(0),
        name="down_gradient",
    )(ca, cb, weight, activated)


def dispatch_kernel(pick_ref, *refs):
    out_ref, all_ref = refs[-2:]
    size = all_ref.shape[0] // (len(refs) - 2)

    @pl.when(pl.program_id(0) == 0)
    def _():
        for s, ref in enumerate(refs[:-2]):
            all_ref[s * size:(s + 1) * size, :] = ref[...]

    out_ref[...] = mm(pick_ref[...], all_ref[...]).astype(BF16)


def dispatch(pick, pieces):
    rows, column = pick.shape
    size, width = column // len(pieces), pieces[0].shape[1]
    tile = rows // 4
    return pl.pallas_call(
        dispatch_kernel,
        grid=(rows // tile,),
        in_specs=[pl.BlockSpec((tile, column), lambda i: (i, 0))]
        + [pl.BlockSpec((size, width), lambda i: (0, 0))] * len(pieces),
        out_specs=pl.BlockSpec((tile, width), lambda i: (i, 0)),
        out_shape=jax.ShapeDtypeStruct((rows, width), BF16),
        scratch_shapes=[pltpu.VMEM((column, width), BF16)],
        compiler_params=pltpu.CompilerParams(vmem_limit_bytes=VMEM_BYTES),
        cost_estimate=cost(0),
        name="dispatch",
    )(pick, *pieces)


def combine_kernel(pick_ref, rows_ref, *outs):
    total = mm(pick_ref[...], rows_ref[...]).astype(BF16)
    size = total.shape[0] // len(outs)
    for s, out in enumerate(outs):
        out[...] = total[s * size:(s + 1) * size]


def combine(pick, rows, count, microseconds=0):
    column, slots = pick.shape
    width = rows.shape[1]
    tile = max(t for t in range(HEAD_SIZE, 513, HEAD_SIZE) if width % t == 0)
    size = column // count
    out = pl.BlockSpec((size, tile), lambda i: (0, i))
    return pl.pallas_call(
        combine_kernel,
        grid=(width // tile,),
        in_specs=[pl.BlockSpec((column, slots), lambda i: (0, 0)), pl.BlockSpec((slots, tile), lambda i: (0, i))],
        out_specs=[out] * count,
        out_shape=[jax.ShapeDtypeStruct((size, width), BF16)] * count,
        compiler_params=pltpu.CompilerParams(vmem_limit_bytes=VMEM_BYTES),
        cost_estimate=cost(microseconds),
        name="combine",
    )(pick, rows)


def after(array, *earlier):
    return lax.optimization_barrier((array, *earlier))[0]


def shards(
    tokens,
    routes,
    prefix_len,
    query_weight,
    key_matrix,
    value_matrix,
    out_weight,
    router_weight,
    attention_gain,
    mixture_gain,
    query_gain,
    key_norm_gain,
    expert_gate,
    expert_up,
    expert_down,
    cotangent,
):
    planes, members = lax.axis_size("dp"), lax.axis_size("expert")
    devices = planes * members
    plane, member = lax.axis_index("dp"), lax.axis_index("expert")
    own_rows, model = tokens.shape
    span = own_rows * members
    column = own_rows * planes
    experts = devices
    width = query_weight.shape[1]
    piece = key_matrix.shape[1]
    group = HEAD_SIZE // piece
    block_slots = max(2, 6 * own_rows * TOP // (5 * experts))
    slots = planes * block_slots
    padded = -(-experts // HEAD_SIZE) * HEAD_SIZE
    half = model // 2
    first = 5 * model // 8
    rest = model - first
    part_rows = model // planes
    gate, up, down = expert_gate[0], expert_up[0], expert_down[0]

    def gather(array, axis, dimension=0):
        return lax.all_gather(array, axis, axis=dimension, tiled=True)

    def exchange(array, axis):
        return lax.all_to_all(array, axis, split_axis=0, concat_axis=0, tiled=True)

    def plane_pieces(array):
        def shift(value, by):
            return lax.ppermute(value, "dp", [(i, (i + by) % planes) for i in range(planes)])

        pieces = [array] + [None] * (planes - 1)
        for s in range(1, planes // 2 + 1):
            pieces[s] = shift(pieces[s - 1], 1)
            if planes - s > s:
                pieces[planes - s] = shift(pieces[(planes - s + 1) % planes], -1)
        return pieces

    def plane_sum_direct(pieces):
        total = pieces[0].astype(F32)
        for s in range(1, planes):
            total += lax.ppermute(pieces[s], "dp", [(i, (i - s) % planes) for i in range(planes)]).astype(F32)
        return total

    def plane_sum(pieces, between=(), last=()):
        def shift(value, by):
            return lax.ppermute(value, "dp", [(i, (i + by) % planes) for i in range(planes)]).astype(F32)

        total = pieces[0].astype(F32)
        middle = planes // 2
        for order, by in ((range(middle, 0, -1), -1), (range(middle + 1, planes), 1)):
            running = None
            for s in order:
                if running is None:
                    running = pieces[s]
                else:
                    running = (after(shift(running, by), *between) + pieces[s].astype(F32)).astype(BF16)
            if running is not None:
                total += after(shift(running, by), *last)
        return total

    def reorder(array, dimension):
        size = array.shape[dimension] // planes
        return jnp.concatenate(
            [lax.dynamic_slice_in_dim(array, (plane - s) % planes * size, size, dimension) for s in range(planes)],
            axis=dimension)

    def cut(array):
        return [array[s * (array.shape[0] // planes):(s + 1) * (array.shape[0] // planes)] for s in range(planes)]

    residual_in = tokens.astype(F32)
    scale_attention = row_scale(residual_in)
    normed_own = (residual_in * scale_attention * attention_gain).astype(BF16)
    normed = gather(reorder(normed_own, 1), "expert")

    kv_own = jnp.concatenate([key_matrix, value_matrix], axis=1)
    place = member % group
    kv_parts = [kv_own]
    for shift in range(1, group):
        pairs = [(e - e % group + (e % group + shift) % group, e) for e in range(members)]
        kv_parts.append(lax.ppermute(kv_own, "expert", pairs))

    def kv_piece(j):
        value = kv_parts[0]
        for shift in range(1, group):
            value = jnp.where((place + shift) % group == j, kv_parts[shift], value)
        return value

    ordered = [kv_piece(j) for j in range(group)]
    qkv_part = jnp.concatenate(
        [query_weight] + [p[:, :piece] for p in ordered] + [p[:, piece:] for p in ordered], axis=1)

    expert_ids = jnp.arange(experts, dtype=jnp.int32)
    mask_own = jnp.sum((routes[:, :, None] == expert_ids[None, None, :]).astype(F32), axis=1)
    mask_wide = jnp.pad(mask_own, ((0, 0), (0, padded - experts))).astype(BF16)
    qkv_pieces = plane_pieces(qkv_part)
    upstream_pieces = plane_pieces(
        after(jnp.concatenate([cotangent[:, :half], mask_wide], axis=1), *qkv_pieces[1:]))
    router_rows = gather(after(router_weight.T, normed), "expert").reshape(2 * members, half)
    out_piece = out_weight.shape[1]
    out_pieces = plane_pieces(after(out_weight, *upstream_pieces[1:]))
    cosine, sine = rotary_tables(span)

    mask_plane = jnp.concatenate(
        [lax.dynamic_slice(p, (0, half + plane * members), (own_rows, members)) for p in upstream_pieces], axis=0)
    triangle = (jnp.arange(column)[:, None] >= jnp.arange(column)[None, :]).astype(BF16)
    rank = jnp.where(mask_plane > 0, mm(triangle, mask_plane) - 1.0, -1.0).astype(jnp.int32)
    pick = (rank.T[:, None, :] == jnp.arange(slots, dtype=jnp.int32)[None, :, None])
    pick = pick.reshape(members * slots, column).astype(BF16)
    unpick = rank[:, :, None] == jnp.arange(slots, dtype=jnp.int32)[None, None, :]
    unpick = unpick.reshape(column, members * slots).astype(BF16)
    upstream_sent = dispatch(pick, upstream_pieces)
    upstream_a = exchange(upstream_sent, "expert")

    qraw, kraw, query_low, key_low, value_low = project(
        after(normed, cosine, sine, router_rows), qkv_pieces, cosine, sine, query_gain, key_norm_gain)
    attended_low, inverse = attend(prefix_len, query_low, key_low, value_low)
    attended_all = gather(attended_low, "expert").reshape(members, span, width)

    upstream_pieces = plane_pieces(after(jnp.concatenate([cotangent[:, half:], router_rows], axis=0), *out_pieces[1:]))

    out_rows = out_project(
        plane.astype(jnp.int32).reshape(1),
        after(attended_all, upstream_a, upstream_pieces[1], upstream_pieces[-1]), out_pieces)
    projected = exchange(after(out_rows, *upstream_pieces[2:-1]), "expert").reshape(members, own_rows, out_piece)
    projected = jnp.transpose(projected, (1, 0, 2)).reshape(own_rows, model)

    upstream_sent = dispatch(after(pick, out_rows), upstream_pieces)
    upstream_b = exchange(upstream_sent, "expert")
    pick = after(pick, upstream_sent)
    router = jnp.concatenate([p[own_rows:].reshape(experts, part_rows) for p in upstream_pieces], axis=1)
    router = jnp.pad(reorder(router, 1), ((0, padded - experts), (0, 0)))

    after_attn = residual_in + projected.astype(F32)
    scale_mixture = row_scale(after_attn)
    mixed_low = (after_attn * scale_mixture * mixture_gain).astype(BF16)
    arrived = []
    for columns in (slice(0, half), slice(half, model)):
        sent = dispatch(pick, plane_pieces(mixed_low[:, columns]))
        arrived.append(exchange(after(sent, upstream_b), "expert"))

    out_columns = reorder(jnp.concatenate(after(out_pieces, arrived[0]), axis=0), 0)
    out_heads = exchange(after(out_columns, arrived[1]).reshape(members, width, out_piece), "expert")
    upstream_down = down_back(upstream_a, upstream_b, down)
    own_expert = (plane * members + member).astype(jnp.int32).reshape(1)
    activated, gate_grad, up_grad, weight_wide, route_columns = expert_forward(
        experts, own_expert, arrived[0], arrived[1], upstream_a, router, gate, up, upstream_down)
    back_first = exchange(row_gradient(gate_grad, up_grad, gate, up, 0, first), "expert")
    back_second = exchange(row_gradient(gate_grad, up_grad, gate, up, first, model, route_columns), "expert")
    produced = produce(activated, weight_wide, down, first)
    back_first = after(back_first, out_heads, *produced)
    mixed_first = plane_sum_direct(combine(unpick, back_first, planes, 40))
    mixed_second = plane_sum_direct(combine(unpick, back_second, planes, 40))
    mixture_rows = exchange(after(produced[0], back_second), "expert")

    upstream = cotangent.astype(F32)
    mask = mask_own > 0
    logits = jnp.where(mask, mm_t(mixed_low, router[:experts]), VERY_NEGATIVE)
    raised = jnp.where(mask, jnp.exp(logits - jnp.max(logits, axis=-1, keepdims=True)), 0.0)
    weight_own = raised / jnp.sum(raised, axis=-1, keepdims=True)
    route_back = mixed_second[:, rest:rest + experts] + mixed_second[:, rest + experts:rest + 2 * experts]
    chosen_grad = weight_own * (route_back - jnp.sum(weight_own * route_back, axis=-1, keepdims=True))
    logit_grad = chosen_grad.astype(BF16)
    mixed_first = after(mixed_first, mixture_rows)
    mixed_grad = mm(logit_grad, router[:experts]) + jnp.concatenate([mixed_first, mixed_second[:, :rest]], axis=1)
    mixture_back, mixture_terms = normalize_back(mixed_grad, after_attn, scale_mixture, mixture_gain)
    after_grad = upstream + mixture_back
    after_low = after_grad.astype(BF16)

    router_part = t_mm(logit_grad, mixed_low).astype(BF16).reshape(members, planes, model)
    router_part = jnp.pad(router_part, ((0, 0), (0, 8 - planes), (0, 0)))
    mixture_part = jnp.sum(mixture_terms, axis=0, keepdims=True)

    after_all = gather(after_low, "expert")
    mixture_parts = combine(unpick, after(mixture_rows, after_low), planes)
    mixture_first = plane_sum(mixture_parts)
    gate_gradient, up_gradient = hidden_gradient(
        arrived[0], arrived[1], *after((gate_grad, up_grad), after_low, *mixture_parts))
    after_all = after(after_all, gate_gradient, router_part, mixture_part, mixture_first)
    mixture_rows = exchange(after(produced[1], gate_gradient), "expert")
    out_partial = out_gradient(member.astype(jnp.int32).reshape(1), attended_all, after_all, out_piece)
    out_share = lax.psum_scatter(
        after(out_partial, mixture_first).reshape(members * width, out_piece), "dp", scatter_dimension=0, tiled=True).astype(F32)
    attended_grad = out_back(after(after_all, out_partial), out_heads)
    dq, dk, dv, query_terms, key_terms = attend_back(
        prefix_len, query_low, key_low, value_low, attended_low, inverse, attended_grad, qraw, kraw, cosine, sine,
        query_gain, key_norm_gain)
    normed_partial = unproject(
        own_rows, dq, dk, dv, qkv_pieces, normed, reorder(attention_gain, 0), router_part, mixture_part,
        query_terms, key_terms)
    query_partial = t_mm(normed, dq).astype(BF16)
    mixture_parts = combine(unpick, after(mixture_rows, normed_partial), planes)
    mixture_second = plane_sum(mixture_parts)
    arrived_sums = exchange(after(normed_partial, out_share, query_partial, *mixture_parts), "expert")
    normed_sums = jnp.sum(arrived_sums.astype(F32), axis=0)
    input_back, _ = normalize_back(
        reorder(normed_sums[:own_rows], 1), residual_in, scale_attention, attention_gain)
    input_grad = after_grad + input_back
    layer_out = (after_attn + jnp.concatenate([mixture_first, mixture_second], axis=1)).astype(BF16)

    kv_partial = jnp.concatenate([t_mm(normed, dk), t_mm(normed, dv)], axis=1)

    def kv_cols(j):
        start = j * piece
        return jnp.concatenate(
            [lax.dynamic_slice(kv_partial, (0, start), (model, piece)),
             lax.dynamic_slice(kv_partial, (0, HEAD_SIZE + start), (model, piece))], axis=1)

    kv_total = kv_cols(place)
    for shift in range(1, group):
        pairs = [(e, e - e % group + (e % group + shift) % group) for e in range(members)]
        kv_total += lax.ppermute(kv_cols((place + shift) % group).astype(BF16), "expert", pairs).astype(F32)
    kv_share = plane_sum(cut(kv_total.astype(BF16)))
    down_grad = down_gradient(upstream_a, upstream_b, weight_wide, after(activated, normed_partial))
    query_share = plane_sum(cut(after(query_partial, mixture_second, kv_share)), [down_grad], [normed_sums])
    key_share = kv_share[:, :piece]
    value_share = kv_share[:, piece:]

    last = normed_sums[own_rows:]
    attention_sum, mixture_sum, head_sum = (last[8 + 2 * n] + last[9 + 2 * n] for n in range(3))
    gains = jnp.concatenate([reorder(attention_sum, 0), mixture_sum, head_sum[:2 * HEAD_SIZE]])
    total = jnp.concatenate([gains, last[:planes].reshape(-1)]).reshape(-1, HEAD_SIZE)
    step = 1
    while step < planes:
        total = total + lax.ppermute(total, "dp", [(i, i ^ step) for i in range(planes)])
        step *= 2
    total = total.reshape(-1)
    gains, router_total = total[:gains.shape[0]], total[gains.shape[0]:].reshape(planes, model)
    router_share = lax.dynamic_slice(router_total, (0, plane * part_rows), (planes, part_rows)).T
    attention_total, mixture_total = gains[:model], gains[model:2 * model]
    query_total, key_total = gains[2 * model:2 * model + HEAD_SIZE], gains[2 * model + HEAD_SIZE:]
    return (
        layer_out,
        input_grad,
        query_share,
        key_share,
        value_share,
        out_share,
        router_share,
        attention_total,
        mixture_total,
        query_total,
        key_total,
        gate_gradient,
        up_gradient,
        down_grad,
    )


def solution(mesh):
    rows = P(("dp", "expert"), None)
    grid = P("dp", "expert")
    experts = P(("dp", "expert"), None, None)
    in_specs = (rows, rows, P("dp"), grid, grid, grid, grid, grid, P(), P(), P(), P(), experts, experts, experts, rows)
    out_specs = (rows, rows, grid, grid, grid, grid, grid, P(), P(), P(), P(), experts, experts, experts)
    return jax.shard_map(shards, mesh=mesh, in_specs=in_specs, out_specs=out_specs, check_vma=False)
```

```python
import functools
import math

import jax
import jax.numpy as jnp
from jax import lax
from jax.experimental import pallas as pl
from jax.experimental.pallas import tpu as pltpu
from jax.sharding import PartitionSpec as P

QUERY_HEADS = 32
KEY_VALUE_HEADS = 4
HEAD_SIZE = 128
TOP = 8
EPS = 1e-06
ROTARY_BASE = 1000000.0
VERY_NEGATIVE = -1e30
SOFTMAX_SCALE = HEAD_SIZE ** (-0.5)
LOG2_SCALE = SOFTMAX_SCALE * math.log2(math.e)
VMEM_BYTES = 24 * 1024 * 1024
F32 = jnp.float32
BF16 = jnp.bfloat16


def cost(microseconds):
    return pl.CostEstimate(flops=int(microseconds * 1.1e9) + 1, bytes_accessed=1, transcendentals=0)


def mm(a, b):
    return lax.dot_general(a, b, (((1,), (0,)), ((), ())), preferred_element_type=F32)


def mm_t(a, b):
    return lax.dot_general(a, b, (((1,), (1,)), ((), ())), preferred_element_type=F32)


def t_mm(a, b):
    return lax.dot_general(a, b, (((0,), (0,)), ((), ())), preferred_element_type=F32)


def row_scale(source):
    return lax.rsqrt(jnp.mean(source * source, axis=-1, keepdims=True) + EPS)


def normalize_back(upstream, source, scaling, gain_row):
    unit_rows = source * scaling
    weighted = upstream * gain_row
    inner_mean = jnp.mean(weighted * unit_rows, axis=-1, keepdims=True)
    return (scaling * (weighted - unit_rows * inner_mean), upstream * unit_rows)


def rotary_tables(span):
    half = HEAD_SIZE // 2
    frequency = jnp.power(ROTARY_BASE, -jnp.arange(half, dtype=F32) * 2.0 / HEAD_SIZE)
    angles = jnp.arange(span, dtype=jnp.int32).astype(F32)[:, None] * frequency[None, :]
    cosine, sine = jnp.cos(angles), jnp.sin(angles)
    return (
        jnp.concatenate([cosine, cosine], axis=-1),
        jnp.concatenate([-sine, sine], axis=-1),
    )


def turned(u, gain, cosine, sine):
    n = u * row_scale(u) * gain
    return (n * cosine + pltpu.roll(n, HEAD_SIZE // 2, 1) * sine).astype(BF16)


def pieces_product(x, refs):
    size = refs[0].shape[0]
    total = mm(x[:, :size], refs[0][...])
    for s in range(1, len(refs)):
        total += mm(x[:, s * size:(s + 1) * size], refs[s][...])
    return total


def project_kernel(x_ref, cos_ref, sin_ref, qg_ref, kg_ref, *refs):
    weights, (qraw_ref, kraw_ref, q_ref, k_ref, v_ref) = refs[:-5], refs[-5:]
    total = pieces_product(x_ref[...], weights)
    width = q_ref.shape[1]
    cosine, sine = cos_ref[...], sin_ref[...]
    qraw_ref[...] = total[:, :width]
    for h in range(width // HEAD_SIZE):
        cols = slice(h * HEAD_SIZE, (h + 1) * HEAD_SIZE)
        q_ref[:, cols] = turned(total[:, cols], qg_ref[...], cosine, sine)
    key = total[:, width:width + HEAD_SIZE]
    kraw_ref[...] = key
    k_ref[...] = turned(key, kg_ref[...], cosine, sine)
    v_ref[...] = total[:, width + HEAD_SIZE:].astype(BF16)


def project(x, weights, cosine, sine, q_gain, k_gain):
    span, model = x.shape
    width = weights[0].shape[1] - 2 * HEAD_SIZE
    tile = 256
    row = lambda w: pl.BlockSpec((tile, w), lambda i: (i, 0))
    whole = lambda a, b: pl.BlockSpec((a, b), lambda i: (0, 0))
    out = [(width, F32), (HEAD_SIZE, F32), (width, BF16), (HEAD_SIZE, BF16), (HEAD_SIZE, BF16)]
    return pl.pallas_call(
        project_kernel,
        grid=(span // tile,),
        in_specs=[row(model), row(HEAD_SIZE), row(HEAD_SIZE), whole(1, HEAD_SIZE), whole(1, HEAD_SIZE)]
        + [whole(*w.shape) for w in weights],
        out_specs=[row(w) for w, _ in out],
        out_shape=[jax.ShapeDtypeStruct((span, w), t) for w, t in out],
        compiler_params=pltpu.CompilerParams(vmem_limit_bytes=VMEM_BYTES),
        cost_estimate=cost(0),
        name="project",
    )(x, cosine, sine, q_gain[None], k_gain[None], *weights)


def block_limits(span, tile):
    return [(r0, max(r0 + tile, span // 2)) for r0 in range(0, span, tile)]


def masked(values, r0, limit, prefix):
    tile = values.shape[0]
    rows = r0 + lax.broadcasted_iota(jnp.int32, (tile, limit - r0), 0)
    cols = r0 + lax.broadcasted_iota(jnp.int32, (tile, limit - r0), 1)
    right = jnp.where((cols <= rows) | (cols < prefix), values[:, r0:], 0.0)
    return right if r0 == 0 else jnp.concatenate([values[:, :r0], right], axis=1)


def attend_kernel(tile, prefix_ref, q_ref, k_ref, v_ref, o_ref, l_ref, wide_ref):
    span = q_ref.shape[0]

    @pl.when(pl.program_id(0) == 0)
    def _():
        wide_ref[:, :HEAD_SIZE] = v_ref[...]
        wide_ref[:, HEAD_SIZE:] = jnp.ones((span, HEAD_SIZE), BF16)

    prefix = prefix_ref[0]
    for r0, limit in block_limits(span, tile):
        rows = slice(r0, r0 + tile)
        scores = mm_t(q_ref[rows, :], k_ref[:limit, :])
        weights = masked(jnp.exp2(scores * LOG2_SCALE), r0, limit, prefix)
        sums = mm(weights.astype(BF16), wide_ref[:limit, :])
        inverse = 1.0 / sums[:, HEAD_SIZE:]
        o_ref[rows, :] = (sums[:, :HEAD_SIZE] * inverse).astype(BF16)
        l_ref[rows, :] = inverse


def attend(prefix, q, k, v):
    span, width = q.shape
    heads = width // HEAD_SIZE
    head = pl.BlockSpec((span, HEAD_SIZE), lambda h: (0, h))
    shared = pl.BlockSpec((span, HEAD_SIZE), lambda h: (0, 0))
    return pl.pallas_call(
        functools.partial(attend_kernel, 256),
        grid=(heads,),
        in_specs=[pl.BlockSpec(memory_space=pltpu.SMEM), head, shared, shared],
        out_specs=[head, head],
        out_shape=[jax.ShapeDtypeStruct((span, width), BF16), jax.ShapeDtypeStruct((span, width), F32)],
        scratch_shapes=[pltpu.VMEM((span, 2 * HEAD_SIZE), BF16)],
        compiler_params=pltpu.CompilerParams(vmem_limit_bytes=VMEM_BYTES),
        cost_estimate=cost(0),
        name="attend",
    )(prefix, q, k, v)


def attend_back_kernel(tile, prefix_ref, q_ref, k_ref, v_ref, o_ref, l_ref, do_ref, qraw_ref, kraw_ref, cos_ref, sin_ref,
                       qg_ref, kg_ref, dq_ref, dk_ref, dv_ref, qgg_ref, kgg_ref, dk_sum, dv_sum):
    span = q_ref.shape[0]
    step = pl.program_id(0)

    @pl.when(step == 0)
    def _():
        dk_sum[...] = jnp.zeros_like(dk_sum)
        dv_sum[...] = jnp.zeros_like(dv_sum)
        qgg_ref[...] = jnp.zeros_like(qgg_ref)

    def unturned(grad, rows):
        return grad * cos_ref[rows, :] - pltpu.roll(grad, HEAD_SIZE // 2, 1) * sin_ref[rows, :]

    prefix = prefix_ref[0]
    for r0, limit in block_limits(span, tile):
        rows = slice(r0, r0 + tile)
        q, do = q_ref[rows, :], do_ref[rows, :]
        keys, values = k_ref[:limit, :], v_ref[:limit, :]
        weights = masked(jnp.exp2(mm_t(q, keys) * LOG2_SCALE), r0, limit, prefix)
        probs = weights * jnp.concatenate([l_ref[rows, :]] * (limit // HEAD_SIZE), axis=1)
        delta = jnp.sum(do.astype(F32) * o_ref[rows, :].astype(F32), axis=1, keepdims=True)
        score_grad = (probs * (mm_t(do, values) - delta)).astype(BF16)
        dv_sum[:limit, :] += t_mm(probs.astype(BF16), do)
        dk_sum[:limit, :] += t_mm(score_grad, q)
        turn = unturned(mm(score_grad, keys) * SOFTMAX_SCALE, rows)
        raw = qraw_ref[rows, :]
        back, terms = normalize_back(turn, raw, row_scale(raw), qg_ref[...])
        dq_ref[rows, :] = back.astype(BF16)
        qgg_ref[...] += jnp.sum(terms, axis=0, keepdims=True)

    @pl.when(step == pl.num_programs(0) - 1)
    def _():
        raw = kraw_ref[...]
        turn = unturned(dk_sum[...] * SOFTMAX_SCALE, slice(None))
        back, terms = normalize_back(turn, raw, row_scale(raw), kg_ref[...])
        dk_ref[...] = back.astype(BF16)
        dv_ref[...] = dv_sum[...].astype(BF16)
        kgg_ref[...] = jnp.sum(terms, axis=0, keepdims=True)


def attend_back(prefix, q, k, v, o, inverse, do, qraw, kraw, cosine, sine, q_gain, k_gain):
    span, width = q.shape
    heads = width // HEAD_SIZE
    head = pl.BlockSpec((span, HEAD_SIZE), lambda h: (0, h))
    shared = pl.BlockSpec((span, HEAD_SIZE), lambda h: (0, 0))
    gain = pl.BlockSpec((1, HEAD_SIZE), lambda h: (0, 0))
    return pl.pallas_call(
        functools.partial(attend_back_kernel, 256),
        grid=(heads,),
        in_specs=[pl.BlockSpec(memory_space=pltpu.SMEM), head, shared, shared, head, head, head, head, shared, shared,
                  shared, gain, gain],
        out_specs=[head, shared, shared, gain, gain],
        out_shape=[
            jax.ShapeDtypeStruct((span, width), BF16),
            jax.ShapeDtypeStruct((span, HEAD_SIZE), BF16),
            jax.ShapeDtypeStruct((span, HEAD_SIZE), BF16),
            jax.ShapeDtypeStruct((1, HEAD_SIZE), F32),
            jax.ShapeDtypeStruct((1, HEAD_SIZE), F32),
        ],
        scratch_shapes=[pltpu.VMEM((span, HEAD_SIZE), F32), pltpu.VMEM((span, HEAD_SIZE), F32)],
        compiler_params=pltpu.CompilerParams(vmem_limit_bytes=VMEM_BYTES),
        cost_estimate=cost(0),
        name="attend_back",
    )(prefix, q, k, v, o, inverse, do, qraw, kraw, cosine, sine, q_gain[None], k_gain[None])


def unproject_kernel(own_rows, dq_ref, dk_ref, dv_ref, x_ref, gain_ref, router_ref, mix_ref, qg_ref, kg_ref,
                     *refs):
    weights, out_ref, sum_ref = refs[:-2], refs[-2], refs[-1]
    span, model = x_ref.shape
    size = weights[0].shape[0]
    tile = 512
    each = tile // own_rows
    for r in range(span // tile):
        rows = slice(r * tile, (r + 1) * tile)
        grads = jnp.concatenate([dq_ref[rows, :], dk_ref[rows, :], dv_ref[rows, :]], axis=1)
        for s, weight in enumerate(weights):
            cols = slice(s * size, (s + 1) * size)
            total = mm_t(grads, weight[...])
            low = total.astype(BF16)
            for m in range(each):
                out_ref[r * each + m, :own_rows, cols] = low[m * own_rows:(m + 1) * own_rows]
            part = jnp.sum(total * x_ref[rows, cols].astype(F32), axis=0, keepdims=True)
            if r == 0:
                sum_ref[:, cols] = part
            else:
                sum_ref[:, cols] += part
    heads = jnp.concatenate([qg_ref[...], kg_ref[...], jnp.zeros((1, model - 2 * HEAD_SIZE), F32)], axis=1)
    place = lax.broadcasted_iota(jnp.int32, (8, model), 0)
    sums = jnp.zeros((8, model), F32)
    for n, values in enumerate((sum_ref[...] / gain_ref[...], mix_ref[...], heads)):
        high = values.astype(BF16).astype(F32)
        sums = jnp.where(place == 2 * n, high, jnp.where(place == 2 * n + 1, values - high, sums))
    sums = sums.astype(BF16)
    for m in range(out_ref.shape[0]):
        out_ref[m, own_rows:own_rows + 8, :] = router_ref[m]
        out_ref[m, own_rows + 8:, :] = sums


def unproject(own_rows, dq, dk, dv, pieces, x, gain, router_part, mixture_part, query_part, key_part):
    span, model = x.shape
    return pl.pallas_call(
        functools.partial(unproject_kernel, own_rows),
        out_shape=jax.ShapeDtypeStruct((span // own_rows, own_rows + 16, model), BF16),
        scratch_shapes=[pltpu.VMEM((1, model), F32)],
        compiler_params=pltpu.CompilerParams(vmem_limit_bytes=44 * 1024 * 1024),
        cost_estimate=cost(0),
        name="unproject",
    )(dq, dk, dv, x, gain[None], router_part, mixture_part, query_part, key_part, *pieces)


def out_project_kernel(plane_ref, a_ref, *refs):
    out_ref = refs[-1]
    pieces = refs[:-1]
    members, _, width = a_ref.shape
    planes, each = len(pieces), members // len(pieces)
    total = None
    for s, piece in enumerate(pieces):
        block = lax.rem(plane_ref[0] + planes - s, planes) * each
        for i in range(each):
            part = mm(a_ref[block + i], piece[i * width:(i + 1) * width, :])
            total = part if total is None else total + part
    out_ref[...] = total.astype(BF16)


def out_project(plane, attended_all, pieces):
    members, span, width = attended_all.shape
    size, columns = pieces[0].shape
    tile = 256
    return pl.pallas_call(
        out_project_kernel,
        grid=(span // tile,),
        in_specs=[pl.BlockSpec(memory_space=pltpu.SMEM), pl.BlockSpec((members, tile, width), lambda i: (0, i, 0))]
        + [pl.BlockSpec((size, columns), lambda i: (0, 0))] * len(pieces),
        out_specs=pl.BlockSpec((tile, columns), lambda i: (i, 0)),
        out_shape=jax.ShapeDtypeStruct((span, columns), BF16),
        compiler_params=pltpu.CompilerParams(vmem_limit_bytes=VMEM_BYTES),
        cost_estimate=cost(0),
        name="out_project",
    )(plane, attended_all, *pieces)


def out_back_kernel(g_ref, w_ref, out_ref):
    columns = w_ref.shape[2]
    total = mm_t(g_ref[:, :columns], w_ref[0])
    for m in range(1, w_ref.shape[0]):
        total += mm_t(g_ref[:, m * columns:(m + 1) * columns], w_ref[m])
    out_ref[...] = total.astype(BF16)


def out_back(after_all, heads):
    span, model = after_all.shape
    members, width, columns = heads.shape
    tile = 512
    return pl.pallas_call(
        out_back_kernel,
        grid=(span // tile,),
        in_specs=[pl.BlockSpec((tile, model), lambda i: (i, 0)),
                  pl.BlockSpec((members, width, columns), lambda i: (0, 0, 0))],
        out_specs=pl.BlockSpec((tile, width), lambda i: (i, 0)),
        out_shape=jax.ShapeDtypeStruct((span, width), BF16),
        compiler_params=pltpu.CompilerParams(vmem_limit_bytes=56 * 1024 * 1024),
        cost_estimate=cost(0),
        name="out_back",
    )(after_all, heads)


def out_gradient_kernel(member_ref, a_ref, g_ref, out_ref):
    out_ref[0] = t_mm(a_ref[0], g_ref[...]).astype(BF16)


def out_gradient(member, attended_all, after_all, columns):
    members, span, width = attended_all.shape
    return pl.pallas_call(
        out_gradient_kernel,
        grid_spec=pltpu.PrefetchScalarGridSpec(
            num_scalar_prefetch=1,
            grid=(members,),
            in_specs=[pl.BlockSpec((1, span, width), lambda m, me: (m, 0, 0)),
                      pl.BlockSpec((span, columns), lambda m, me: (0, me[0]))],
            out_specs=pl.BlockSpec((1, width, columns), lambda m, me: (m, 0, 0)),
        ),
        out_shape=jax.ShapeDtypeStruct((members, width, columns), BF16),
        compiler_params=pltpu.CompilerParams(vmem_limit_bytes=56 * 1024 * 1024),
        cost_estimate=cost(0),
        name="out_gradient",
    )(member, attended_all, after_all)


def expert_kernel(experts, own_ref, xa_ref, xb_ref, mask_ref, router_ref, gate_ref, up_ref, down_ref,
                  act_ref, gg_ref, ug_ref, w_ref, route_ref):
    half = xa_ref.shape[1]
    own = own_ref[0]
    xa, xb = xa_ref[...], xb_ref[...]

    def product(weight):
        return mm(xa, weight[:half, :]) + mm(xb, weight[half:, :])

    gate_raw, up_raw = product(gate_ref), product(up_ref)
    mask = mask_ref[...].astype(F32)
    logits = mm_t(xa, router_ref[:, :half]) + mm_t(xb, router_ref[:, half:])
    logits = jnp.where(mask > 0, logits, VERY_NEGATIVE)
    raised = jnp.where(mask > 0, jnp.exp(logits - jnp.max(logits, axis=-1, keepdims=True)), 0.0)
    total = jnp.maximum(jnp.sum(raised, axis=-1, keepdims=True), 1e-30)
    lanes = lax.broadcasted_iota(jnp.int32, raised.shape, 1)
    weight = jnp.sum(jnp.where(lanes == own, raised, 0.0), axis=-1, keepdims=True) / total
    w_ref[...] = jnp.broadcast_to(weight, w_ref.shape)

    sig = 1.0 / (1.0 + jnp.exp(-gate_raw))
    silu = gate_raw * sig
    activated = (silu * up_raw).astype(BF16)
    act_ref[...] = activated
    down = down_ref[...]
    route = jnp.sum(activated.astype(F32) * down, axis=-1, keepdims=True)
    grad = weight * down
    gg_ref[...] = (grad * up_raw * sig * (1.0 + gate_raw * (1.0 - sig))).astype(BF16)
    ug_ref[...] = (grad * silu).astype(BF16)
    high = route.astype(BF16).astype(F32)
    lanes = lax.broadcasted_iota(jnp.int32, route_ref.shape, 1)
    route_ref[...] = jnp.where(
        lanes == own, high, jnp.where(lanes == experts + own, route - high, 0.0)).astype(BF16)


def expert_forward(experts, own, xa, xb, masked_rows, router, gate, up, upstream_down):
    rows, half = xa.shape
    model, hidden = gate.shape
    padded = router.shape[0]
    route_width = -(-2 * experts // HEAD_SIZE) * HEAD_SIZE
    tile = rows // 4
    row = lambda w: pl.BlockSpec((tile, w), lambda i: (i, 0))
    whole = lambda a, b: pl.BlockSpec((a, b), lambda i: (0, 0))
    out = [(hidden, BF16), (hidden, BF16), (hidden, BF16), (HEAD_SIZE, F32), (route_width, BF16)]
    return pl.pallas_call(
        functools.partial(expert_kernel, experts),
        grid=(rows // tile,),
        in_specs=[pl.BlockSpec(memory_space=pltpu.SMEM), row(half), row(half),
                  pl.BlockSpec((tile, padded), lambda i: (i, half // padded)), whole(padded, model),
                  whole(model, hidden), whole(model, hidden), row(hidden)],
        out_specs=[row(w) for w, _ in out],
        out_shape=[jax.ShapeDtypeStruct((rows, w), t) for w, t in out],
        compiler_params=pltpu.CompilerParams(vmem_limit_bytes=32 * 1024 * 1024),
        cost_estimate=cost(18),
        name="expert_forward",
    )(own, xa, xb, masked_rows, router, gate, up, upstream_down)


def row_gradient_kernel(start, stop, gg_ref, ug_ref, gate_ref, up_ref, *rest):
    part = slice(start, stop)
    total = (mm_t(gg_ref[...], gate_ref[part, :]) + mm_t(ug_ref[...], up_ref[part, :])).astype(BF16)
    out_ref = rest[-1]
    out_ref[:, :total.shape[1]] = total
    if len(rest) == 2:
        out_ref[:, total.shape[1]:] = rest[0][...]


def row_gradient(gg, ug, gate, up, start, stop, route=None):
    rows, hidden = gg.shape
    tile = rows // 4
    row = lambda w: pl.BlockSpec((tile, w), lambda i: (i, 0))
    weight = pl.BlockSpec(gate.shape, lambda i: (0, 0))
    extra = [] if route is None else [route]
    width = stop - start + sum(e.shape[1] for e in extra)
    return pl.pallas_call(
        functools.partial(row_gradient_kernel, start, stop),
        grid=(rows // tile,),
        in_specs=[row(hidden), row(hidden), weight, weight] + [row(e.shape[1]) for e in extra],
        out_specs=row(width),
        out_shape=jax.ShapeDtypeStruct((rows, width), BF16),
        compiler_params=pltpu.CompilerParams(vmem_limit_bytes=VMEM_BYTES),
        cost_estimate=cost(8),
        name="row_gradient",
    )(gg, ug, gate, up, *extra)


def down_back_kernel(ca_ref, cb_ref, down_ref, out_ref):
    half = cb_ref.shape[1]
    out_ref[...] = mm_t(ca_ref[...], down_ref[:, :half]) + mm_t(cb_ref[...], down_ref[:, half:])


def down_back(ca, cb, down):
    rows, half = cb.shape
    hidden, model = down.shape
    tile = 256
    whole = pl.BlockSpec((rows, half), lambda i: (0, 0))
    return pl.pallas_call(
        down_back_kernel,
        grid=(hidden // tile,),
        in_specs=[whole, whole, pl.BlockSpec((tile, model), lambda i: (i, 0))],
        out_specs=pl.BlockSpec((rows, tile), lambda i: (0, i)),
        out_shape=jax.ShapeDtypeStruct((rows, hidden), F32),
        compiler_params=pltpu.CompilerParams(vmem_limit_bytes=VMEM_BYTES),
        cost_estimate=cost(0),
        name="down_back",
    )(ca, cb, down)


def produce_kernel(act_ref, w_ref, down_ref, *outs):
    total = (w_ref[:, :1] * mm(act_ref[...], down_ref[...])).astype(BF16)
    first = outs[0].shape[1]
    outs[0][...] = total[:, :first]
    outs[1][...] = total[:, first:]


def produce(activated, weight, down, first):
    rows, hidden = activated.shape
    model = down.shape[1]
    tile = rows // 4
    row = lambda w: pl.BlockSpec((tile, w), lambda i: (i, 0))
    return pl.pallas_call(
        produce_kernel,
        grid=(rows // tile,),
        in_specs=[row(hidden), row(HEAD_SIZE), pl.BlockSpec((hidden, model), lambda i: (0, 0))],
        out_specs=[row(first), row(model - first)],
        out_shape=[jax.ShapeDtypeStruct((rows, w), BF16) for w in (first, model - first)],
        compiler_params=pltpu.CompilerParams(vmem_limit_bytes=VMEM_BYTES),
        cost_estimate=cost(0),
        name="produce",
    )(activated, weight, down)


def hidden_gradient_kernel(xa_ref, xb_ref, gg_ref, ug_ref, dg_ref, du_ref):
    in_first = pl.program_id(0) < pl.num_programs(0) // 2
    for x_ref, now in ((xa_ref, in_first), (xb_ref, jnp.logical_not(in_first))):
        @pl.when(now)
        def _():
            dg_ref[0] = t_mm(x_ref[...], gg_ref[...])
            du_ref[0] = t_mm(x_ref[...], ug_ref[...])


def hidden_gradient(xa, xb, gg, ug):
    rows, half = xa.shape
    hidden = gg.shape[1]
    tile = 256
    count = half // tile
    whole = pl.BlockSpec((rows, hidden), lambda i: (0, 0))
    out = pl.BlockSpec((1, tile, hidden), lambda i: (0, i, 0))
    return pl.pallas_call(
        hidden_gradient_kernel,
        grid=(2 * count,),
        in_specs=[pl.BlockSpec((rows, tile), lambda i: (0, jnp.minimum(i, count - 1))),
                  pl.BlockSpec((rows, tile), lambda i: (0, jnp.maximum(i - count, 0))), whole, whole],
        out_specs=[out, out],
        out_shape=[jax.ShapeDtypeStruct((1, 2 * half, hidden), F32)] * 2,
        compiler_params=pltpu.CompilerParams(vmem_limit_bytes=VMEM_BYTES),
        cost_estimate=cost(0),
        name="hidden_gradient",
    )(xa, xb, gg, ug)


def down_gradient_kernel(ca_ref, cb_ref, w_ref, act_ref, out_ref):
    in_first = pl.program_id(0) < pl.num_programs(0) // 2
    for c_ref, now in ((ca_ref, in_first), (cb_ref, jnp.logical_not(in_first))):
        @pl.when(now)
        def _():
            out_ref[0] = t_mm(act_ref[...], (w_ref[:, :1] * c_ref[...].astype(F32)).astype(BF16))


def down_gradient(ca, cb, weight, activated):
    rows, half = cb.shape
    hidden = activated.shape[1]
    tile = 256
    count = half // tile
    return pl.pallas_call(
        down_gradient_kernel,
        grid=(2 * count,),
        in_specs=[pl.BlockSpec((rows, tile), lambda i: (0, jnp.minimum(i, count - 1))),
                  pl.BlockSpec((rows, tile), lambda i: (0, jnp.maximum(i - count, 0))),
                  pl.BlockSpec((rows, HEAD_SIZE), lambda i: (0, 0)), pl.BlockSpec((rows, hidden), lambda i: (0, 0))],
        out_specs=pl.BlockSpec((1, hidden, tile), lambda i: (0, 0, i)),
        out_shape=jax.ShapeDtypeStruct((1, hidden, 2 * half), F32),
        compiler_params=pltpu.CompilerParams(vmem_limit_bytes=VMEM_BYTES),
        cost_estimate=cost(0),
        name="down_gradient",
    )(ca, cb, weight, activated)


def dispatch_kernel(pick_ref, *refs):
    out_ref, all_ref = refs[-2:]
    size = all_ref.shape[0] // (len(refs) - 2)

    @pl.when(pl.program_id(0) == 0)
    def _():
        for s, ref in enumerate(refs[:-2]):
            all_ref[s * size:(s + 1) * size, :] = ref[...]

    out_ref[...] = mm(pick_ref[...], all_ref[...]).astype(BF16)


def dispatch(pick, pieces):
    rows, column = pick.shape
    size, width = column // len(pieces), pieces[0].shape[1]
    tile = rows // 4
    return pl.pallas_call(
        dispatch_kernel,
        grid=(rows // tile,),
        in_specs=[pl.BlockSpec((tile, column), lambda i: (i, 0))]
        + [pl.BlockSpec((size, width), lambda i: (0, 0))] * len(pieces),
        out_specs=pl.BlockSpec((tile, width), lambda i: (i, 0)),
        out_shape=jax.ShapeDtypeStruct((rows, width), BF16),
        scratch_shapes=[pltpu.VMEM((column, width), BF16)],
        compiler_params=pltpu.CompilerParams(vmem_limit_bytes=VMEM_BYTES),
        cost_estimate=cost(0),
        name="dispatch",
    )(pick, *pieces)


def combine_kernel(pick_ref, rows_ref, *outs):
    total = mm(pick_ref[...], rows_ref[...]).astype(BF16)
    size = total.shape[0] // len(outs)
    for s, out in enumerate(outs):
        out[...] = total[s * size:(s + 1) * size]


def combine(pick, rows, count, microseconds=0):
    column, slots = pick.shape
    width = rows.shape[1]
    tile = max(t for t in range(HEAD_SIZE, 513, HEAD_SIZE) if width % t == 0)
    size = column // count
    out = pl.BlockSpec((size, tile), lambda i: (0, i))
    return pl.pallas_call(
        combine_kernel,
        grid=(width // tile,),
        in_specs=[pl.BlockSpec((column, slots), lambda i: (0, 0)), pl.BlockSpec((slots, tile), lambda i: (0, i))],
        out_specs=[out] * count,
        out_shape=[jax.ShapeDtypeStruct((size, width), BF16)] * count,
        compiler_params=pltpu.CompilerParams(vmem_limit_bytes=VMEM_BYTES),
        cost_estimate=cost(microseconds),
        name="combine",
    )(pick, rows)


def after(array, *earlier):
    return lax.optimization_barrier((array, *earlier))[0]


def shards(
    tokens,
    routes,
    prefix_len,
    query_weight,
    key_matrix,
    value_matrix,
    out_weight,
    router_weight,
    attention_gain,
    mixture_gain,
    query_gain,
    key_norm_gain,
    expert_gate,
    expert_up,
    expert_down,
    cotangent,
):
    planes, members = lax.axis_size("dp"), lax.axis_size("expert")
    devices = planes * members
    plane, member = lax.axis_index("dp"), lax.axis_index("expert")
    own_rows, model = tokens.shape
    span = own_rows * members
    column = own_rows * planes
    experts = devices
    width = query_weight.shape[1]
    piece = key_matrix.shape[1]
    group = HEAD_SIZE // piece
    block_slots = max(2, 6 * own_rows * TOP // (5 * experts))
    slots = planes * block_slots
    padded = -(-experts // HEAD_SIZE) * HEAD_SIZE
    half = model // 2
    first = 5 * model // 8
    rest = model - first
    part_rows = model // planes
    gate, up, down = expert_gate[0], expert_up[0], expert_down[0]

    def gather(array, axis, dimension=0):
        return lax.all_gather(array, axis, axis=dimension, tiled=True)

    def exchange(array, axis):
        return lax.all_to_all(array, axis, split_axis=0, concat_axis=0, tiled=True)

    def plane_pieces(array):
        def shift(value, by):
            return lax.ppermute(value, "dp", [(i, (i + by) % planes) for i in range(planes)])

        pieces = [array] + [None] * (planes - 1)
        for s in range(1, planes // 2 + 1):
            pieces[s] = shift(pieces[s - 1], 1)
            if planes - s > s:
                pieces[planes - s] = shift(pieces[(planes - s + 1) % planes], -1)
        return pieces

    def plane_sum_direct(pieces):
        total = pieces[0].astype(F32)
        for s in range(1, planes):
            total += lax.ppermute(pieces[s], "dp", [(i, (i - s) % planes) for i in range(planes)]).astype(F32)
        return total

    def plane_sum(pieces, between=(), last=()):
        def shift(value, by):
            return lax.ppermute(value, "dp", [(i, (i + by) % planes) for i in range(planes)]).astype(F32)

        total = pieces[0].astype(F32)
        middle = planes // 2
        for order, by in ((range(middle, 0, -1), -1), (range(middle + 1, planes), 1)):
            running = None
            for s in order:
                if running is None:
                    running = pieces[s]
                else:
                    running = (after(shift(running, by), *between) + pieces[s].astype(F32)).astype(BF16)
            if running is not None:
                total += after(shift(running, by), *last)
                sent = running if by < 0 else sent
        return total, sent

    def reorder(array, dimension):
        size = array.shape[dimension] // planes
        return jnp.concatenate(
            [lax.dynamic_slice_in_dim(array, (plane - s) % planes * size, size, dimension) for s in range(planes)],
            axis=dimension)

    def cut(array):
        return [array[s * (array.shape[0] // planes):(s + 1) * (array.shape[0] // planes)] for s in range(planes)]

    residual_in = tokens.astype(F32)
    scale_attention = row_scale(residual_in)
    normed_own = (residual_in * scale_attention * attention_gain).astype(BF16)
    normed = gather(reorder(normed_own, 1), "expert")

    kv_own = jnp.concatenate([key_matrix, value_matrix], axis=1)
    place = member % group
    kv_parts = [kv_own]
    for shift in range(1, group):
        pairs = [(e - e % group + (e % group + shift) % group, e) for e in range(members)]
        kv_parts.append(lax.ppermute(kv_own, "expert", pairs))

    def kv_piece(j):
        value = kv_parts[0]
        for shift in range(1, group):
            value = jnp.where((place + shift) % group == j, kv_parts[shift], value)
        return value

    ordered = [kv_piece(j) for j in range(group)]
    qkv_part = jnp.concatenate(
        [query_weight] + [p[:, :piece] for p in ordered] + [p[:, piece:] for p in ordered], axis=1)

    expert_ids = jnp.arange(experts, dtype=jnp.int32)
    mask_own = jnp.sum((routes[:, :, None] == expert_ids[None, None, :]).astype(F32), axis=1)
    mask_wide = jnp.pad(mask_own, ((0, 0), (0, padded - experts))).astype(BF16)
    qkv_pieces = plane_pieces(qkv_part)
    upstream_pieces = plane_pieces(
        after(jnp.concatenate([cotangent[:, :half], mask_wide], axis=1), *qkv_pieces[1:]))
    router_rows = gather(after(router_weight.T, normed), "expert").reshape(2 * members, half)
    out_piece = out_weight.shape[1]
    out_pieces = plane_pieces(after(out_weight, *upstream_pieces[1:]))
    cosine, sine = rotary_tables(span)

    mask_plane = jnp.concatenate(
        [lax.dynamic_slice(p, (0, half + plane * members), (own_rows, members)) for p in upstream_pieces], axis=0)
    triangle = (jnp.arange(column)[:, None] >= jnp.arange(column)[None, :]).astype(BF16)
    rank = jnp.where(mask_plane > 0, mm(triangle, mask_plane) - 1.0, -1.0).astype(jnp.int32)
    pick = (rank.T[:, None, :] == jnp.arange(slots, dtype=jnp.int32)[None, :, None])
    pick = pick.reshape(members * slots, column).astype(BF16)
    unpick = rank[:, :, None] == jnp.arange(slots, dtype=jnp.int32)[None, None, :]
    unpick = unpick.reshape(column, members * slots).astype(BF16)
    upstream_sent = dispatch(pick, upstream_pieces)
    upstream_a = exchange(upstream_sent, "expert")

    qraw, kraw, query_low, key_low, value_low = project(
        after(normed, cosine, sine, router_rows), qkv_pieces, cosine, sine, query_gain, key_norm_gain)
    attended_low, inverse = attend(prefix_len, query_low, key_low, value_low)
    attended_all = gather(attended_low, "expert").reshape(members, span, width)

    upstream_pieces = plane_pieces(after(jnp.concatenate([cotangent[:, half:], router_rows], axis=0), *out_pieces[1:]))

    out_rows = out_project(
        plane.astype(jnp.int32).reshape(1),
        after(attended_all, upstream_a, upstream_pieces[1], upstream_pieces[-1]), out_pieces)
    projected = exchange(after(out_rows, *upstream_pieces[2:-1]), "expert").reshape(members, own_rows, out_piece)
    projected = jnp.transpose(projected, (1, 0, 2)).reshape(own_rows, model)

    upstream_sent = dispatch(after(pick, out_rows), upstream_pieces)
    upstream_b = exchange(upstream_sent, "expert")
    pick = after(pick, upstream_sent)
    router = jnp.concatenate([p[own_rows:].reshape(experts, part_rows) for p in upstream_pieces], axis=1)
    router = jnp.pad(reorder(router, 1), ((0, padded - experts), (0, 0)))

    after_attn = residual_in + projected.astype(F32)
    scale_mixture = row_scale(after_attn)
    mixed_low = (after_attn * scale_mixture * mixture_gain).astype(BF16)
    arrived = []
    for columns in (slice(0, half), slice(half, model)):
        sent = dispatch(pick, plane_pieces(mixed_low[:, columns]))
        arrived.append(exchange(after(sent, upstream_b), "expert"))

    out_columns = reorder(jnp.concatenate(after(out_pieces, arrived[0]), axis=0), 0)
    out_heads = exchange(after(out_columns, arrived[1]).reshape(members, width, out_piece), "expert")
    upstream_down = down_back(upstream_a, upstream_b, down)
    own_expert = (plane * members + member).astype(jnp.int32).reshape(1)
    activated, gate_grad, up_grad, weight_wide, route_columns = expert_forward(
        experts, own_expert, arrived[0], arrived[1], upstream_a, router, gate, up, upstream_down)
    back_first = exchange(row_gradient(gate_grad, up_grad, gate, up, 0, first), "expert")
    back_second = exchange(row_gradient(gate_grad, up_grad, gate, up, first, model, route_columns), "expert")
    produced = produce(activated, weight_wide, down, first)
    back_first = after(back_first, out_heads, *produced)
    mixed_first = plane_sum_direct(combine(unpick, back_first, planes, 40))
    mixed_second = plane_sum_direct(combine(unpick, back_second, planes, 40))
    mixture_rows = exchange(after(produced[0], back_second), "expert")

    upstream = cotangent.astype(F32)
    mask = mask_own > 0
    logits = jnp.where(mask, mm_t(mixed_low, router[:experts]), VERY_NEGATIVE)
    raised = jnp.where(mask, jnp.exp(logits - jnp.max(logits, axis=-1, keepdims=True)), 0.0)
    weight_own = raised / jnp.sum(raised, axis=-1, keepdims=True)
    route_back = mixed_second[:, rest:rest + experts] + mixed_second[:, rest + experts:rest + 2 * experts]
    chosen_grad = weight_own * (route_back - jnp.sum(weight_own * route_back, axis=-1, keepdims=True))
    logit_grad = chosen_grad.astype(BF16)
    mixed_first = after(mixed_first, mixture_rows)
    mixed_grad = mm(logit_grad, router[:experts]) + jnp.concatenate([mixed_first, mixed_second[:, :rest]], axis=1)
    mixture_back, mixture_terms = normalize_back(mixed_grad, after_attn, scale_mixture, mixture_gain)
    after_grad = upstream + mixture_back
    after_low = after_grad.astype(BF16)

    router_part = t_mm(logit_grad, mixed_low).astype(BF16).reshape(members, planes, model)
    router_part = jnp.pad(router_part, ((0, 0), (0, 8 - planes), (0, 0)))
    mixture_part = jnp.sum(mixture_terms, axis=0, keepdims=True)

    after_all = gather(after_low, "expert")
    mixture_parts = combine(unpick, after(mixture_rows, after_low), planes)
    mixture_first, _ = plane_sum(mixture_parts)
    gate_gradient, up_gradient = hidden_gradient(
        arrived[0], arrived[1], *after((gate_grad, up_grad), after_low, *mixture_parts))
    after_all = after(after_all, gate_gradient, router_part, mixture_part, mixture_first)
    mixture_rows = exchange(after(produced[1], gate_gradient), "expert")
    out_partial = out_gradient(member.astype(jnp.int32).reshape(1), attended_all, after_all, out_piece)
    out_share = lax.psum_scatter(
        after(out_partial, mixture_first).reshape(members * width, out_piece), "dp", scatter_dimension=0, tiled=True).astype(F32)
    attended_grad = out_back(after(after_all, out_partial), out_heads)
    dq, dk, dv, query_terms, key_terms = attend_back(
        prefix_len, query_low, key_low, value_low, attended_low, inverse, attended_grad, qraw, kraw, cosine, sine,
        query_gain, key_norm_gain)
    normed_partial = unproject(
        own_rows, dq, dk, dv, qkv_pieces, normed, reorder(attention_gain, 0), router_part, mixture_part,
        query_terms, key_terms)
    query_partial = t_mm(normed, dq).astype(BF16)
    mixture_parts = combine(unpick, after(mixture_rows, normed_partial), planes)
    mixture_second, _ = plane_sum(mixture_parts)
    arrived_sums = exchange(after(normed_partial, out_share, query_partial, *mixture_parts), "expert")
    normed_sums = jnp.sum(arrived_sums.astype(F32), axis=0)
    input_back, _ = normalize_back(
        reorder(normed_sums[:own_rows], 1), residual_in, scale_attention, attention_gain)
    input_grad = after_grad + input_back
    layer_out = (after_attn + jnp.concatenate([mixture_first, mixture_second], axis=1)).astype(BF16)

    kv_partial = jnp.concatenate([t_mm(normed, dk), t_mm(normed, dv)], axis=1)

    def kv_cols(j):
        start = j * piece
        return jnp.concatenate(
            [lax.dynamic_slice(kv_partial, (0, start), (model, piece)),
             lax.dynamic_slice(kv_partial, (0, HEAD_SIZE + start), (model, piece))], axis=1)

    kv_total = kv_cols(place)
    for shift in range(1, group):
        pairs = [(e, e - e % group + (e % group + shift) % group) for e in range(members)]
        kv_total += lax.ppermute(kv_cols((place + shift) % group).astype(BF16), "expert", pairs).astype(F32)
    down_grad = down_gradient(upstream_a, upstream_b, weight_wide, after(activated, normed_partial))
    query_share, halfway = plane_sum(cut(after(query_partial, mixture_second)), [down_grad], [normed_sums])
    kv_share = plane_sum_direct(cut(after(kv_total.astype(BF16), halfway)))
    key_share = kv_share[:, :piece]
    value_share = kv_share[:, piece:]

    last = normed_sums[own_rows:]
    attention_sum, mixture_sum, head_sum = (last[8 + 2 * n] + last[9 + 2 * n] for n in range(3))
    gains = jnp.concatenate([reorder(attention_sum, 0), mixture_sum, head_sum[:2 * HEAD_SIZE]])
    total = jnp.concatenate([gains, last[:planes].reshape(-1)]).reshape(-1, HEAD_SIZE)
    step = 1
    while step < planes:
        total = total + lax.ppermute(total, "dp", [(i, i ^ step) for i in range(planes)])
        step *= 2
    total = total.reshape(-1)
    gains, router_total = total[:gains.shape[0]], total[gains.shape[0]:].reshape(planes, model)
    router_share = lax.dynamic_slice(router_total, (0, plane * part_rows), (planes, part_rows)).T
    attention_total, mixture_total = gains[:model], gains[model:2 * model]
    query_total, key_total = gains[2 * model:2 * model + HEAD_SIZE], gains[2 * model + HEAD_SIZE:]
    return (
        layer_out,
        input_grad,
        query_share,
        key_share,
        value_share,
        out_share,
        router_share,
        attention_total,
        mixture_total,
        query_total,
        key_total,
        gate_gradient,
        up_gradient,
        down_grad,
    )


def solution(mesh):
    rows = P(("dp", "expert"), None)
    grid = P("dp", "expert")
    experts = P(("dp", "expert"), None, None)
    in_specs = (rows, rows, P("dp"), grid, grid, grid, grid, grid, P(), P(), P(), P(), experts, experts, experts, rows)
    out_specs = (rows, rows, grid, grid, grid, grid, grid, P(), P(), P(), P(), experts, experts, experts)
    return jax.shard_map(shards, mesh=mesh, in_specs=in_specs, out_specs=out_specs, check_vma=False)
```
